32 devices in a mesh: grp: 8 (over z, y), blk: 4 (over x, core).
Axes of the slice: x: 2, y: 2, z: 4, core: 2. Of those that a mesh axis runs over, the one named last changes fastest.
Arguments:
- features: bfloat16 [16384, 256], P(('grp', 'blk')), may hold values from -6 to 6
- d_out: float32 [16384, 256], P(('grp', 'blk')), may hold values from -6 to 6
- bucket_batch: int32 [8], P('grp'), may hold values from 1 to 2, as said below
- valid_len: int32 [8, 2], P('grp'), may hold values from 0 to 2048, as said below
- time_start: int32 [8, 2], P('grp'), may hold values from 0 to 983
- time_width: int32 [8, 2], P('grp'), may hold values from 0 to 40
- freq_start: int32 [8, 2], P('grp'), may hold values from 0 to 228
- freq_width: int32 [8, 2], P('grp'), may hold values from 0 to 27
- gains: float32 [5, 256], replicated, may hold values from 0.5 to 1.5
- inner_gain: float32 [512], replicated, may hold values from 0.5 to 1.5
- ffn1_in: bfloat16 [256, 1024], replicated, may hold values from -0.375 to 0.375
- ffn1_out: bfloat16 [1024, 256], replicated, may hold values from -0.375 to 0.375
- qkv_w: bfloat16 [256, 768], replicated, may hold values from -0.375 to 0.375
- out_w: bfloat16 [256, 256], replicated, may hold values from -6 to 6
- cg_up: bfloat16 [256, 1024], replicated, may hold values from -0.375 to 0.375
- cg_conv: bfloat16 [31, 512], replicated, may hold values from -1 to 1
- cg_down: bfloat16 [512, 256], replicated, may hold values from -0.25 to 0.25
- merge_conv: bfloat16 [31, 512], replicated, may hold values from -1 to 1
- merge_w: bfloat16 [512, 256], replicated, may hold values from -0.25 to 0.25
- ffn2_in: bfloat16 [256, 1024], replicated, may hold values from -0.375 to 0.375
- ffn2_out: bfloat16 [1024, 256], replicated, may hold values from -0.375 to 0.375
Outputs:
- out: bfloat16 [16384, 256], P(('grp', 'blk'))
- d_features: float32 [16384, 256], P(('grp', 'blk'))
- grad_gains: float32 [5, 256], replicated
- grad_inner_gain: float32 [512], replicated
- grad_ffn1_in: float32 [256, 1024], replicated
- grad_ffn1_out: float32 [1024, 256], replicated
- grad_qkv_w: float32 [256, 768], replicated
- grad_out_w: float32 [256, 256], replicated
- grad_cg_up: float32 [256, 1024], replicated
- grad_cg_conv: float32 [31, 512], replicated
- grad_cg_down: float32 [512, 256], replicated
- grad_merge_conv: float32 [31, 512], replicated
- grad_merge_w: float32 [512, 256], replicated
- grad_ffn2_in: float32 [256, 1024], replicated
- grad_ffn2_out: float32 [1024, 256], replicated
The draws below stay inside these ranges and needn't reach their ends.
Inputs may be any that keep to these rules, and one draw needn't show every extreme that they name: Number of utterances in bucket g; its padded length is 2048 / bucket_batch[g]. Both 1 and 2 occur in every draw. `valid_len`: for a slot u below the bucket's batch size: between a quarter of the padded length and all of it, one slot of every bucket exactly the padded length. Slots at or above the batch size hold 0.
All inputs are finite; a program needn't handle non-finite values.
Results may differ from the reference program's by a relative error of at most 0.015.
Values may be sent and summed in bfloat16 or wider, within the bound.
No kernel may reach another device: no remote copies, remote signals or barrier semaphores. Data moves between devices by JAX's collectives and lax.ppermute only.
A program may use at most 128 MiB of HBM per device.

```python
import math
import jax
import jax.numpy as jnp
from jax import lax

D = 256
HEADS = 4
HEAD_DIM = 64
FF = 1024
CG = 1024
CGH = 512
KERNEL = 31
TOK_DEV = 512
BMAX = 2
TMASK = 40
FMASK = 27
GROUPS = 8
GROUP_TOK = 2048
ROWS = 16384


def bucket_plan(key):
    subkeys = jax.random.split(key, 4)
    batch_sizes = jax.random.randint(subkeys[0], (GROUPS,), 1, BMAX + 1)
    shuffled = jax.random.permutation(subkeys[1], GROUPS)
    batch_sizes = batch_sizes.at[shuffled[0]].set(BMAX).at[shuffled[1]].set(1)
    padded = GROUP_TOK // batch_sizes
    low_end = padded // 4
    random_bits = jax.random.randint(subkeys[2], (GROUPS, BMAX), 0, 1 << 24)
    lengths = low_end[:, None] + random_bits % (padded - low_end + 1)[:, None]
    full_slot = jax.random.randint(subkeys[3], (GROUPS,), 0, BMAX) % batch_sizes
    slot_ids = jnp.arange(BMAX)
    lengths = jnp.where(slot_ids[None, :] == full_slot[:, None], padded[:, None], lengths)
    lengths = jnp.where(slot_ids[None, :] < batch_sizes[:, None], lengths, 0)
    return (batch_sizes.astype(jnp.int32), lengths.astype(jnp.int32))


def draw_bucket_batch(key, part):
    return bucket_plan(key)[0]


def draw_valid_len(key, part):
    return bucket_plan(key)[1]


def place_ends(array, stream_key, least, top_value):
    spot = [jax.random.randint(jax.random.fold_in(stream_key, axis), (), 0, length) for axis, length in enumerate(array.shape)]
    widest = array.shape.index(max(array.shape))
    neighbour = spot[:widest] + [(spot[widest] + 1) % array.shape[widest]] + spot[widest + 1:]
    return array.at[tuple(spot)].set(least).at[tuple(neighbour)].set(top_value)


def block_levels(rng, dims, cuts, low, high):
    factor_of = 1.0
    for axis_at, parts in cuts:
        draws = jax.random.uniform(jax.random.fold_in(jax.random.fold_in(rng, 6), axis_at), (parts,), jnp.float32, low / len(cuts), high / len(cuts))
        factor_of = factor_of * jnp.repeat(jnp.exp(draws), dims[axis_at] // parts).reshape((-1,) + (1,) * (len(dims) - 1 - axis_at))
    return factor_of


def bell_draw(stream_key, shape, scale, bound, shards=(), kind=jnp.bfloat16):
    drawn = scale * jax.random.normal(stream_key, shape, jnp.float32)
    if shards:
        drawn = drawn * block_levels(stream_key, shape, shards, -0.22, 0.18)
    return jnp.clip(drawn, -bound, bound).astype(kind)


def setup_inputs(seed: int = 0) -> dict:
    arg_keys = jax.random.split(jax.random.key(seed), 22)
    return {
        "features": bell_draw(arg_keys[0], (ROWS, D), 1.0, 6.0, ((0, 32),)),
        "d_out": bell_draw(arg_keys[1], (ROWS, D), 1.0, 6.0, ((0, 32),), jnp.float32),
        "bucket_batch": draw_bucket_batch(jax.random.fold_in(arg_keys[21], 71), 0),
        "valid_len": draw_valid_len(jax.random.fold_in(arg_keys[21], 71), 0),
        "time_start": place_ends(jax.random.randint(arg_keys[4], (GROUPS, BMAX), 0, GROUP_TOK // BMAX - TMASK), jax.random.fold_in(arg_keys[4], 1), 0, (GROUP_TOK // BMAX - TMASK) - 1).astype(jnp.int32),
        "time_width": place_ends(jax.random.randint(arg_keys[5], (GROUPS, BMAX), 0, TMASK + 1), jax.random.fold_in(arg_keys[5], 1), 0, TMASK).astype(jnp.int32),
        "freq_start": place_ends(jax.random.randint(arg_keys[6], (GROUPS, BMAX), 0, D - FMASK), jax.random.fold_in(arg_keys[6], 1), 0, (D - FMASK) - 1).astype(jnp.int32),
        "freq_width": place_ends(jax.random.randint(arg_keys[7], (GROUPS, BMAX), 0, FMASK + 1), jax.random.fold_in(arg_keys[7], 1), 0, FMASK).astype(jnp.int32),
        "gains": jnp.clip(1.0 + 0.1 * jax.random.normal(arg_keys[8], (5, D), jnp.float32), 0.5, 1.5),
        "inner_gain": jnp.clip(1.0 + 0.1 * jax.random.normal(arg_keys[9], (CGH,), jnp.float32), 0.5, 1.5),
        "ffn1_in": bell_draw(arg_keys[10], (D, FF), D ** -0.5, 0.375),
        "ffn1_out": bell_draw(arg_keys[11], (FF, D), (FF // 4) ** -0.5, 0.375),
        "qkv_w": bell_draw(arg_keys[12], (D, 3 * D), D ** -0.5, 0.375),
        "out_w": bell_draw(arg_keys[13], (D, D), 1 ** -0.5, 6.0),
        "cg_up": bell_draw(arg_keys[14], (D, CG), D ** -0.5, 0.375),
        "cg_conv": bell_draw(arg_keys[15], (KERNEL, CGH), KERNEL ** -0.5, 1.0),
        "cg_down": bell_draw(arg_keys[16], (CGH, D), CGH ** -0.5, 0.25),
        "merge_conv": bell_draw(arg_keys[17], (KERNEL, 2 * D), KERNEL ** -0.5, 1.0),
        "merge_w": bell_draw(arg_keys[18], (2 * D, D), (2 * D) ** -0.5, 0.25),
        "ffn2_in": bell_draw(arg_keys[19], (D, FF), D ** -0.5, 0.375),
        "ffn2_out": bell_draw(arg_keys[20], (FF, D), (FF // 4) ** -0.5, 0.375),
    }


PRECISE = lax.Precision.HIGHEST
LOG_BASE = 1.4426950408889634
EPSILON = 1e-05
MASKED_SCORE = -1e+30

@jax.custom_vjp
def low(v):
    return lax.optimization_barrier(v.astype(jnp.bfloat16)).astype(jnp.float32)

@jax.custom_vjp
def low_back(v):
    return v

def low_keep(v):
    return (low(v), None)

def low_pass(kept, grad):
    return (grad,)

def back_keep(v):
    return (v, None)

def back_low(kept, grad):
    return (low(grad),)
low.defvjp(low_keep, low_pass)
low_back.defvjp(back_keep, back_low)

def lookup(entries, indices):
    slot_ids = jnp.arange(entries.shape[0], dtype=jnp.int32)
    return lax.optimization_barrier(jnp.sum(jnp.where(indices[:, None] == slot_ids[None, :], entries[None, :], 0), 1)).astype(jnp.int32)

def layer_norm(inputs, gain):
    center = inputs - lax.optimization_barrier(jnp.mean(inputs, -1, keepdims=True))
    spread = lax.optimization_barrier(jnp.mean(center * center, -1, keepdims=True))
    return center * lax.rsqrt(spread + EPSILON) * gain

def matmul(left, right):
    return jnp.dot(left, right, precision=PRECISE, preferred_element_type=jnp.float32)

def linear(inputs, weight):
    return low_back(matmul(low(inputs), weight))

def rotate(inputs, position, direction):
    row_count = inputs.shape[0]
    half_dim = HEAD_DIM // 2
    frequency = jnp.exp(jnp.arange(half_dim, dtype=jnp.float32) * (-2.0 * math.log(10000.0) / HEAD_DIM))
    angles = position.astype(jnp.float32)[:, None] * frequency[None, :]
    cosine = jnp.cos(angles)[:, None, :]
    sine_part = direction * jnp.sin(angles)[:, None, :]
    pairs_view = inputs.reshape(row_count, HEADS, 2, half_dim)
    former = pairs_view[:, :, 0]
    latter = pairs_view[:, :, 1]
    turned = jnp.stack([former * cosine - latter * sine_part, former * sine_part + latter * cosine], 2)
    return turned.reshape(row_count, HEADS * HEAD_DIM)

def depthwise(inputs, weight, position, padded):
    row_count = inputs.shape[0]
    half_kernel = KERNEL // 2
    widened = jnp.pad(inputs, ((half_kernel, half_kernel), (0, 0)))
    result = jnp.zeros_like(inputs)
    for tap_index in range(KERNEL):
        shifted = position + (tap_index - half_kernel)
        inside = ((shifted >= 0) & (shifted < padded)).astype(inputs.dtype)[:, None]
        result = result + widened[tap_index:tap_index + row_count] * inside * weight[tap_index]
    return result

def attention(queries, key_rows, value_rows, utterance, key_valid):
    row_count = queries.shape[0]
    block_rows = math.gcd(512, row_count)
    score_scale = HEAD_DIM ** (-0.5)
    key_heads = key_rows.reshape(row_count, HEADS, HEAD_DIM)
    value_heads = value_rows.reshape(row_count, HEADS, HEAD_DIM)

    @jax.checkpoint
    def one_block(pieces):
        query_block, query_utterance = pieces
        query_heads = query_block.reshape(block_rows, HEADS, HEAD_DIM)
        scores = low_back(jnp.einsum('qhd,khd->hqk', query_heads, key_heads, precision=PRECISE))
        scaled = scores * score_scale * LOG_BASE
        visible = (query_utterance[:, None] == utterance[None, :]) & key_valid[None, :]
        ceiling = jnp.floor(lax.optimization_barrier(jnp.max(jnp.where(visible, scaled, MASKED_SCORE), -1, keepdims=True)))
        weights = jnp.where(visible, jnp.exp2(jnp.where(visible, scaled - ceiling, -200.0)), 0.0)
        weight_sum = lax.optimization_barrier(jnp.sum(weights, -1))
        summed = low_back(jnp.einsum('hqk,khd->qhd', low(weights), value_heads, precision=PRECISE))
        return (summed / weight_sum.T[:, :, None]).reshape(block_rows, HEADS * HEAD_DIM)
    blocks = lax.map(one_block, (queries.reshape(-1, block_rows, HEADS * HEAD_DIM), utterance.reshape(-1, block_rows)))
    return blocks.reshape(row_count, HEADS * HEAD_DIM)

def feed_forward(inputs, gain, weight_in, weight_out):
    hidden = low(jax.nn.silu(linear(layer_norm(inputs, gain), weight_in)))
    return low_back(matmul(hidden, weight_out))

def group_forward(weights, features, batch_size, lengths, time_begin, time_span, band_begin, band_span):
    gains, inner_gain, ffn1_in, ffn1_out, qkv_w, out_w, cg_up, cg_conv, cg_down, merge_conv, merge_w, ffn2_in, ffn2_out = weights
    padded = GROUP_TOK // batch_size
    shard_rows = TOK_DEV // batch_size
    canonical = jnp.arange(GROUP_TOK, dtype=jnp.int32)
    utterance = canonical // padded
    position = canonical % padded
    source_row = position // shard_rows * TOK_DEV + position % shard_rows * batch_size + utterance
    frame_len = lookup(lengths, utterance)
    time_low = lookup(time_begin, utterance)
    time_high = time_low + lookup(time_span, utterance)
    band_low = lookup(band_begin, utterance)
    band_high = band_low + lookup(band_span, utterance)
    frame_keep = (position < frame_len) & jnp.logical_not((position >= time_low) & (position < time_high))
    channel = jnp.arange(D, dtype=jnp.int32)
    band_hit = (channel[None, :] >= band_low[:, None]) & (channel[None, :] < band_high[:, None])
    keep_mask = (frame_keep[:, None] & jnp.logical_not(band_hit)).astype(jnp.float32)
    inputs = features[source_row] * keep_mask
    x_one = inputs + 0.5 * feed_forward(inputs, gains[0], ffn1_in, ffn1_out)
    qkv_rows = linear(layer_norm(x_one, gains[1]), qkv_w)
    queries = low(rotate(qkv_rows[:, :D], position, 1.0))
    key_rows = low(rotate(qkv_rows[:, D:2 * D], position, 1.0))
    value_rows = low(qkv_rows[:, 2 * D:])
    attended = low(attention(queries, key_rows, value_rows, utterance, position < frame_len))
    att_branch = low_back(matmul(attended, out_w))
    opened = jax.nn.gelu(linear(layer_norm(x_one, gains[2]), cg_up))
    rest_part = opened[:, :CGH]
    gate_part = opened[:, CGH:]
    normed_gate = low(layer_norm(gate_part, inner_gain))
    mixed_gate = low_back(depthwise(normed_gate, cg_conv, position, padded))
    gated_low = low(rest_part * mixed_gate)
    cg_branch = low_back(matmul(gated_low, cg_down))
    joined = low(jnp.concatenate([att_branch, cg_branch], 1))
    united_sum = joined + low_back(depthwise(joined, merge_conv, position, padded))
    x_two = x_one + low_back(matmul(low(united_sum), merge_w))
    x_three = x_two + 0.5 * feed_forward(x_two, gains[3], ffn2_in, ffn2_out)
    final_norm = layer_norm(x_three, gains[4])
    row_index = jnp.arange(GROUP_TOK, dtype=jnp.int32)
    local_row = row_index % TOK_DEV
    back_index = local_row % batch_size * padded + row_index // TOK_DEV * shard_rows + local_row // batch_size
    return final_norm[back_index]

def reference(features, d_out, bucket_batch, valid_len, time_start, time_width, freq_start, freq_width, gains, inner_gain, ffn1_in, ffn1_out, qkv_w, out_w, cg_up, cg_conv, cg_down, merge_conv, merge_w, ffn2_in, ffn2_out):
    weights = tuple((weight_arg.astype(jnp.float32) for weight_arg in (gains, inner_gain, ffn1_in, ffn1_out, qkv_w, out_w, cg_up, cg_conv, cg_down, merge_conv, merge_w, ffn2_in, ffn2_out)))

    def forward(inputs, params):

        def per_group(pieces):
            return group_forward(params, *pieces)
        outcome = lax.map(jax.checkpoint(per_group), (inputs.reshape(GROUPS, GROUP_TOK, D), bucket_batch, valid_len, time_start, time_width, freq_start, freq_width))
        return outcome.reshape(ROWS, D)
    output, pullback = jax.vjp(forward, features.astype(jnp.float32), weights)
    grad_features, grad_weights = pullback(d_out.astype(jnp.float32))
    return (output.astype(jnp.bfloat16), grad_features, grad_weights[0], grad_weights[1], grad_weights[2], grad_weights[3], grad_weights[4], grad_weights[5], grad_weights[6], grad_weights[7], grad_weights[8], grad_weights[9], grad_weights[10], grad_weights[11], grad_weights[12])
```

```python
import functools
import math

import jax
import jax.numpy as jnp
import numpy as np
from jax import lax
from jax.experimental import pallas as pl
from jax.experimental.pallas import tpu as pltpu
from jax.sharding import PartitionSpec as P

HEADS = 4
HEAD_DIM = 64
HALO = 32
LOG_BASE = 1.4426950408889634
EPSILON = 1e-05
SCORE_SCALE = HEAD_DIM ** (-0.5)
EXP_SCALE = SCORE_SCALE * LOG_BASE
HIDE = -(2.0 ** 100)
AXES = ("grp", "blk")
F32 = jnp.float32
BF16 = jnp.bfloat16
LANES = 128
VMEM_BYTES = 16 * 1024 * 1024
UNIT = 0.35e9


def mm(left, right):
    return jnp.dot(left, right, preferred_element_type=F32)


def mm_nt(left, right):
    return lax.dot_general(left, right, (((1,), (1,)), ((), ())), preferred_element_type=F32)


def mm_tn(left, right):
    return lax.dot_general(left, right, (((0,), (0,)), ((), ())), preferred_element_type=F32)


def unit(v):
    center = v - jnp.mean(v, -1, keepdims=True)
    rs = lax.rsqrt(jnp.mean(center * center, -1, keepdims=True) + EPSILON)
    return center * rs, rs


def unit_back(up, m, rs, gain):
    eg = up * gain
    grad = rs * (eg - jnp.mean(eg, -1, keepdims=True) - m * jnp.mean(eg * m, -1, keepdims=True))
    return grad, jnp.sum(up * m, 0, keepdims=True)


def silu_parts(u):
    sig = 0.5 + 0.5 * jnp.tanh(0.5 * u)
    h = u * sig
    return h, sig + h * (1.0 - sig)


def gelu_parts(t):
    root = math.sqrt(2.0 / math.pi)
    t2 = t * t
    th = jnp.tanh(root * t * (1.0 + 0.044715 * t2))
    half = 0.5 + 0.5 * th
    slope = half + 0.5 * root * t * (1.0 - th * th) * (1.0 + 3.0 * 0.044715 * t2)
    return t * half, slope


def rows_of(sc, r0, shape):
    row = lax.broadcasted_iota(jnp.int32, shape, 0) + r0
    shift = sc[0] - 1
    utt = row & shift
    pos = (row >> shift) + sc[1] * (512 >> shift)
    return utt, pos


def keep_mask(sc, r0, shape):
    utt, pos = rows_of(sc, r0, shape)
    ch = lax.broadcasted_iota(jnp.int32, shape, 1)
    first = utt == 0

    def pick(i):
        return jnp.where(first, sc[i], sc[i + 1])

    ok = (pos < pick(2)) & jnp.logical_not((pos >= pick(4)) & (pos < pick(6)))
    ok = ok & jnp.logical_not((ch >= pick(8)) & (ch < pick(10)))
    return ok


def turn_tables(sc, freq, rows):
    shift = sc[0] - 1
    coarse = lax.broadcasted_iota(jnp.int32, (rows // 16, LANES), 0) * 16
    fine = lax.broadcasted_iota(jnp.int32, (16, LANES), 0)
    a = ((coarse >> shift) + sc[1] * (rows >> shift)).astype(F32) * freq
    c = (fine >> shift).astype(F32) * freq
    ca, sa, cc, cs = jnp.cos(a), jnp.sin(a), jnp.cos(c), jnp.sin(c)
    cos = ca[:, None, :] * cc[None] - sa[:, None, :] * cs[None]
    sin = sa[:, None, :] * cc[None] + ca[:, None, :] * cs[None]
    return cos.reshape(rows, LANES), sin.reshape(rows, LANES)


def rotate(v, cos, sin, direction):
    lane = lax.broadcasted_iota(jnp.int32, (v.shape[0], LANES), 1)
    lower = (lane & 63) < 32
    signed = jnp.where(lower, -direction, direction) * sin
    parts = []
    for i in range(v.shape[1] // LANES):
        p = v[:, i * LANES : (i + 1) * LANES]
        other = jnp.where(lower, pltpu.roll(p, LANES - 32, 1), pltpu.roll(p, 32, 1))
        parts.append(p * cos + other * signed)
    return jnp.concatenate(parts, 1)


def edge_sends(sc, refs, a_ref, b_ref):
    odd = (sc[1] & 1) == 1
    col = 0
    for ref in refs if isinstance(refs, tuple) else (refs,):
        rows, width = ref.shape
        first = ref[0:HALO, :]
        last = ref[rows - HALO : rows, :]
        cols = slice(col, col + width)
        col += width

        @pl.when(odd)
        def _():
            a_ref[:, cols] = first
            b_ref[:, cols] = last

        @pl.when(jnp.logical_not(odd))
        def _():
            a_ref[:, cols] = last
            b_ref[:, cols] = first


def fill_wide(sc, wide, sources, ha, hb):
    odd = (sc[1] & 1) == 1
    at = 0
    for z in sources:
        rows, width = z.shape
        for c in range(width // LANES):
            cols = slice(at * LANES, (at + 1) * LANES)
            a, b = ha[:, cols].astype(F32), hb[:, cols].astype(F32)
            wide[at, 0:HALO, :] = jnp.where(odd, a, b)
            wide[at, HALO : HALO + rows, :] = z[:, c * LANES : (c + 1) * LANES].astype(F32)
            wide[at, HALO + rows : 2 * HALO + rows, :] = jnp.where(odd, b, a)
            at += 1


CONV_ROWS = 64


def conv_fwd(sc, wide, taps, out, rows):
    batch = sc[0]
    for c in range(taps.shape[1] // LANES):
        cols = slice(c * LANES, (c + 1) * LANES)
        ws = [taps[k : k + 1, cols].astype(F32) for k in range(31)]

        def body(i, carry):
            r0 = pl.multiple_of(i * CONV_ROWS, CONV_ROWS)
            acc = jnp.zeros((CONV_ROWS, LANES), F32)
            for k in range(31):
                acc = acc + wide[c, pl.ds(r0 + HALO + batch * (k - 15), CONV_ROWS), :] * ws[k]
            out[pl.ds(r0, CONV_ROWS), cols] = acc
            return carry

        lax.fori_loop(0, rows // CONV_ROWS, body, 0)


BACK_ROWS = 32


def conv_back(sc, wide, taps, z, out, tap_out, rows):
    batch = sc[0]
    for c in range(taps.shape[1] // LANES):
        cols = slice(c * LANES, (c + 1) * LANES)
        for start, stop in ((0, 16), (16, 31)):
            ws = [taps[k : k + 1, cols].astype(F32) for k in range(start, stop)]

            def body(i, sums):
                r0 = pl.multiple_of(i * BACK_ROWS, BACK_ROWS)
                here = pl.ds(r0, BACK_ROWS)
                zc = z[here, cols].astype(F32)
                acc = out[here, cols]
                new = []
                for k in range(start, stop):
                    e = wide[c, pl.ds(r0 + HALO - batch * (k - 15), BACK_ROWS), :]
                    acc = acc + e * ws[k - start]
                    prod = (e * zc).reshape(BACK_ROWS // 8, 8, LANES)
                    new.append(sums[k - start] + jnp.sum(prod, 0))
                out[here, cols] = acc
                return tuple(new)

            zero = tuple(jnp.zeros((8, LANES), F32) for _ in range(stop - start))
            sums = lax.fori_loop(0, rows // BACK_ROWS, body, zero)
            for k in range(start, stop):
                tap_out[k : k + 1, cols] = jnp.sum(sums[k - start], 0, keepdims=True)


def tiles(rows, size=256):
    size = min(size, rows)
    return [slice(i, i + size) for i in range(0, rows, size)]


def pre_kernel(*refs):
    hbm, refs = refs[:12], refs[12:]
    sc, x1_o, a1_o, h_o, d_o, a2_o, q_o, kv_o, kvs_o = refs[:9]
    bb, vl, ts, tw, fs, fw, gains, freq, feat, w1, w2, wq, sems = refs[9:]
    loads = [
        pltpu.make_async_copy(src, dst, sems.at[i])
        for i, (src, dst) in enumerate(zip(hbm, (bb, vl, ts, tw, fs, fw, gains, freq, feat, w1, w2, wq)))
    ]
    for load in loads:
        load.start()
    for load in loads[:8]:
        load.wait()
    sc[0] = bb[0]
    sc[1] = lax.axis_index("blk")
    for i in range(2):
        sc[2 + i] = vl[0, i]
        sc[4 + i] = ts[0, i]
        sc[6 + i] = ts[0, i] + tw[0, i]
        sc[8 + i] = fs[0, i]
        sc[10 + i] = fs[0, i] + fw[0, i]
    for i in range(12, 16):
        sc[i] = 0
    loads = loads[8:]
    rows = feat.shape[0]
    cos, sin = turn_tables(sc, freq[...], rows)
    parts = tiles(rows)
    for i, t in enumerate(parts):
        shape = (t.stop - t.start, 256)
        if i == 0:
            loads[0].wait()
        x = jnp.where(keep_mask(sc, t.start, shape), feat[t, :].astype(F32), 0.0)
        m, _ = unit(x)
        a1 = (m * gains[0:1, :]).astype(BF16)
        a1_o[t, :] = a1
        if i == 0:
            loads[1].wait()
        h, d = silu_parts(mm(a1, w1[...]))
        h = h.astype(BF16)
        h_o[t, :] = h
        d_o[t, :] = d.astype(BF16)
        if i == 0:
            loads[2].wait()
        x1 = x + 0.5 * mm(h, w2[...])
        x1_o[t, :] = x1
        m, _ = unit(x1)
        a2 = (m * gains[1:2, :]).astype(BF16)
        a2_o[t, :] = a2
        if i == 0:
            loads[3].wait()
        qkv = mm(a2, wq[...])
        q_o[t, :] = rotate(qkv[:, 0:256], cos[t], sin[t], 1.0).astype(BF16)
        k = rotate(qkv[:, 256:512], cos[t], sin[t], 1.0).astype(BF16)
        v = qkv[:, 512:768].astype(BF16)
        for o in (kv_o, kvs_o):
            o[t, 0:256] = k
            o[t, 256:512] = v


def gate_kernel(sc, x1, gains, inner, up, a3_o, rest_o, slope_o, n_o, mg_o, rs_o, ea_o, eb_o):
    rows = x1.shape[0]
    for t in tiles(rows):
        m, _ = unit(x1[t, :])
        a3 = (m * gains[2:3, :]).astype(BF16)
        a3_o[t, :] = a3
        y, slope = gelu_parts(mm(a3, up[...]))
        slope_o[t, :] = slope.astype(BF16)
        rest_o[t, :] = y[:, 0:512]
        mg, rs = unit(y[:, 512:1024])
        mg_o[t, :] = mg
        rs_o[t, :] = rs
        n_o[t, :] = (mg * inner[...]).astype(BF16)
    edge_sends(sc, n_o, ea_o, eb_o)


def mixed_kernel(sc, n, ha, hb, rest, taps, down, mixed_o, gated_o, cat_o, wide):
    rows = n.shape[0]
    fill_wide(sc, wide, (n,), ha, hb)
    conv_fwd(sc, wide, taps, mixed_o, rows)
    for t in tiles(rows):
        gated = (rest[t, :] * mixed_o[t, :]).astype(BF16)
        gated_o[t, :] = gated
        cat_o[t, :] = mm(gated, down[...]).astype(BF16)


def head_masks(rows):
    lane = lax.broadcasted_iota(jnp.int32, (rows, LANES), 1)
    return lane


def query_aug(sc, q, h, lane, utt):
    half = h % 2
    pair = q[:, (h // 2) * LANES : (h // 2 + 1) * LANES].astype(F32)
    off = HEAD_DIM * (1 - half)
    flags = jnp.where((lane == off + utt), 1.0, 0.0)
    mine = (lane >> 6) == half
    return jnp.where(mine, pair, flags).astype(BF16), jnp.where(mine, pair, 0.0).astype(BF16)


def key_bias(sc, src, lane, rows):
    row = lax.broadcasted_iota(jnp.int32, (rows, LANES), 0)
    shift = sc[0] - 1
    utt = row & shift
    pos = (row >> shift) + src * (rows >> shift)
    ok = pos < jnp.where(utt == 0, sc[2], sc[3])
    col = lane & 63
    seen = ok & (col == utt)
    return jnp.where((col < 2) & jnp.logical_not(seen), HIDE, 0.0)


def key_aug(kv, h, lane, bias):
    half = h % 2
    pair = kv[:, (h // 2) * LANES : (h // 2 + 1) * LANES].astype(F32)
    mine = (lane >> 6) == half
    return jnp.where(mine, pair, bias).astype(BF16)


def att_kernel(first, final, masks, sc, q, *rest):
    kvs, rest = rest[: len(masks)], rest[len(masks) :]
    if not first:
        c_i, l_i, acc_i = rest[:3]
        rest = rest[3:]
    if final:
        catg, out_w, c_o, l_o, oT_o, ob_o, att_o, ea_o, eb_o, acc_o = rest
    else:
        c_o, l_o, acc_o = rest
    rows = q.shape[0]
    lane = lax.broadcasted_iota(jnp.int32, (rows, LANES), 1)
    utt = lax.broadcasted_iota(jnp.int32, (rows, LANES), 0) & (sc[0] - 1)
    qs = [query_aug(sc, q, h, lane, utt)[0] for h in range(HEADS)]
    if first:
        c_o[...] = jnp.full((8, rows), -1e30, F32)
        l_o[...] = jnp.zeros((8, rows), F32)
        acc_o[...] = jnp.zeros((HEADS * HEAD_DIM, rows), F32)
    else:
        c_o[...] = c_i[...]
        l_o[...] = l_i[...]
        acc_o[...] = acc_i[...]
    for mask, kv in zip(masks, kvs):
        bias = key_bias(sc, sc[1] ^ mask, lane, rows)
        vT = kv[:, 256:512].astype(F32).T.astype(BF16)
        for h in range(HEADS):
            s = mm_nt(key_aug(kv, h, lane, bias), qs[h])
            old = c_o[h : h + 1, :]
            new = jnp.maximum(old, jnp.floor(jnp.max(s, 0, keepdims=True) * EXP_SCALE))
            w = jnp.exp2(s * EXP_SCALE - new)
            scale = jnp.exp2(old - new)
            c_o[h : h + 1, :] = new
            l_o[h : h + 1, :] = l_o[h : h + 1, :] * scale + jnp.sum(w, 0, keepdims=True)
            hr = slice(h * HEAD_DIM, (h + 1) * HEAD_DIM)
            acc_o[hr, :] = acc_o[hr, :] * scale + mm(vT[hr, :], w.astype(BF16))
    if final:
        for h in range(HEADS):
            hr = slice(h * HEAD_DIM, (h + 1) * HEAD_DIM)
            oT_o[hr, :] = acc_o[hr, :] / l_o[h : h + 1, :]
        ob = oT_o[...].T.astype(BF16)
        ob_o[...] = ob
        att_o[...] = mm(ob, out_w[...]).astype(BF16)
        edge_sends(sc, (att_o, catg), ea_o, eb_o)


def merge_kernel(
    sc, att, catg, ha, hb, x1, taps, mw, dout, gains, w1, w2,
    out_o, un_o, em_o, ec_o, df_o, g2_o, a4_o, h_o, e2_o, du_o, gg_o, ea_o, eb_o, wide, conv,
):
    rows = att.shape[0]
    fill_wide(sc, wide, (att, catg), ha, hb)
    conv_fwd(sc, wide, taps, conv, rows)
    g3g = jnp.zeros((1, 256), F32)
    g4g = jnp.zeros((1, 256), F32)
    for t in tiles(rows):
        cat = jnp.concatenate([att[t, :], catg[t, :]], 1).astype(F32)
        united = (cat + conv[t, :]).astype(BF16)
        un_o[t, :] = united
        x2 = x1[t, :] + mm(united, mw[...])
        m2, rs2 = unit(x2)
        a4 = (m2 * gains[3:4, :]).astype(BF16)
        a4_o[t, :] = a4
        h, d = silu_parts(mm(a4, w1[...]))
        h = h.astype(BF16)
        h_o[t, :] = h
        x3 = x2 + 0.5 * mm(h, w2[...])
        m3, rs3 = unit(x3)
        out_o[t, :] = (m3 * gains[4:5, :]).astype(BF16)
        g3, gg = unit_back(dout[t, :], m3, rs3, gains[4:5, :])
        g4g = g4g + gg
        e2 = (0.5 * g3).astype(BF16)
        e2_o[t, :] = e2
        du = (mm_nt(e2, w2[...]) * d).astype(BF16)
        du_o[t, :] = du
        back, gg = unit_back(mm_nt(du, w1[...]), m2, rs2, gains[3:4, :])
        g3g = g3g + gg
        g2 = g3 + back
        g2_o[t, :] = g2
        em = g2.astype(BF16)
        em_o[t, :] = em
        df = mm_nt(em, mw[...])
        df_o[t, :] = df
        ec_o[t, :] = df.astype(BF16)
    gg_o[...] = jnp.concatenate([g3g, g4g, jnp.zeros((6, 256), F32)], 0)
    edge_sends(sc, ec_o, ea_o, eb_o)


def put_cols(buf, row, value):
    n = value.shape[0]
    for c in range(value.shape[1] // 256):
        buf[row + c * n : row + (c + 1) * n, :] = value[:, c * 256 : (c + 1) * 256].astype(BF16)


def grads_kernel(a4, h, e2, du, un, em, buf):
    put_cols(buf, 0, mm_tn(a4[...], du[...]))
    put_cols(buf, 1024, mm_tn(h[...], e2[...]))
    put_cols(buf, 2048, mm_tn(un[...], em[...]))


def split_kernel(
    sc, ec, ha, hb, df, att, catg, rest, mixed, oT, l, taps, down, out_w,
    eatt_o, ecg_o, emix_o, dm_o, eaT_o, ean_o, del_o, tg_o, ea_o, eb_o, wide, conv, catf,
):
    rows = ec.shape[0]
    fill_wide(sc, wide, (ec,), ha, hb)
    conv[...] = df[...]
    catf[:, 0:256] = att[...].astype(F32)
    catf[:, 256:512] = catg[...].astype(F32)
    tg_o[...] = jnp.zeros((32, 512), F32)
    conv_back(sc, wide, taps, catf, conv, tg_o, rows)
    for t in tiles(rows):
        eatt_o[t, :] = conv[t, 0:256].astype(BF16)
        ecg = conv[t, 256:512].astype(BF16)
        ecg_o[t, :] = ecg
        dg = mm_nt(ecg, down[...])
        emix_o[t, :] = (dg * rest[t, :]).astype(BF16)
        dm_o[t, :] = dg * mixed[t, :]
    edge_sends(sc, emix_o, ea_o, eb_o)
    doT = mm_nt(out_w[...], eatt_o[...])
    del_o[...] = jnp.zeros((8, rows), F32)
    for h in range(HEADS):
        hr = slice(h * HEAD_DIM, (h + 1) * HEAD_DIM)
        inv = 1.0 / l[h : h + 1, :]
        eaT = (doT[hr, :] * inv).astype(BF16)
        eaT_o[hr, :] = eaT
        del_o[h : h + 1, :] = jnp.sum(doT[hr, :] * oT[hr, :], 0, keepdims=True) * inv
    ean_o[...] = eaT_o[...].astype(F32).T.astype(BF16)


def attback_kernel(first, masks, sc, q, *rest):
    kvs, rest = rest[: len(masks)], rest[len(masks) :]
    c, eaT, ean, delta = rest[:4]
    rest = rest[4:]
    if first:
        dq_i = None
    else:
        dq_i, rest = rest[0], rest[1:]
    dq_o, d_os = rest[0], rest[1:]
    rows = q.shape[0]
    lane = lax.broadcasted_iota(jnp.int32, (rows, LANES), 1)
    utt = lax.broadcasted_iota(jnp.int32, (rows, LANES), 0) & (sc[0] - 1)
    sub = lax.broadcasted_iota(jnp.int32, (LANES, rows), 0)
    if first:
        dq_o[...] = jnp.zeros((HEADS * HEAD_DIM, rows), F32)
    else:
        dq_o[...] = dq_i[...]
    for mask, kv, d_o in zip(masks, kvs, d_os):
        bias = key_bias(sc, sc[1] ^ mask, lane, rows)
        kT = kv[:, 0:256].astype(F32).T.astype(BF16)
        for pair in range(HEADS // 2):
            cols = slice(pair * LANES, (pair + 1) * LANES)
            vcols = slice(256 + pair * LANES, 256 + (pair + 1) * LANES)
            dk = jnp.zeros((rows, LANES), F32)
            dv = jnp.zeros((rows, LANES), F32)
            for half in range(2):
                h = pair * 2 + half
                hr = slice(h * HEAD_DIM, (h + 1) * HEAD_DIM)
                mine = (lane >> 6) == half
                qa, qm = query_aug(sc, q, h, lane, utt)
                s = mm_nt(key_aug(kv, h, lane, bias), qa)
                w = jnp.exp2(s * EXP_SCALE - c[h : h + 1, :])
                eaTm = jnp.where((sub >> 6) == half, eaT[cols, :].astype(F32), 0.0).astype(BF16)
                dp = mm(kv[:, vcols], eaTm)
                ds = (w * (dp - delta[h : h + 1, :])).astype(BF16)
                eam = jnp.where(mine, ean[:, cols].astype(F32), 0.0).astype(BF16)
                dk = dk + mm(ds, qm)
                dv = dv + mm(w.astype(BF16), eam)
                dq_o[hr, :] += mm(kT[hr, :], ds)
            d_o[:, cols] = (dk * SCORE_SCALE).astype(d_o.dtype)
            d_o[:, vcols] = dv.astype(d_o.dtype)


def gateback_kernel(
    sc, emix, ha, hb, n, mg, rs, dm, slope, a3, x1, gated, ecg, ob, eatt, taps, inner, up, gains,
    bcg_o, gg_o, tg_o, gi_o, buf, wide, conv,
):
    rows = emix.shape[0]
    fill_wide(sc, wide, (emix,), ha, hb)
    conv[...] = jnp.zeros_like(conv)
    tg_o[...] = jnp.zeros((32, 512), F32)
    conv_back(sc, wide, taps, n, conv, tg_o, rows)
    gi = jnp.zeros((1, 512), F32)
    gc = jnp.zeros((1, 256), F32)
    ups = []
    for t in tiles(rows):
        dgate, g = unit_back(conv[t, :], mg[t, :], rs[t, :], inner[...])
        gi = gi + g
        sl = slope[t, :].astype(F32)
        eup = jnp.concatenate([dm[t, :] * sl[:, 0:512], dgate * sl[:, 512:1024]], 1).astype(BF16)
        ups.append(eup)
        m, rs1 = unit(x1[t, :])
        back, g = unit_back(mm_nt(eup, up[...]), m, rs1, gains[2:3, :])
        gc = gc + g
        bcg_o[t, :] = back
    gi_o[...] = jnp.concatenate([gi, jnp.zeros((7, 512), F32)], 0)
    gg_o[...] = jnp.concatenate([gc, jnp.zeros((7, 256), F32)], 0)
    eup = jnp.concatenate(ups, 0)
    put_cols(buf, 0, mm_tn(a3[...], eup))
    put_cols(buf, 1024, mm_tn(gated[...], ecg[...]))
    put_cols(buf, 1536, mm_tn(ob[...], eatt[...]))


def last_kernel(
    sc, dqT, dkv0, dkv1, dkv2, a2, x1, g2, bcg, a1, h, d, freq, wq, gains, feat, w1, w2,
    dx_o, gg_o, buf,
):
    rows = x1.shape[0]
    cos, sin = turn_tables(sc, freq[...], rows)
    dq = dqT[...].T * SCORE_SCALE
    g0 = jnp.zeros((1, 256), F32)
    g1g = jnp.zeros((1, 256), F32)
    eqkvs, e1s, dus = [], [], []
    for t in tiles(rows):
        dkv = dkv0[t, :] + dkv1[t, :].astype(F32) + dkv2[t, :].astype(F32)
        eq = rotate(dq[t], cos[t], sin[t], -1.0).astype(BF16)
        ek = rotate(dkv[:, 0:256], cos[t], sin[t], -1.0).astype(BF16)
        eqkv = jnp.concatenate([eq, ek, dkv[:, 256:512].astype(BF16)], 1)
        eqkvs.append(eqkv)
        m, rs = unit(x1[t, :])
        back, g = unit_back(mm_nt(eqkv, wq[...]), m, rs, gains[1:2, :])
        g1g = g1g + g
        g1 = g2[t, :] + back + bcg[t, :]
        e1 = (0.5 * g1).astype(BF16)
        e1s.append(e1)
        du = (mm_nt(e1, w2[...]) * d[t, :].astype(F32)).astype(BF16)
        dus.append(du)
        keep = keep_mask(sc, t.start, (t.stop - t.start, 256))
        m, rs = unit(jnp.where(keep, feat[t, :].astype(F32), 0.0))
        back, g = unit_back(mm_nt(du, w1[...]), m, rs, gains[0:1, :])
        g0 = g0 + g
        dx_o[t, :] = jnp.where(keep, g1 + back, 0.0)
    gg_o[...] = jnp.concatenate([g0, g1g, jnp.zeros((6, 256), F32)], 0)
    put_cols(buf, 0, mm_tn(a1[...], jnp.concatenate(dus, 0)))
    put_cols(buf, 1024, mm_tn(h[...], jnp.concatenate(e1s, 0)))
    put_cols(buf, 2048, mm_tn(a2[...], jnp.concatenate(eqkvs, 0)))


def join_kernel(left, right, out):
    out[...] = (left[...].astype(F32) + right[...].astype(F32)).astype(BF16)


def rank():
    return lax.axis_index("grp") * lax.axis_size("blk") + lax.axis_index("blk")


def pack_kernel(p1, p2, p3, tg_gate, tg_merge, gi, gg01, gg2, gg34, keep, send, extra):
    half = keep.shape[0]
    extra[0:32, :] = tg_gate[:, 0:256].astype(BF16)
    extra[32:64, :] = tg_gate[:, 256:512].astype(BF16)
    extra[64:96, :] = tg_merge[:, 0:256].astype(BF16)
    extra[96:128, :] = tg_merge[:, 256:512].astype(BF16)
    small = [gg01[0:2, :], gg2[0:1, :], gg34[0:2, :], gi[0:1, 0:256], gi[0:1, 256:512], jnp.zeros((9, 256), F32)]
    extra[128:144, :] = jnp.concatenate(small, 0).astype(BF16)
    extra[144:, :] = jnp.zeros((extra.shape[0] - 144, 256), BF16)
    spans = []
    start = 0
    for ref in (p1, p2, p3, extra):
        n = ref.shape[0]
        for j in range(2):
            low, high = max(start, j * half), min(start + n, (j + 1) * half)
            if low < high:
                spans.append((ref, j, low - start, low - j * half, high - low))
        start += n
    bit = rank() % 2
    for own in range(2):

        @pl.when(bit == own)
        def _():
            for ref, j, at, to, n in spans:
                dst = keep if j == own else send
                dst[to : to + n, :] = ref[at : at + n, :]


def slot_bit(pair):
    index = rank()
    mask = jnp.where(index % 2 == 0, pair[0], pair[1])
    return (index // mask) % 2


def fold_kernel(pair, mine, got, *outs):
    if pair is None:
        outs[0][...] = (mine[...].astype(F32) + got[...].astype(F32)).astype(BF16)
        return
    keep, send = outs
    half = keep.shape[0]
    bit = slot_bit(pair)
    for ref, b in ((send, 1 - bit), (keep, bit)):
        here = pl.ds(pl.multiple_of(b * half, 16), half)
        ref[...] = (mine[here, :].astype(F32) + got[here, :].astype(F32)).astype(BF16)


def grow_kernel(pair, mine, got, out):
    half = mine.shape[0]
    bit = slot_bit(pair)
    out[pl.ds(pl.multiple_of(bit * half, 16), half), :] = mine[...]
    out[pl.ds(pl.multiple_of((1 - bit) * half, 16), half), :] = got[...]


def unpack_kernel(layout, mine, got, *refs):
    count = len(layout)
    outs, bufs, whole, sems = refs[:count], refs[count : 2 * count], refs[2 * count], refs[2 * count + 1]
    half = mine.shape[0]
    bit = rank() % 2
    whole[pl.ds(pl.multiple_of(bit * half, 16), half), :] = mine[...]
    whole[pl.ds(pl.multiple_of((1 - bit) * half, 16), half), :] = got[...]
    copies = []
    for i, (row, n, cols) in enumerate(layout):
        buf = bufs[i]
        if n == 5:
            buf[...] = whole[row : row + 16, :].astype(F32)[0:5, :]
        elif n == 1:
            v = whole[row - 5 : row + 11, :].astype(F32)
            buf[0:1, 0:256] = v[5:6, :]
            buf[0:1, 256:512] = v[6:7, :]
        else:
            full = -(-n // 16) * 16
            for c in range(cols // 256):
                v = whole[row + c * full : row + (c + 1) * full, :].astype(F32)
                buf[:, c * 256 : (c + 1) * 256] = v[0:n, :]
        copies.append(pltpu.make_async_copy(buf, outs[i], sems.at[i]))
        copies[-1].start()
    for copy in copies:
        copy.wait()


def small_call(kernel, outs, ins, us, scratch=(), limit=None, out_space=None):
    vmem = pl.BlockSpec(memory_space=pltpu.VMEM)
    return pl.pallas_call(
        kernel,
        out_shape=[jax.ShapeDtypeStruct(s, d) for s, d in outs],
        in_specs=[vmem] * len(ins),
        out_specs=[vmem if out_space is None else pl.BlockSpec(memory_space=out_space)] * len(outs),
        scratch_shapes=list(scratch),
        compiler_params=pltpu.CompilerParams(vmem_limit_bytes=limit or VMEM_BYTES),
        cost_estimate=pl.CostEstimate(flops=int(us * UNIT), bytes_accessed=1, transcendentals=0),
    )(*ins)


def reduce_all(keep, send, layout):
    grp, blk = lax.axis_size("grp"), lax.axis_size("blk")
    count = grp * blk
    width = keep.shape[1]
    masks = [1 << i for i in range(1, count.bit_length() - 1)]
    first = list(masks)
    second = list(masks)
    if len(masks) > 2:
        first[1], first[2] = first[2], first[1]
        second[0], second[1] = second[1], second[0]
    slots = list(zip(first, second))

    def exchange(value, pair):
        return lax.ppermute(value, AXES, [(i, i ^ pair[i % 2]) for i in range(count)])

    got = exchange(send, (1, 1))
    for pair in slots:
        half = keep.shape[0] // 2
        outs = [((half, width), BF16)] * 2
        keep, send = small_call(functools.partial(fold_kernel, pair), outs, [keep, got], 0.5)
        got = exchange(send, pair)
    (mine,) = small_call(functools.partial(fold_kernel, None), [(keep.shape, BF16)], [keep, got], 0.3)
    for pair in reversed(slots):
        got = exchange(mine, pair)
        shape = (2 * mine.shape[0], width)
        (mine,) = small_call(functools.partial(grow_kernel, pair), [(shape, BF16)], [mine, got], 0.4)
    got = exchange(mine, (1, 1))
    shapes = [(n, cols) for _, n, cols in layout]
    return small_call(
        functools.partial(unpack_kernel, layout), [(s, F32) for s in shapes], [mine, got], 3.0,
        [pltpu.VMEM(s, F32) for s in shapes]
        + [pltpu.VMEM((2 * mine.shape[0], width), BF16), pltpu.SemaphoreType.DMA((len(shapes),))],
        32 * 1024 * 1024, pltpu.HBM,
    )


def plain(kernel, ins, outs, kept, *refs):
    head = refs[: ins]
    made = refs[ins + kept : ins + kept + outs]
    scratch = refs[ins + 2 * kept + outs :]
    kernel(*head, *made, *scratch)


class Layer:
    def __init__(self, plan):
        self.plan = plan
        self.step = 0
        self.have = {}

    def __getitem__(self, key):
        return self.have[key]

    def __setitem__(self, key, value):
        self.have[key] = value

    def run(self, kernel, outs, extra=(), scratch=(), us=1.0):
        name, reads = self.plan[self.step]
        later = [r for _, more in self.plan[self.step + 1 :] for r in more]
        kept = sorted(k for k in self.have if k in later and k not in reads and k != "sc")
        self.step += 1
        smem = pl.BlockSpec(memory_space=pltpu.SMEM)
        vmem = pl.BlockSpec(memory_space=pltpu.VMEM)
        ins = [self.have[r] for r in reads] + list(extra)
        in_specs = [smem if r == "sc" else vmem for r in reads] + [vmem] * len(extra)
        shapes = [jax.ShapeDtypeStruct(s, d) for _, s, d in outs]
        shapes += [jax.ShapeDtypeStruct(self.have[k].shape, self.have[k].dtype) for k in kept]
        made = pl.pallas_call(
            functools.partial(plain, kernel, len(ins), len(outs), len(kept)),
            out_shape=shapes,
            in_specs=in_specs + [vmem] * len(kept),
            out_specs=[vmem] * len(shapes),
            scratch_shapes=list(scratch),
            input_output_aliases={len(ins) + i: len(outs) + i for i in range(len(kept))},
            compiler_params=pltpu.CompilerParams(vmem_limit_bytes=VMEM_BYTES),
            cost_estimate=pl.CostEstimate(flops=int(us * UNIT), bytes_accessed=1, transcendentals=0),
            name=name,
        )(*ins, *[self.have[k] for k in kept])
        for key, value in zip([o[0] for o in outs] + kept, made):
            self.have[key] = value


def swap(value, axis, mask):
    count = math.prod(lax.axis_size(a) for a in axis) if isinstance(axis, tuple) else lax.axis_size(axis)
    return lax.ppermute(value, axis, [(i, i ^ mask) for i in range(count)])


def halo(ea, eb):
    count = lax.axis_size("blk")
    near = [(i, i ^ 1) for i in range(count)]
    far = []
    for i in range(1, count - 1, 2):
        far += [(i, i + 1), (i + 1, i)]
    return lax.ppermute(ea, "blk", near), lax.ppermute(eb, "blk", far)


def local(
    features, d_out, bucket_batch, valid_len, time_start, time_width, freq_start, freq_width,
    gains, inner_gain, ffn1_in, ffn1_out, qkv_w, out_w, cg_up, cg_conv, cg_down, merge_conv,
    merge_w, ffn2_in, ffn2_out,
):
    rows, width = features.shape
    half = cg_down.shape[0]
    ff = ffn1_in.shape[1]
    blocks = lax.axis_size("blk")
    me = lax.axis_index("blk")
    freq = np.exp(np.arange(32, dtype=np.float64) * (-2.0 * math.log(10000.0) / HEAD_DIM))
    freq = jnp.asarray(np.tile(freq, 4)[None, :].astype(np.float32))
    wide = pltpu.VMEM((half // LANES, rows + 2 * HALO, LANES), F32)
    plane = pltpu.VMEM((rows, half), F32)
    pairs = [(m, m | 1) for m in range(0, blocks, 2)]
    kvs = [(f"kv{a}", f"kv{b}") for a, b in pairs]
    even = [a for a, _ in pairs[1:]]
    state = ["c", "l", "acc"]
    plan = [("gate", ["sc", "x1"])]
    plan += [("att_first", ["sc", "q", *kvs[0]])]
    plan += [("mixed", ["sc", "n", "na", "nb", "rest"])]
    far_masks = [m for a, b in pairs[1:] for m in (a, b)]
    plan += [("att_mid", ["sc", "q", f"kv{m}", *state]) for m in far_masks[:-1]]
    plan += [
        ("att_last", ["sc", "q", f"kv{far_masks[-1]}", *state, "catg"]),
        ("merge", ["sc", "att", "catg", "ha", "hb", "x1"]),
        ("grads2", ["a4", "h2", "e2", "du2", "un", "em"]),
        ("split", ["sc", "ec", "ca", "cb", "df", "att", "catg", "rest", "mixed", "oT", "l"]),
    ]
    back = ["c", "eaT", "ean", "delta"]
    for e in even:
        for m in (e + 1, e):
            plan += [("attback", ["sc", "q", f"kv{m}", *back] + (["dqT"] if m != even[0] + 1 else []))]
        plan += [("join_kv", [f"pd{e}", f"in{e}"])]
    plan += [("attback", ["sc", "q", "kv1", "kv0", *back, "dqT"])]
    plan += [
        ("gateback", ["sc", "emix", "ma", "mb", "n", "mg", "rs", "dm", "slope", "a3", "x1", "gated", "ecg", "ob", "eatt"]),
    ]
    total = f"far{even[0]}"
    for e in even[1:]:
        plan += [("join_far", [total, f"far{e}"])]
        total = f"t{e}"
    plan += [
        ("last", ["sc", "dqT", "own", "near", total, "a2", "x1", "g2", "bcg", "a1", "h1", "d1"]),
        ("pack", ["part1", "buf2", "buf3", "tg_gate", "tg_merge", "gi", "gg01", "gg2", "gg34"]),
    ]
    run = Layer(plan)
    smem = pl.BlockSpec(memory_space=pltpu.SMEM)
    vmem = pl.BlockSpec(memory_space=pltpu.VMEM)
    raw = (bucket_batch, valid_len, time_start, time_width, freq_start, freq_width, gains, freq,
           features, ffn1_in, ffn1_out, qkv_w)
    def narrow(name, kind=BF16):
        return (name, (rows, width), kind)

    def middle(name, kind=BF16):
        return (name, (rows, half), kind)

    def broad(name, kind=BF16):
        return (name, (rows, ff), kind)

    outs = [narrow("x1", F32), narrow("a1"), broad("h1"), broad("d1"), narrow("a2"), narrow("q"), middle("kv0"), middle("kvs")]
    made = pl.pallas_call(
        pre_kernel,
        out_shape=[jax.ShapeDtypeStruct((16,), jnp.int32)] + [jax.ShapeDtypeStruct(o[1], o[2]) for o in outs],
        in_specs=[pl.BlockSpec(memory_space=pltpu.HBM)] * 12,
        out_specs=[smem] + [vmem] * 8,
        scratch_shapes=[pltpu.SMEM(v.shape, v.dtype) for v in raw[:6]]
        + [pltpu.VMEM(v.shape, v.dtype) for v in raw[6:]] + [pltpu.SemaphoreType.DMA((12,))],
        compiler_params=pltpu.CompilerParams(vmem_limit_bytes=VMEM_BYTES),
        cost_estimate=pl.CostEstimate(flops=int(4.0 * UNIT), bytes_accessed=1, transcendentals=0),
        name="pre",
    )(raw[0], *[pltpu.with_memory_space_constraint(v, pltpu.HBM) for v in raw[1:]])
    for key, value in zip(["sc"] + [o[0] for o in outs], made):
        run[key] = value
    held = {0: run["kvs"]}
    bit = blocks // 2
    while bit > 1:
        held.update({m | bit: swap(held[m], "blk", bit) for m in list(held)})
        bit //= 2
    held[1] = swap(held[0], "blk", 1)

    def send_edges():
        return halo(run["ea"], run["eb"])

    edge = [("ea", (HALO, half), BF16), ("eb", (HALO, half), BF16)]
    stats = [("c", (8, rows), F32), ("l", (8, rows), F32)]

    run.run(
        gate_kernel,
        [narrow("a3"), middle("rest", F32), broad("slope"), middle("n"), middle("mg", F32), ("rs", (rows, 1), F32)] + edge,
        [gains, inner_gain[None, :], cg_up], us=2.5,
    )
    edges = send_edges()
    run["kv1"] = held[1]
    run.run(functools.partial(att_kernel, True, False, pairs[0]), stats + [("acc", (width, rows), F32)], us=0.5)
    run["na"], run["nb"] = edges
    run.run(
        mixed_kernel, [middle("mixed", F32), middle("gated"), narrow("catg")],
        [cg_conv, cg_down], [wide], us=5.3,
    )
    for a, b in pairs[1:]:
        late, _ = lax.optimization_barrier((held[a], run["catg"]))
        run[f"kv{a}"] = late
        mate = swap(late, "blk", 1)
        run.run(
            functools.partial(att_kernel, False, False, (a,)), stats + [("acc", (width, rows), F32)], us=2.8,
        )
        run[f"kv{b}"] = mate
        if b < blocks - 1:
            run.run(
                functools.partial(att_kernel, False, False, (b,)), stats + [("acc", (width, rows), F32)], us=2.8,
            )
    run.run(
        functools.partial(att_kernel, False, True, (blocks - 1,)),
        stats + [("oT", (width, rows), F32), narrow("ob"), narrow("att")] + edge,
        [out_w], [pltpu.VMEM((width, rows), F32)], us=3.0,
    )
    run["ha"], run["hb"] = send_edges()
    run.run(
        merge_kernel,
        [narrow("out"), middle("un"), narrow("em"), middle("ec"), middle("df", F32), narrow("g2", F32), narrow("a4"),
         broad("h2"), narrow("e2"), broad("du2"), ("gg34", (8, width), F32)] + edge,
        [merge_conv, merge_w, d_out, gains, ffn2_in, ffn2_out], [wide, plane], us=9.1,
    )
    edges = send_edges()
    run.run(grads_kernel, [("part1", (2560, width), BF16)], us=0.9)
    run["ca"], run["cb"] = edges
    run.run(
        split_kernel,
        [narrow("eatt"), narrow("ecg"), middle("emix"), middle("dm", F32), ("eaT", (width, rows), BF16), narrow("ean"),
         ("delta", (8, rows), F32), ("tg_merge", (32, half), F32)] + edge,
        [merge_conv, cg_down, out_w], [wide, plane, plane], us=8.3,
    )
    edges = send_edges()

    tall = ("dqT", (width, rows), F32)
    pair_sum = (rows, 2 * width)
    for e in even:
        for m in (e + 1, e):
            run.run(
                functools.partial(attback_kernel, m == even[0] + 1, (m,)), [tall, (f"pd{m}", pair_sum, BF16)], us=0.5
            )
            if m == even[0] + 1:
                run["ma"], run["mb"] = edges
            if m & 1:
                arrival = swap(run[f"pd{m}"], "blk", 1)
        run[f"in{e}"] = arrival
        run.run(join_kernel, [(f"s{e}", pair_sum, BF16)], us=0.2)
    fars = {e: swap(run[f"s{e}"], "blk", e) for e in even}
    run.run(
        functools.partial(attback_kernel, False, (1, 0)), [tall, ("pd1", pair_sum, BF16), ("own", pair_sum, F32)], us=6.3
    )
    near = swap(run["pd1"], "blk", 1)
    run.run(
        gateback_kernel,
        [narrow("bcg", F32), ("gg2", (8, width), F32), ("tg_gate", (32, half), F32), ("gi", (8, half), F32),
         ("buf2", (1792, width), BF16)],
        [cg_conv, inner_gain[None, :], cg_up, gains], [wide, plane], us=1.0,
    )
    run["near"] = near
    for e in even:
        run[f"far{e}"] = fars[e]
    for e in even[1:]:
        run.run(join_kernel, [(f"t{e}", pair_sum, BF16)], us=0.2)
    run.run(
        last_kernel,
        [narrow("dx", F32), ("gg01", (8, width), F32), ("buf3", (2816, width), BF16)],
        [freq, qkv_w, gains, features, ffn1_in, ffn1_out], us=4.2,
    )
    count = lax.axis_size("grp") * blocks
    used = 2560 + 1792 + 2816 + 144
    total = -(-used // (16 * count)) * 16 * count
    run.run(
        pack_kernel, [("keep", (total // 2, width), BF16), ("send", (total // 2, width), BF16)],
        (), [pltpu.VMEM((total - used + 144, width), BF16)], us=1.0,
    )
    layout = (
        (7296, 5, 256), (7301, 1, 512), (4352, 256, 1024), (5376, 1024, 256), (6400, 256, 768), (4096, 256, 256),
        (2560, 256, 1024), (7168, 31, 512), (3584, 512, 256), (7232, 31, 512), (2048, 512, 256), (0, 256, 1024),
        (1024, 1024, 256),
    )
    sums = reduce_all(run["keep"], run["send"], layout)
    return (run["out"], run["dx"], sums[0], sums[1][0], *sums[2:])


def solution(mesh):
    rows = P(("grp", "blk"), None)
    in_specs = (rows, rows, P("grp")) + (P("grp", None),) * 5 + (P(),) * 13
    out_specs = (rows, rows) + (P(),) * 13
    return jax.shard_map(local, mesh=mesh, in_specs=in_specs, out_specs=out_specs, check_vma=False)
```

```python
import functools
import math

import jax
import jax.numpy as jnp
import numpy as np
from jax import lax
from jax.experimental import pallas as pl
from jax.experimental.pallas import tpu as pltpu
from jax.sharding import PartitionSpec as P

HEADS = 4
HEAD_DIM = 64
HALO = 32
LOG_BASE = 1.4426950408889634
EPSILON = 1e-05
SCORE_SCALE = HEAD_DIM ** (-0.5)
EXP_SCALE = SCORE_SCALE * LOG_BASE
HIDE = -(2.0 ** 100)
AXES = ("grp", "blk")
F32 = jnp.float32
BF16 = jnp.bfloat16
LANES = 128
VMEM_BYTES = 16 * 1024 * 1024
UNIT = 0.35e9
CARRY_BYTES = 30 * 1024 * 1024


def mm(left, right):
    return jnp.dot(left, right, preferred_element_type=F32)


def mm_nt(left, right):
    return lax.dot_general(left, right, (((1,), (1,)), ((), ())), preferred_element_type=F32)


def mm_tn(left, right):
    return lax.dot_general(left, right, (((0,), (0,)), ((), ())), preferred_element_type=F32)


def unit(v):
    center = v - jnp.mean(v, -1, keepdims=True)
    rs = lax.rsqrt(jnp.mean(center * center, -1, keepdims=True) + EPSILON)
    return center * rs, rs


def unit_back(up, m, rs, gain):
    eg = up * gain
    return rs * (eg - jnp.mean(eg, -1, keepdims=True) - m * jnp.mean(eg * m, -1, keepdims=True))


def silu_parts(u):
    sig = 0.5 + 0.5 * jnp.tanh(0.5 * u)
    h = u * sig
    return h, sig + h * (1.0 - sig)


def gelu_parts(t):
    root = math.sqrt(2.0 / math.pi)
    t2 = t * t
    th = jnp.tanh(root * t * (1.0 + 0.044715 * t2))
    half = 0.5 + 0.5 * th
    slope = half + 0.5 * root * t * (1.0 - th * th) * (1.0 + 3.0 * 0.044715 * t2)
    return t * half, slope


def rows_of(sc, r0, shape):
    row = lax.broadcasted_iota(jnp.int32, shape, 0) + r0
    shift = sc[0] - 1
    utt = row & shift
    pos = (row >> shift) + sc[1] * (512 >> shift)
    return utt, pos


def keep_mask(sc, r0, shape):
    utt, pos = rows_of(sc, r0, shape)
    ch = lax.broadcasted_iota(jnp.int32, shape, 1)
    first = utt == 0

    def pick(i):
        return jnp.where(first, sc[i], sc[i + 1])

    ok = (pos < pick(2)) & jnp.logical_not((pos >= pick(4)) & (pos < pick(6)))
    ok = ok & jnp.logical_not((ch >= pick(8)) & (ch < pick(10)))
    return ok


def turn_tables(sc, freq, rows):
    shift = sc[0] - 1
    coarse = lax.broadcasted_iota(jnp.int32, (rows // 16, LANES), 0) * 16
    fine = lax.broadcasted_iota(jnp.int32, (16, LANES), 0)
    a = ((coarse >> shift) + sc[1] * (rows >> shift)).astype(F32) * freq
    c = (fine >> shift).astype(F32) * freq
    ca, sa, cc, cs = jnp.cos(a), jnp.sin(a), jnp.cos(c), jnp.sin(c)
    cos = ca[:, None, :] * cc[None] - sa[:, None, :] * cs[None]
    sin = sa[:, None, :] * cc[None] + ca[:, None, :] * cs[None]
    return cos.reshape(rows, LANES), sin.reshape(rows, LANES)


def rotate(v, cos, sin, direction):
    lane = lax.broadcasted_iota(jnp.int32, (v.shape[0], LANES), 1)
    lower = (lane & 63) < 32
    signed = jnp.where(lower, -direction, direction) * sin
    parts = []
    for i in range(v.shape[1] // LANES):
        p = v[:, i * LANES : (i + 1) * LANES]
        other = jnp.where(lower, pltpu.roll(p, LANES - 32, 1), pltpu.roll(p, 32, 1))
        parts.append(p * cos + other * signed)
    return jnp.concatenate(parts, 1)


def edge_sends(sc, refs, a_ref, b_ref):
    odd = (sc[1] & 1) == 1
    col = 0
    count = a_ref.shape[0]
    for ref in refs if isinstance(refs, tuple) else (refs,):
        rows, width = ref.shape
        first = ref[0:count, :].astype(BF16)
        last = ref[rows - count : rows, :].astype(BF16)
        cols = slice(col, col + width)
        col += width

        @pl.when(odd)
        def _():
            a_ref[:, cols] = first
            b_ref[:, cols] = last

        @pl.when(jnp.logical_not(odd))
        def _():
            a_ref[:, cols] = last
            b_ref[:, cols] = first


def sides(sc, ha, hb, cols, before, after):
    odd = (sc[1] & 1) == 1
    first = jnp.where(odd, ha[before, cols].astype(F32), hb[before, cols].astype(F32))
    return first, jnp.where(odd, hb[after, cols].astype(F32), ha[after, cols].astype(F32))


LOWER, UPPER = slice(0, HALO), slice(HALO, 2 * HALO)


def fill_wide(sc, wide, sources, ha, hb, spots=None):
    at = 0
    for z in sources:
        rows, width = z.shape
        for c in range(width // LANES):
            cols = slice(at * LANES, (at + 1) * LANES)
            if spots is None:
                before, after = ha[:, cols].astype(F32), hb[:, cols].astype(F32)
            else:
                before, after = sides(sc, ha, hb, cols, *spots)
            wide[at, 0:HALO, :] = before
            wide[at, HALO : HALO + rows, :] = z[:, c * LANES : (c + 1) * LANES].astype(F32)
            wide[at, HALO + rows : 2 * HALO + rows, :] = after
            at += 1


CONV_ROWS = 128
TAPS = 31


def local_conv_kernel(direction, add, sc, *refs):
    *sources, taps, out, wide = refs
    if add:
        base, sources = sources[0], sources[1:]
        out[...] = base[...]
    rows = out.shape[0]
    at = 0
    for z in sources:
        for c in range(z.shape[1] // LANES):
            wide[at, 0:HALO, :] = jnp.zeros((HALO, LANES), F32)
            wide[at, HALO : HALO + rows, :] = z[:, c * LANES : (c + 1) * LANES].astype(F32)
            wide[at, HALO + rows : 2 * HALO + rows, :] = jnp.zeros((HALO, LANES), F32)
            at += 1
    conv(sc, wide, taps, out, rows, direction, add)


def add_edges(sc, rim, taps, ha, hb, spots, plane, out, direction):
    step = sc[0] * direction
    rows = plane.shape[0]
    for c in range(taps.shape[1] // LANES):
        cols = slice(c * LANES, (c + 1) * LANES)
        before, after = sides(sc, ha, hb, cols, *spots)
        rim[c, 0:HALO, :] = before
        rim[c, HALO : 5 * HALO, :] = jnp.zeros((4 * HALO, LANES), F32)
        rim[c, 5 * HALO : 6 * HALO, :] = after
    if out is not plane:
        out[HALO : rows - HALO, :] = plane[HALO : rows - HALO, :]
    for c in range(taps.shape[1] // LANES):
        cols = slice(c * LANES, (c + 1) * LANES)
        for base, start in ((0, 0), (3 * HALO, rows - HALO)):
            acc = plane[start : start + HALO, cols]
            for k in range(TAPS):
                tap = taps[k : k + 1, cols].astype(F32)
                acc = acc + rim[c, pl.ds(base + HALO + step * (k - TAPS // 2), HALO), :] * tap
            out[start : start + HALO, cols] = acc


def conv(sc, wide, taps, out, rows, direction, add):
    step = sc[0] * direction
    for c in range(taps.shape[1] // LANES):
        cols = slice(c * LANES, (c + 1) * LANES)
        ws = [taps[k : k + 1, cols].astype(F32) for k in range(TAPS)]

        def body(i, carry):
            r0 = pl.multiple_of(i * CONV_ROWS, CONV_ROWS)
            here = pl.ds(r0, CONV_ROWS)
            acc = out[here, cols] if add else jnp.zeros((CONV_ROWS, LANES), F32)
            for k in range(TAPS):
                acc = acc + wide[c, pl.ds(r0 + HALO + step * (k - TAPS // 2), CONV_ROWS), :] * ws[k]
            out[here, cols] = acc
            return carry

        lax.fori_loop(0, rows // CONV_ROWS, body, 0)


def correlate(sc, wide, sources, out, row, rows):
    batch = sc[0]
    blocks = [(z, c) for z in sources for c in range(z.shape[1] // LANES)]
    for at, (z, c) in enumerate(blocks):
        cols = slice(c * LANES, (c + 1) * LANES)
        for start, stop in ((0, 16), (16, TAPS)):

            def body(i, sums):
                r0 = pl.multiple_of(i * CONV_ROWS, CONV_ROWS)
                zc = z[pl.ds(r0, CONV_ROWS), cols].astype(F32)
                new = []
                for k in range(start, stop):
                    e = wide[at, pl.ds(r0 + HALO - batch * (k - TAPS // 2), CONV_ROWS), :]
                    new.append(sums[k - start] + jnp.sum((e * zc).reshape(CONV_ROWS // 8, 8, LANES), 0))
                return tuple(new)

            zero = tuple(jnp.zeros((8, LANES), F32) for _ in range(stop - start))
            sums = lax.fori_loop(0, rows // CONV_ROWS, body, zero)
            for k in range(start, stop):
                to = row + at * TAPS + k
                out[to : to + 1, :] = jnp.sum(sums[k - start], 0, keepdims=True)


def taps_kernel(sc, ec, ca, cb, att, catg, emix, before, after, n, g4, gi, small_o, wide, total):
    rows = ec.shape[0]
    fill_wide(sc, wide, (ec,), ca, cb, (UPPER, LOWER))
    correlate(sc, wide, (att, catg), total, 0, rows)
    fill_wide(sc, wide, (emix,), before, after)
    correlate(sc, wide, (n,), total, 4 * TAPS, rows)
    at = 8 * TAPS
    for ref in (g4, gi):
        for c in range(ref.shape[1] // LANES):
            total[at : at + 1, :] = ref[0:1, c * LANES : (c + 1) * LANES]
            at += 1
    total[at:, :] = jnp.zeros((total.shape[0] - at, LANES), F32)
    small_o[...] = total[...].astype(BF16)


def tiles(rows, size=256):
    size = min(size, rows)
    return [slice(i, i + size) for i in range(0, rows, size)]


def pre_kernel(*refs):
    hbm, refs = refs[:12], refs[12:]
    sc, x1_o, a1_o, h_o, d_o, a2_o, q_o, kv_o, kvs_o = refs[:9]
    bb, vl, ts, tw, fs, fw, gains, freq, feat, w1, w2, wq, sems = refs[9:]
    loads = [
        pltpu.make_async_copy(src, dst, sems.at[i])
        for i, (src, dst) in enumerate(zip(hbm, (bb, vl, ts, tw, fs, fw, gains, freq, feat, w1, w2, wq)))
    ]
    for load in loads:
        load.start()
    for load in loads[:8]:
        load.wait()
    sc[0] = bb[0]
    sc[1] = lax.axis_index("blk")
    for i in range(2):
        sc[2 + i] = vl[0, i]
        sc[4 + i] = ts[0, i]
        sc[6 + i] = ts[0, i] + tw[0, i]
        sc[8 + i] = fs[0, i]
        sc[10 + i] = fs[0, i] + fw[0, i]
    for i in range(12, 16):
        sc[i] = 0
    loads = loads[8:]
    rows = feat.shape[0]
    cos, sin = turn_tables(sc, freq[...], rows)
    parts = tiles(rows)
    for i, t in enumerate(parts):
        shape = (t.stop - t.start, 256)
        if i == 0:
            loads[0].wait()
        x = jnp.where(keep_mask(sc, t.start, shape), feat[t, :].astype(F32), 0.0)
        m, _ = unit(x)
        a1 = (m * gains[0:1, :]).astype(BF16)
        a1_o[t, :] = a1
        if i == 0:
            loads[1].wait()
        h, d = silu_parts(mm(a1, w1[...]))
        h = h.astype(BF16)
        h_o[t, :] = h
        d_o[t, :] = d.astype(BF16)
        if i == 0:
            loads[2].wait()
        x1 = x + 0.5 * mm(h, w2[...])
        x1_o[t, :] = x1
        m, _ = unit(x1)
        a2 = (m * gains[1:2, :]).astype(BF16)
        a2_o[t, :] = a2
        if i == 0:
            loads[3].wait()
        qkv = mm(a2, wq[...])
        q_o[t, :] = rotate(qkv[:, 0:256], cos[t], sin[t], 1.0).astype(BF16)
        k = rotate(qkv[:, 256:512], cos[t], sin[t], 1.0).astype(BF16)
        v = qkv[:, 512:768].astype(BF16)
        for o in (kv_o, kvs_o):
            o[t, 0:256] = k
            o[t, 256:512] = v


def gate_kernel(sc, x1, gains, inner, up, a3_o, rest_o, slope_o, n_o, mg_o, rs_o, ea_o, eb_o):
    rows = x1.shape[0]
    for t in tiles(rows):
        m, _ = unit(x1[t, :])
        a3 = (m * gains[2:3, :]).astype(BF16)
        a3_o[t, :] = a3
        y, slope = gelu_parts(mm(a3, up[...]))
        slope_o[t, :] = slope.astype(BF16)
        rest_o[t, :] = y[:, 0:512]
        mg, rs = unit(y[:, 512:1024])
        mg_o[t, :] = mg
        rs_o[t, :] = rs
        n_o[t, :] = (mg * inner[...]).astype(BF16)
    edge_sends(sc, n_o, ea_o.at[HALO:], eb_o.at[HALO:])
    edge_sends(sc, rest_o, ea_o.at[0:HALO], eb_o.at[0:HALO])


def mixed_kernel(sc, plane, ha, hb, rest, taps, down, mixed_o, gated_o, cat_o, rim):
    rows = plane.shape[0]
    add_edges(sc, rim, taps, ha, hb, (UPPER, UPPER), plane, mixed_o, 1)
    for t in tiles(rows):
        gated = (rest[t, :] * mixed_o[t, :]).astype(BF16)
        gated_o[t, :] = gated
        cat_o[t, :] = mm(gated, down[...]).astype(BF16)


def head_masks(rows):
    lane = lax.broadcasted_iota(jnp.int32, (rows, LANES), 1)
    return lane


def query_aug(sc, q, h, lane, utt):
    half = h % 2
    pair = q[:, (h // 2) * LANES : (h // 2 + 1) * LANES].astype(F32)
    off = HEAD_DIM * (1 - half)
    flags = jnp.where((lane == off + utt), 1.0, 0.0)
    mine = (lane >> 6) == half
    return jnp.where(mine, pair, flags).astype(BF16), jnp.where(mine, pair, 0.0).astype(BF16)


def key_bias(sc, src, lane, rows):
    row = lax.broadcasted_iota(jnp.int32, (rows, LANES), 0)
    shift = sc[0] - 1
    utt = row & shift
    pos = (row >> shift) + src * (rows >> shift)
    ok = pos < jnp.where(utt == 0, sc[2], sc[3])
    col = lane & 63
    seen = ok & (col == utt)
    return jnp.where((col < 2) & jnp.logical_not(seen), HIDE, 0.0)


def key_aug(kv, h, lane, bias):
    half = h % 2
    pair = kv[:, (h // 2) * LANES : (h // 2 + 1) * LANES].astype(F32)
    mine = (lane >> 6) == half
    return jnp.where(mine, pair, bias).astype(BF16)


def att_kernel(first, final, masks, sc, q, *rest):
    kvs, rest = rest[: len(masks)], rest[len(masks) :]
    if not first:
        c_i, l_i, acc_i = rest[:3]
        rest = rest[3:]
    if final:
        catg, out_w, c_o, l_o, *blocks, oT_o, ob_o, att_o, ea_o, eb_o, acc_o = rest
    else:
        c_o, l_o, *blocks, acc_o = rest
    if first:
        qm_o, blocks = blocks[0], blocks[1:]
    rows = q.shape[0]
    lane = lax.broadcasted_iota(jnp.int32, (rows, LANES), 1)
    utt = lax.broadcasted_iota(jnp.int32, (rows, LANES), 0) & (sc[0] - 1)
    qs = []
    for h in range(HEADS):
        with_flags, alone = query_aug(sc, q, h, lane, utt)
        qs.append(with_flags)
        if first:
            qm_o[h * rows : (h + 1) * rows, :] = alone
    if first:
        c_o[...] = jnp.full((8, rows), -1e30, F32)
        l_o[...] = jnp.zeros((8, rows), F32)
        acc_o[...] = jnp.zeros((HEADS * HEAD_DIM, rows), F32)
    else:
        c_o[...] = c_i[...]
        l_o[...] = l_i[...]
        acc_o[...] = acc_i[...]
    for mask, kv, w_o, top_o in zip(masks, kvs, blocks[0::2], blocks[1::2]):
        bias = key_bias(sc, sc[1] ^ mask, lane, rows)
        vT = kv[:, 256:512].astype(F32).T.astype(BF16)
        for h in range(HEADS):
            s = mm_nt(key_aug(kv, h, lane, bias), qs[h])
            old = c_o[h : h + 1, :]
            new = jnp.maximum(old, jnp.floor(jnp.max(s, 0, keepdims=True) * EXP_SCALE))
            w = jnp.exp2(s * EXP_SCALE - new)
            low = w.astype(BF16)
            w_o[h * rows : (h + 1) * rows, :] = low
            scale = jnp.exp2(old - new)
            c_o[h : h + 1, :] = new
            l_o[h : h + 1, :] = l_o[h : h + 1, :] * scale + jnp.sum(w, 0, keepdims=True)
            hr = slice(h * HEAD_DIM, (h + 1) * HEAD_DIM)
            acc_o[hr, :] = acc_o[hr, :] * scale + mm(vT[hr, :], low)
        top_o[...] = c_o[...]
    if final:
        for h in range(HEADS):
            hr = slice(h * HEAD_DIM, (h + 1) * HEAD_DIM)
            oT_o[hr, :] = acc_o[hr, :] / l_o[h : h + 1, :]
        ob = oT_o[...].T.astype(BF16)
        ob_o[...] = ob
        att_o[...] = mm(ob, out_w[...]).astype(BF16)
        edge_sends(sc, (att_o, catg), ea_o, eb_o)


def merge_kernel(
    sc, plane_i, att, catg, ha, hb, x1, taps, mw, dout, gains, w1, w2,
    out_o, un_o, em_o, ec_o, df_o, g2_o, a4_o, h_o, e2_o, du_o, g4_o, ea_o, eb_o, rim, plane,
):
    rows = att.shape[0]
    add_edges(sc, rim, taps, ha, hb, (LOWER, LOWER), plane_i, plane, 1)
    g4g = jnp.zeros((1, 256), F32)
    for t in tiles(rows):
        cat = jnp.concatenate([att[t, :], catg[t, :]], 1).astype(F32)
        united = (cat + plane[t, :]).astype(BF16)
        un_o[t, :] = united
        x2 = x1[t, :] + mm(united, mw[...])
        m2, rs2 = unit(x2)
        a4 = (m2 * gains[3:4, :]).astype(BF16)
        a4_o[t, :] = a4
        h, d = silu_parts(mm(a4, w1[...]))
        h = h.astype(BF16)
        h_o[t, :] = h
        x3 = x2 + 0.5 * mm(h, w2[...])
        m3, rs3 = unit(x3)
        out_o[t, :] = (m3 * gains[4:5, :]).astype(BF16)
        g3 = unit_back(dout[t, :], m3, rs3, gains[4:5, :])
        g4g = g4g + jnp.sum(dout[t, :] * m3, 0, keepdims=True)
        e2 = (0.5 * g3).astype(BF16)
        e2_o[t, :] = e2
        du = (mm_nt(e2, w2[...]) * d).astype(BF16)
        du_o[t, :] = du
        g2 = g3 + unit_back(mm_nt(du, w1[...]), m2, rs2, gains[3:4, :])
        g2_o[t, :] = g2
        em = g2.astype(BF16)
        em_o[t, :] = em
        df = mm_nt(em, mw[...])
        df_o[t, :] = df
        ec_o[t, :] = df.astype(BF16)
    g4_o[...] = jnp.broadcast_to(g4g, (8, 256))
    edge_sends(sc, ec_o, ea_o, eb_o)


def put_cols(buf, row, value):
    n = value.shape[0]
    for c in range(value.shape[1] // LANES):
        buf[row + c * n : row + (c + 1) * n, :] = value[:, c * LANES : (c + 1) * LANES].astype(BF16)


def grads_kernel(a4, h, e2, du, un, em, buf):
    put_cols(buf, 0, mm_tn(a4[...], du[...]))
    put_cols(buf, 2048, mm_tn(h[...], e2[...]))
    put_cols(buf, 4096, mm_tn(un[...], em[...]))


def split_kernel(
    sc, plane_i, ec, ha, hb, na, nb, rest, mixed, oT, l, taps, down, out_w,
    eatt_o, ecg_o, emix_o, dm_o, eaT_o, del_o, mb_o, ma_o, rim, plane,
):
    rows = plane_i.shape[0]
    add_edges(sc, rim, taps, ha, hb, (UPPER, LOWER), plane_i, plane, -1)
    for t in tiles(rows):
        eatt_o[t, :] = plane[t, 0:256].astype(BF16)
        ecg = plane[t, 256:512].astype(BF16)
        ecg_o[t, :] = ecg
        dg = mm_nt(ecg, down[...])
        emix_o[t, :] = (dg * rest[t, :]).astype(BF16)
        dm_o[t, :] = dg * mixed[t, :]
    every = slice(0, 2 * HALO)
    outside = []
    for c in range(2):
        cols = slice((c + 2) * LANES, (c + 3) * LANES)
        before, after = sides(sc, ha, hb, cols, every, every)
        rim[c, 0 : 2 * HALO, :] = before
        rim[c, 2 * HALO : 3 * HALO, :] = ec[0:HALO, cols].astype(F32)
        rim[c, 3 * HALO : 4 * HALO, :] = ec[rows - HALO : rows, cols].astype(F32)
        rim[c, 4 * HALO : 6 * HALO, :] = after
        parts = []
        for base in (0, 3 * HALO):
            acc = rim[c, base + HALO : base + 2 * HALO, :]
            for k in range(TAPS):
                tap = taps[k : k + 1, cols].astype(F32)
                acc = acc + rim[c, pl.ds(base + HALO - sc[0] * (k - TAPS // 2), HALO), :] * tap
            parts.append(acc)
        outside.append(jnp.concatenate(parts, 0))
    dg = mm_nt(jnp.concatenate(outside, 1).astype(BF16), down[...])
    before, after = sides(sc, na, nb, slice(None), LOWER, LOWER)
    mb_o[...] = (dg[0:HALO, :] * before).astype(BF16)
    ma_o[...] = (dg[HALO : 2 * HALO, :] * after).astype(BF16)
    doT = mm_nt(out_w[...], eatt_o[...])
    del_o[...] = jnp.zeros((8, rows), F32)
    for h in range(HEADS):
        hr = slice(h * HEAD_DIM, (h + 1) * HEAD_DIM)
        inv = 1.0 / l[h : h + 1, :]
        eaT = (doT[hr, :] * inv).astype(BF16)
        eaT_o[hr, :] = eaT
        del_o[h : h + 1, :] = jnp.sum(doT[hr, :] * oT[hr, :], 0, keepdims=True) * inv


def attback_kernel(first, kv, w, top, qm, c, eaT, delta, *rest):
    if first:
        dq_i = None
    else:
        dq_i, rest = rest[0], rest[1:]
    dq_o, d_o = rest
    rows = kv.shape[0]
    lane = lax.broadcasted_iota(jnp.int32, (rows, LANES), 1)
    nothing = jnp.zeros((HEAD_DIM, rows), BF16)
    kT = kv[:, 0:256].astype(F32).T.astype(BF16)
    for pair in range(HEADS // 2):
        cols = slice(pair * LANES, (pair + 1) * LANES)
        vcols = slice(256 + pair * LANES, 256 + (pair + 1) * LANES)
        scales = [jnp.exp2(top[h : h + 1, :] - c[h : h + 1, :]) for h in (2 * pair, 2 * pair + 1)]
        heads = [slice(h * HEAD_DIM, (h + 1) * HEAD_DIM) for h in (2 * pair, 2 * pair + 1)]
        grown = jnp.concatenate([eaT[hr, :].astype(F32) * r for hr, r in zip(heads, scales)], 0)
        ea = grown.T
        dk = jnp.zeros((rows, LANES), F32)
        dv = jnp.zeros((rows, LANES), F32)
        for half in range(2):
            h = pair * 2 + half
            hr = heads[half]
            here = slice(h * rows, (h + 1) * rows)
            mine = grown[half * HEAD_DIM : (half + 1) * HEAD_DIM, :].astype(BF16)
            dp = mm(kv[:, vcols], jnp.concatenate([mine, nothing] if half == 0 else [nothing, mine], 0))
            low = w[here, :]
            ds = (low.astype(F32) * (dp - delta[h : h + 1, :] * scales[half])).astype(BF16)
            dk = dk + mm(ds, qm[here, :])
            dv = dv + mm(low, jnp.where((lane >> 6) == half, ea, 0.0).astype(BF16))
            part = mm(kT[hr, :], ds)
            dq_o[hr, :] = part if first else dq_i[hr, :] + part
        d_o[:, cols] = (dk * SCORE_SCALE).astype(d_o.dtype)
        d_o[:, vcols] = dv.astype(d_o.dtype)


def gateback_kernel(
    sc, emix, ha, hb, mg, rs, dm, slope, a3, x1, gated, ecg, ob, eatt, taps, inner, up, gains,
    bcg_o, gi_o, buf, wide, plane,
):
    rows = emix.shape[0]
    fill_wide(sc, wide, (emix,), ha, hb)
    conv(sc, wide, taps, plane, rows, -1, False)
    gi = jnp.zeros((1, 512), F32)
    ups = []
    for t in tiles(rows):
        up_n = plane[t, :]
        dgate = unit_back(up_n, mg[t, :], rs[t, :], inner[...])
        gi = gi + jnp.sum(up_n * mg[t, :], 0, keepdims=True)
        sl = slope[t, :].astype(F32)
        eup = jnp.concatenate([dm[t, :] * sl[:, 0:512], dgate * sl[:, 512:1024]], 1).astype(BF16)
        ups.append(eup)
        m, rs1 = unit(x1[t, :])
        bcg_o[t, :] = unit_back(mm_nt(eup, up[...]), m, rs1, gains[2:3, :])
    gi_o[...] = jnp.broadcast_to(gi, (8, 512))
    eup = jnp.concatenate(ups, 0)
    put_cols(buf, 0, mm_tn(a3[...], eup))
    put_cols(buf, 2048, mm_tn(gated[...], ecg[...]))
    put_cols(buf, 3072, mm_tn(ob[...], eatt[...]))


def last_kernel(
    sc, dqT, dkv0, dkv1, dkv2, a2, x1, g2, bcg, a1, h, d, freq, wq, gains, w2, g1_o, du_o, buf,
):
    rows = x1.shape[0]
    cos, sin = turn_tables(sc, freq[...], rows)
    dq = dqT[...].T * SCORE_SCALE
    eqkvs, e1s = [], []
    for t in tiles(rows):
        dkv = dkv0[t, :] + dkv1[t, :].astype(F32) + dkv2[t, :].astype(F32)
        eq = rotate(dq[t], cos[t], sin[t], -1.0).astype(BF16)
        ek = rotate(dkv[:, 0:256], cos[t], sin[t], -1.0).astype(BF16)
        eqkv = jnp.concatenate([eq, ek, dkv[:, 256:512].astype(BF16)], 1)
        eqkvs.append(eqkv)
        m, rs = unit(x1[t, :])
        g1 = g2[t, :] + unit_back(mm_nt(eqkv, wq[...]), m, rs, gains[1:2, :]) + bcg[t, :]
        g1_o[t, :] = g1
        e1 = (0.5 * g1).astype(BF16)
        e1s.append(e1)
        du_o[t, :] = (mm_nt(e1, w2[...]) * d[t, :].astype(F32)).astype(BF16)
    put_cols(buf, 0, mm_tn(a1[...], du_o[...]))
    put_cols(buf, 2048, mm_tn(h[...], jnp.concatenate(e1s, 0)))
    put_cols(buf, 4096, mm_tn(a2[...], jnp.concatenate(eqkvs, 0)))


def input_kernel(sc, du, g1, gains, feat, w1, dx_o):
    rows = du.shape[0]
    for t in tiles(rows):
        keep = keep_mask(sc, t.start, (t.stop - t.start, 256))
        m, rs = unit(jnp.where(keep, feat[t, :].astype(F32), 0.0))
        back = unit_back(mm_nt(du[t, :], w1[...]), m, rs, gains[0:1, :])
        dx_o[t, :] = jnp.where(keep, g1[t, :] + back, 0.0)


def join_kernel(left, right, out):
    rows = right.shape[0]
    out[0:rows, :] = (left[0:rows, :].astype(F32) + right[...].astype(F32)).astype(BF16)
    if out.shape[0] > rows:
        out[rows:, :] = jnp.zeros((out.shape[0] - rows, out.shape[1]), BF16)


def rank():
    return lax.axis_index("grp") * lax.axis_size("blk") + lax.axis_index("blk")


def overlaps(sizes, low, high):
    start = 0
    for i, n in enumerate(sizes):
        a, b = max(start, low), min(start + n, high)
        if a < b:
            yield i, a - start, a - low, b - a
        start += n


def pack_kernel(sources, *refs):
    parts, keep, sends = refs[:sources], refs[sources], refs[sources + 1 :]
    half = keep.shape[0]
    bit = rank() % 2
    sizes = [ref.shape[0] for ref in parts]
    for own in range(2):

        @pl.when(bit == own)
        def _():
            for i, at, to, n in overlaps(sizes, own * half, (own + 1) * half):
                keep[to : to + n, :] = parts[i][at : at + n, :]
            start = (1 - own) * half
            for send in sends:
                for i, at, to, n in overlaps(sizes, start, start + send.shape[0]):
                    send[to : to + n, :] = parts[i][at : at + n, :]
                start += send.shape[0]


def fold_pieces_kernel(pair, mine, *refs):
    gots, keep, send = refs[:-2], refs[-2], refs[-1]
    half = keep.shape[0]
    bit = slot_bit(pair)
    sizes = [ref.shape[0] for ref in gots]
    for own in range(2):

        @pl.when(bit == own)
        def _():
            for ref, b in ((send, 1 - own), (keep, own)):
                for i, at, to, n in overlaps(sizes, b * half, (b + 1) * half):
                    value = mine[b * half + to : b * half + to + n, :].astype(F32) + gots[i][at : at + n, :].astype(F32)
                    ref[to : to + n, :] = value.astype(BF16)


def pieces_of(rows, count):
    step = -(-rows // (16 * count)) * 16
    return [min(step, rows - i * step) for i in range(count)]


def slot_bit(pair):
    index = rank()
    mask = jnp.where(index % 2 == 0, pair[0], pair[1])
    return (index // mask) % 2


def fold_kernel(pair, alone, *refs):
    if pair is None:
        mine, got, out = refs
        out[...] = (mine[...].astype(F32) + got[...].astype(F32)).astype(BF16)
        return
    *ins, keep, send = refs
    bit = slot_bit(pair)
    at = 0
    sources = list(zip(ins[0 : len(ins) - alone : 2], ins[1 : len(ins) - alone : 2]))
    for pieces in sources + [(ref,) for ref in ins[len(ins) - alone :]]:
        half = pieces[0].shape[0] // 2
        for ref, b in ((send, 1 - bit), (keep, bit)):
            here = pl.ds(pl.multiple_of(b * half, 16), half)
            value = pieces[0][here, :]
            if len(pieces) > 1:
                value = (value.astype(F32) + pieces[1][here, :].astype(F32)).astype(BF16)
            ref[at : at + half, :] = value
        at += half


def grow_into(bit, segments, mine, got, out):
    at = to = 0
    for n in segments:
        piece = slice(at, at + n)
        out[pl.ds(pl.multiple_of(to + bit * n, 16), n), :] = mine[piece, :]
        out[pl.ds(pl.multiple_of(to + (1 - bit) * n, 16), n), :] = got[piece, :]
        at += n
        to += 2 * n
    if at < mine.shape[0]:
        value = mine[at:, :].astype(F32) + got[at:, :].astype(F32)
        out[to : to + mine.shape[0] - at, :] = value.astype(BF16)


def grow_kernel(pair, segments, mine, got, out):
    grow_into(slot_bit(pair), segments, mine, got, out)


def half_pieces(layout, sizes, j):
    bounds = []
    base = at = 0
    for n in sizes:
        bounds.append((base + j * n // 2, base + (j + 1) * n // 2, at))
        base += n
        at += n // 2
    for i, (row, n, cols) in enumerate(layout):
        if row is None or row >= base:
            continue
        for c in range(cols // LANES):
            for low, high, at in bounds:
                a, b = max(low, row + c * n), min(high, row + (c + 1) * n)
                if a < b:
                    yield i, at + a - low, a - row - c * n, b - a, c


def write_half(layout, sizes, j, src, outs, bufs, sems):
    pieces = list(half_pieces(layout, sizes, j))
    copies = []
    for i in range(len(layout)):
        mine = [p for p in pieces if p[0] == i]
        for _, at, to, n, c in mine:
            bufs[i][to : to + n, c * LANES : (c + 1) * LANES] = src[at : at + n, :].astype(F32)
        if len(mine) * LANES == layout[i][2] and all(p[3] == layout[i][1] for p in mine):
            copies.append(pltpu.make_async_copy(bufs[i], outs[i], sems.at[len(copies)]))
            copies[-1].start()
        else:
            for _, at, to, n, c in mine:
                here = (slice(to, to + n), slice(c * LANES, (c + 1) * LANES))
                copies.append(pltpu.make_async_copy(bufs[i].at[here], outs[i].at[here], sems.at[len(copies)]))
                copies[-1].start()
    return copies


GAIN_OF = ((0, 2), (1, 4), (2, 6), (3, 11))


def write_gains(layout, sizes, j, bufs, weights, gains, lines):
    whole = {p[0] for p in half_pieces(layout, sizes, j)}
    for (g, i), weight in zip(GAIN_OF, weights):
        if i not in whole:
            continue
        total = jnp.zeros((256, LANES), F32)
        for c in range(weight.shape[1] // LANES):
            cols = slice(c * LANES, (c + 1) * LANES)
            total = total + bufs[i][:, cols] * weight[:, cols].astype(F32)
        line = lax.dot_general(
            jnp.ones((8, LANES), F32), total, (((1,), (1,)), ((), ())),
            precision=lax.Precision.HIGHEST, preferred_element_type=F32,
        )
        lines[g : g + 1, :] = line[0:1, :] / gains[g : g + 1, :]


def unpack_mine_kernel(layout, sizes, mine, gains, w_a, w_b, w_c, w_d, *refs):
    count = len(layout)
    outs, lines, bufs, sems = refs[:count], refs[count], refs[count + 1 : 2 * count + 1], refs[2 * count + 1]
    bit = rank() % 2
    lines[...] = jnp.zeros((8, 256), F32)
    for j in range(2):

        @pl.when(bit == j)
        def _():
            copies = write_half(layout, sizes, j, mine, outs, bufs, sems)
            write_gains(layout, sizes, j, bufs, (w_a, w_b, w_c, w_d), gains, lines)
            for copy in copies:
                copy.wait()


def unpack_got_kernel(layout, sizes, mine, got, lines, gains, w_a, w_b, w_c, w_d, *refs):
    count = len(layout)
    outs, bufs = refs[count : 2 * count], refs[2 * count : 3 * count]
    small, sems = refs[3 * count :]
    base = sum(sizes) // 2
    small[...] = mine[base:, :].astype(F32) + got[base:, :].astype(F32)
    late = []

    def send(i):
        late.append(pltpu.make_async_copy(bufs[i], outs[i], sems.at[sems.shape[0] - 1 - len(late)]))
        late[-1].start()

    for i, (row, n, cols) in enumerate(layout):
        if row is not None and row >= 2 * base:
            for c in range(cols // LANES):
                at = row - 2 * base + c * n
                bufs[i][:, c * LANES : (c + 1) * LANES] = small[at : at + n, :]
            send(i)
    bit = rank() % 2
    bufs[0][0:4, :] = lines[0:4, :]
    for c in range(2):
        at = 8 * TAPS + c
        bufs[0][4:5, c * LANES : (c + 1) * LANES] = small[at : at + 1, :]
    for j in range(2):

        @pl.when(bit != j)
        def _():
            copies = write_half(layout, sizes, j, got, outs, bufs, sems)
            write_gains(layout, sizes, j, bufs, (w_a, w_b, w_c, w_d), gains, bufs[0])
            for copy in copies:
                copy.wait()

    send(0)
    for copy in late:
        copy.wait()


def small_call(kernel, outs, ins, us, scratch=(), limit=None, out_space=None):
    vmem = pl.BlockSpec(memory_space=pltpu.VMEM)
    return pl.pallas_call(
        kernel,
        out_shape=[jax.ShapeDtypeStruct(s, d) for s, d in outs],
        in_specs=[vmem] * len(ins),
        out_specs=[vmem if out_space is None else pl.BlockSpec(memory_space=out_space)] * len(outs),
        scratch_shapes=list(scratch),
        compiler_params=pltpu.CompilerParams(vmem_limit_bytes=limit or VMEM_BYTES),
        cost_estimate=pl.CostEstimate(flops=int(us * UNIT), bytes_accessed=1, transcendentals=0),
    )(*ins)


def exchange(value, pair):
    count = lax.axis_size("grp") * lax.axis_size("blk")
    return lax.ppermute(value, AXES, [(i, i ^ pair[i % 2]) for i in range(count)])


def slot_pairs():
    count = lax.axis_size("grp") * lax.axis_size("blk")
    masks = [1 << i for i in range(1, count.bit_length() - 1)]
    first = list(masks)
    second = list(masks)
    if len(masks) > 2:
        second[0], second[1], second[2] = masks[2], masks[0], masks[1]
    return list(zip(first, second))


def fold(pair, *ins, alone=0):
    paired = ins[: len(ins) - alone]
    rows = sum(v.shape[0] for v in paired[0::2]) // 2 + sum(v.shape[0] for v in ins[len(paired) :]) // 2
    outs = [((rows, LANES), BF16)] * 2
    return small_call(functools.partial(fold_kernel, pair, alone), outs, ins, 0.5)


def reduce_tail(early, late, small, sizes, layout, weights, beside):
    slots = slot_pairs()
    keep, send = fold(slots[1], *early, *late, small, alone=1)
    got = exchange(send, slots[1])
    send, *ins = lax.optimization_barrier((send, *beside[1]))
    extra = beside[0](ins)
    got, extra = lax.optimization_barrier((got, extra))
    for pair in slots[2:]:
        keep, send = fold(pair, keep, got)
        got = exchange(send, pair)
    (mine,) = small_call(functools.partial(fold_kernel, None, 0), [(keep.shape, BF16)], [keep, got], 0.3)
    rest = small.shape[0]
    for i in reversed(range(len(slots))):
        got = exchange(mine, slots[i])
        if i > 1:
            segments, rows = (mine.shape[0],), 2 * mine.shape[0]
        elif i == 1:
            segments, rows = tuple(n // 8 for n in sizes) + (rest // 2,), 2 * mine.shape[0]
        else:
            segments, rows = tuple(n // 4 for n in sizes), sum(sizes) // 2 + rest
        (mine,) = small_call(functools.partial(grow_kernel, slots[i], segments), [((rows, LANES), BF16)], [mine, got], 0.4)
    got = exchange(mine, (1, 1))
    shapes = [(n, cols) for _, n, cols in layout]
    hbm, vmem = pl.BlockSpec(memory_space=pltpu.HBM), pl.BlockSpec(memory_space=pltpu.VMEM)
    outs = [jax.ShapeDtypeStruct(s, F32) for s in shapes]
    bufs = [pltpu.VMEM(s, F32) for s in shapes]
    params = pltpu.CompilerParams(vmem_limit_bytes=32 * 1024 * 1024)
    *outs, lines = pl.pallas_call(
        functools.partial(unpack_mine_kernel, layout, sizes),
        out_shape=outs + [jax.ShapeDtypeStruct((8, 256), F32)],
        in_specs=[vmem] * 6,
        out_specs=[hbm] * len(shapes) + [vmem],
        scratch_shapes=bufs + [pltpu.SemaphoreType.DMA((24,))],
        compiler_params=params,
        cost_estimate=pl.CostEstimate(flops=int(3.0 * UNIT), bytes_accessed=1, transcendentals=0),
        name="unpack_mine",
    )(mine, *weights)
    sums = pl.pallas_call(
        functools.partial(unpack_got_kernel, layout, sizes),
        out_shape=[jax.ShapeDtypeStruct(s, F32) for s in shapes],
        in_specs=[vmem] * 8 + [hbm] * len(shapes),
        out_specs=[hbm] * len(shapes),
        scratch_shapes=bufs + [pltpu.VMEM((rest, LANES), F32), pltpu.SemaphoreType.DMA((24,))],
        input_output_aliases={8 + i: i for i in range(len(shapes))},
        compiler_params=params,
        cost_estimate=pl.CostEstimate(flops=int(3.0 * UNIT), bytes_accessed=1, transcendentals=0),
        name="unpack_got",
    )(mine, got, lines, *weights, *outs)
    return sums, extra


def plain(kernel, ins, outs, kept, *refs):
    head = refs[: ins]
    made = refs[ins + kept : ins + kept + outs]
    scratch = refs[ins + 2 * kept + outs :]
    kernel(*head, *made, *scratch)


class Layer:
    def __init__(self, plan):
        self.plan = plan
        self.step = 0
        self.have = {}

    def __getitem__(self, key):
        return self.have[key]

    def __setitem__(self, key, value):
        self.have[key] = value

    def run(self, kernel, outs, extra=(), scratch=(), us=1.0):
        name, reads = self.plan[self.step]
        later = [r for _, more in self.plan[self.step + 1 :] for r in more]
        kept = sorted(k for k in self.have if k in later and k not in reads and k != "sc")
        self.step += 1

        def size(key):
            return self.have[key].size * self.have[key].dtype.itemsize

        while sum(map(size, kept)) > CARRY_BYTES:
            kept.remove(max(kept, key=size))
        smem = pl.BlockSpec(memory_space=pltpu.SMEM)
        vmem = pl.BlockSpec(memory_space=pltpu.VMEM)
        ins = [self.have[r] for r in reads] + list(extra)
        in_specs = [smem if r == "sc" else vmem for r in reads] + [vmem] * len(extra)
        shapes = [jax.ShapeDtypeStruct(s, d) for _, s, d in outs]
        shapes += [jax.ShapeDtypeStruct(self.have[k].shape, self.have[k].dtype) for k in kept]
        made = pl.pallas_call(
            functools.partial(plain, kernel, len(ins), len(outs), len(kept)),
            out_shape=shapes,
            in_specs=in_specs + [vmem] * len(kept),
            out_specs=[vmem] * len(shapes),
            scratch_shapes=list(scratch),
            input_output_aliases={len(ins) + i: len(outs) + i for i in range(len(kept))},
            compiler_params=pltpu.CompilerParams(vmem_limit_bytes=VMEM_BYTES),
            cost_estimate=pl.CostEstimate(flops=int(us * UNIT), bytes_accessed=1, transcendentals=0),
            name=name,
        )(*ins, *[self.have[k] for k in kept])
        for key, value in zip([o[0] for o in outs] + kept, made):
            self.have[key] = value


def swap(value, axis, mask):
    count = math.prod(lax.axis_size(a) for a in axis) if isinstance(axis, tuple) else lax.axis_size(axis)
    return lax.ppermute(value, axis, [(i, i ^ mask) for i in range(count)])


def halo(ea, eb):
    count = lax.axis_size("blk")
    near = [(i, i ^ 1) for i in range(count)]
    far = []
    for i in range(1, count - 1, 2):
        far += [(i, i + 1), (i + 1, i)]
    return lax.ppermute(ea, "blk", near), lax.ppermute(eb, "blk", far)


def local(
    features, d_out, bucket_batch, valid_len, time_start, time_width, freq_start, freq_width,
    gains, inner_gain, ffn1_in, ffn1_out, qkv_w, out_w, cg_up, cg_conv, cg_down, merge_conv,
    merge_w, ffn2_in, ffn2_out,
):
    rows, width = features.shape
    half = cg_down.shape[0]
    ff = ffn1_in.shape[1]
    blocks = lax.axis_size("blk")
    me = lax.axis_index("blk")
    freq = np.exp(np.arange(32, dtype=np.float64) * (-2.0 * math.log(10000.0) / HEAD_DIM))
    freq = jnp.asarray(np.tile(freq, 4)[None, :].astype(np.float32))
    wide = pltpu.VMEM((half // LANES, rows + 2 * HALO, LANES), F32)
    plane = pltpu.VMEM((rows, half), F32)
    rim = pltpu.VMEM((half // LANES, 6 * HALO, LANES), F32)
    pairs = [(m, m | 1) for m in range(0, blocks, 2)]
    kvs = [(f"kv{a}", f"kv{b}") for a, b in pairs]
    even = [a for a, _ in pairs[1:]]
    state = ["c", "l", "acc"]
    plan = [("gate", ["sc", "x1"])]
    plan += [("att_first", ["sc", "q", *kvs[0]])]
    plan += [("conv_gate", ["sc", "n"]), ("mixed", ["sc", "plane1", "na", "nb", "rest"])]
    far_masks = [m for a, b in pairs[1:] for m in (a, b)]
    plan += [("att_mid", ["sc", "q", f"kv{m}", *state]) for m in far_masks[:-1]]
    plan += [
        ("att_last", ["sc", "q", f"kv{far_masks[-1]}", *state, "catg"]),
        ("conv_merge", ["sc", "att", "catg"]),
        ("merge", ["sc", "plane2", "att", "catg", "ha", "hb", "x1"]),
        ("grads2", ["a4", "h2", "e2", "du2", "un", "em"]),
        ("conv_back", ["sc", "df", "ec"]),
        ("split", ["sc", "plane3", "ec", "ca", "cb", "na", "nb", "rest", "mixed", "oT", "l"]),
    ]
    back = ["qm", "c", "eaT", "delta"]

    def back_reads(m):
        return [f"kv{m}", f"w{m}", f"top{m}", *back] + ([] if m == even[0] + 1 else ["dqT"])

    for e in even:
        for m in (e + 1, e):
            plan += [("attback", back_reads(m))]
        plan += [("join_kv", [f"pd{e}", f"in{e}"])]
    plan += [
        ("attback", back_reads(1)),
        ("gateback", ["sc", "emix", "mb", "ma", "mg", "rs", "dm", "slope", "a3", "x1", "gated", "ecg", "ob", "eatt"]),
        ("pack_early", ["part1", "buf2"]),
        ("attback", back_reads(0)),
        ("fold_early", ["keep", "got0", "got1", "got2"]),
    ]
    total = f"far{even[0]}"
    for e in even[1:]:
        plan += [("join_far", [total, f"far{e}"])]
        total = f"t{e}"
    plan += [
        ("last", ["sc", "dqT", "own", "near", total, "a2", "x1", "g2", "bcg", "a1", "h1", "d1"]),
        ("pack_late", ["buf3"]),
        ("taps", ["sc", "ec", "ca", "cb", "att", "catg", "emix", "mb", "ma", "n", "g4", "gi"]),
    ]
    run = Layer(plan)
    smem = pl.BlockSpec(memory_space=pltpu.SMEM)
    vmem = pl.BlockSpec(memory_space=pltpu.VMEM)
    raw = (bucket_batch, valid_len, time_start, time_width, freq_start, freq_width, gains, freq,
           features, ffn1_in, ffn1_out, qkv_w)
    def narrow(name, kind=BF16):
        return (name, (rows, width), kind)

    def middle(name, kind=BF16):
        return (name, (rows, half), kind)

    def broad(name, kind=BF16):
        return (name, (rows, ff), kind)

    outs = [narrow("x1", F32), narrow("a1"), broad("h1"), broad("d1"), narrow("a2"), narrow("q"), middle("kv0"), middle("kvs")]
    made = pl.pallas_call(
        pre_kernel,
        out_shape=[jax.ShapeDtypeStruct((16,), jnp.int32)] + [jax.ShapeDtypeStruct(o[1], o[2]) for o in outs],
        in_specs=[pl.BlockSpec(memory_space=pltpu.HBM)] * 12,
        out_specs=[smem] + [vmem] * 8,
        scratch_shapes=[pltpu.SMEM(v.shape, v.dtype) for v in raw[:6]]
        + [pltpu.VMEM(v.shape, v.dtype) for v in raw[6:]] + [pltpu.SemaphoreType.DMA((12,))],
        compiler_params=pltpu.CompilerParams(vmem_limit_bytes=VMEM_BYTES),
        cost_estimate=pl.CostEstimate(flops=int(4.0 * UNIT), bytes_accessed=1, transcendentals=0),
        name="pre",
    )(raw[0], *[pltpu.with_memory_space_constraint(v, pltpu.HBM) for v in raw[1:]])
    for key, value in zip(["sc"] + [o[0] for o in outs], made):
        run[key] = value
    held = {0: run["kvs"]}
    bit = blocks // 2
    while bit > 1:
        held.update({m | bit: swap(held[m], "blk", bit) for m in list(held)})
        bit //= 2
    held[1] = swap(held[0], "blk", 1)

    def send_edges():
        return halo(run["ea"], run["eb"])

    edge = [("ea", (HALO, half), BF16), ("eb", (HALO, half), BF16)]
    edge2 = [("ea", (2 * HALO, half), BF16), ("eb", (2 * HALO, half), BF16)]
    stats = [("c", (8, rows), F32), ("l", (8, rows), F32)]

    def kept(*masks):
        return [o for m in masks for o in ((f"w{m}", (HEADS * rows, rows), BF16), (f"top{m}", (8, rows), F32))]


    run.run(
        gate_kernel,
        [narrow("a3"), middle("rest", F32), broad("slope"), middle("n"), middle("mg", F32), ("rs", (rows, 1), F32)] + edge2,
        [gains, inner_gain[None, :], cg_up], us=2.5,
    )
    edges = send_edges()
    run["kv1"] = held[1]
    run.run(functools.partial(att_kernel, True, False, pairs[0]), stats + [("qm", (HEADS * rows, LANES), BF16)] + kept(*pairs[0]) + [("acc", (width, rows), F32)], us=0.5)
    run.run(functools.partial(local_conv_kernel, 1, False), [middle("plane1", F32)], [cg_conv], [wide], us=0.3)
    run["na"], run["nb"] = edges
    run.run(
        mixed_kernel, [middle("mixed", F32), middle("gated"), narrow("catg")],
        [cg_conv, cg_down], [rim], us=1.5,
    )
    for a, b in pairs[1:]:
        late, _ = lax.optimization_barrier((held[a], run["catg"]))
        run[f"kv{a}"] = late
        mate = swap(late, "blk", 1)
        run.run(
            functools.partial(att_kernel, False, False, (a,)), stats + kept(a) + [("acc", (width, rows), F32)], us=2.8,
        )
        run[f"kv{b}"] = mate
        if b < blocks - 1:
            run.run(
                functools.partial(att_kernel, False, False, (b,)), stats + kept(b) + [("acc", (width, rows), F32)], us=2.8,
            )
    run.run(
        functools.partial(att_kernel, False, True, (blocks - 1,)),
        stats + kept(blocks - 1) + [("oT", (width, rows), F32), narrow("ob"), narrow("att")] + edge,
        [out_w], [pltpu.VMEM((width, rows), F32)], us=3.0,
    )
    edges = send_edges()
    run.run(functools.partial(local_conv_kernel, 1, False), [middle("plane2", F32)], [merge_conv], [wide], us=0.3)
    run["ha"], run["hb"] = edges
    run.run(
        merge_kernel,
        [narrow("out"), middle("un"), narrow("em"), middle("ec"), middle("df", F32), narrow("g2", F32), narrow("a4"),
         broad("h2"), narrow("e2"), broad("du2"), ("g4", (8, width), F32)] + edge2,
        [merge_conv, merge_w, d_out, gains, ffn2_in, ffn2_out], [rim, plane], us=5.5,
    )
    edges = send_edges()
    run.run(grads_kernel, [("part1", (5120, LANES), BF16)], us=0.3)
    run.run(functools.partial(local_conv_kernel, -1, True), [middle("plane3", F32)], [merge_conv], [wide], us=0.3)
    run["ca"], run["cb"] = edges
    run.run(
        split_kernel,
        [narrow("eatt"), narrow("ecg"), middle("emix"), middle("dm", F32), ("eaT", (width, rows), BF16),
         ("delta", (8, rows), F32), ("mb", (HALO, half), BF16), ("ma", (HALO, half), BF16)],
        [merge_conv, cg_down, out_w], [rim, plane], us=2.0,
    )

    tall = ("dqT", (width, rows), F32)
    pair_sum = (rows, 2 * width)
    for e in even:
        for m in (e + 1, e):
            run.run(
                functools.partial(attback_kernel, m == even[0] + 1), [tall, (f"pd{m}", pair_sum, BF16)], us=0.5
            )
            if m & 1:
                arrival = swap(run[f"pd{m}"], "blk", 1)
        run[f"in{e}"] = arrival
        run.run(join_kernel, [(f"s{e}", (rows + 32, 2 * width), BF16)], us=0.2)
    fars = {e: swap(run[f"s{e}"], "blk", e) for e in even}
    run.run(functools.partial(attback_kernel, False), [tall, ("pd1", pair_sum, BF16)], us=0.05)
    near = swap(run["pd1"], "blk", 1)
    run.run(
        gateback_kernel,
        [narrow("bcg", F32), ("gi", (8, half), F32), ("buf2", (3584, LANES), BF16)],
        [cg_conv, inner_gain[None, :], cg_up, gains], [wide, plane], us=0.5,
    )
    count = lax.axis_size("grp") * blocks
    used, late, rest = 8704, 5632, 256
    grain = 16 * count // 8
    sizes = (used + 8 * (-((used + late) // 8 + rest // 2) % grain), late)
    slots = slot_pairs()
    cuts = pieces_of(sizes[0] // 2, 3)
    run.run(
        functools.partial(pack_kernel, 2),
        [("keep", (sizes[0] // 2, LANES), BF16)] + [(f"send{i}", (n, LANES), BF16) for i, n in enumerate(cuts)], us=0.1,
    )
    gots = [exchange(run[f"send{i}"], (1, 1)) for i in range(3)]
    run.run(functools.partial(attback_kernel, False), [tall, ("own", pair_sum, F32)], us=0.5)
    for i in range(3):
        run[f"got{i}"] = gots[i]
    for e in even:
        run[f"far{e}"] = fars[e]
    run["near"] = near
    run.run(
        functools.partial(fold_pieces_kernel, slots[0]),
        [("early", (sizes[0] // 4, LANES), BF16), ("send_early", (sizes[0] // 4, LANES), BF16)], us=0.2,
    )
    early_got = exchange(run["send_early"], slots[0])
    for e in even[1:]:
        run.run(join_kernel, [(f"t{e}", (rows + 32, 2 * width), BF16)], us=0.2)
    run.run(
        last_kernel,
        [narrow("g1", F32), broad("du1"), ("buf3", (5632, LANES), BF16)],
        [freq, qkv_w, gains, ffn1_out], us=0.3,
    )
    quarter = ((sizes[1] // 4, LANES), BF16)
    cuts = pieces_of(sizes[1] // 2, 2)
    run.run(
        functools.partial(pack_kernel, 1),
        [("keep3", (sizes[1] // 2, LANES), BF16)] + [(f"late{i}", (n, LANES), BF16) for i, n in enumerate(cuts)], us=0.1,
    )
    gots = [exchange(run[f"late{i}"], (1, 1)) for i in range(2)]
    gots[0], early_got = lax.optimization_barrier((gots[0], early_got))
    keep3, send3 = small_call(functools.partial(fold_pieces_kernel, slots[0]), [quarter, quarter], [run["keep3"], *gots], 0.3)
    late_got = exchange(send3, slots[0])
    _, run["g4"] = lax.optimization_barrier((send3, run["g4"]))
    run.run(taps_kernel, [("small", (rest, LANES), BF16)], (), [wide, pltpu.VMEM((rest, LANES), F32)], us=2.0)
    base = sizes[0]
    tail = base + late
    layout = (
        (None, 5, 256), (tail + 8 * TAPS + 2, 1, 512),
        (base, 256, 1024), (base + 2048, 1024, 256), (base + 4096, 256, 768), (8192, 256, 256),
        (5120, 256, 1024), (tail + 4 * TAPS, TAPS, 512), (7168, 512, 256), (tail, TAPS, 512), (4096, 512, 256),
        (0, 256, 1024), (2048, 1024, 256),
    )

    def input_grad(ins):
        sc, du1, g1 = ins
        smem = pl.BlockSpec(memory_space=pltpu.SMEM)
        vmem = pl.BlockSpec(memory_space=pltpu.VMEM)
        return pl.pallas_call(
            input_kernel,
            out_shape=jax.ShapeDtypeStruct((rows, width), F32),
            in_specs=[smem] + [vmem] * 5,
            out_specs=vmem,
            compiler_params=pltpu.CompilerParams(vmem_limit_bytes=VMEM_BYTES),
            cost_estimate=pl.CostEstimate(flops=int(0.5 * UNIT), bytes_accessed=1, transcendentals=0),
            name="input_grad",
        )(sc, du1, g1, gains, features, ffn1_in)

    sums, dx = reduce_tail(
        (run["early"], early_got), (keep3, late_got), run["small"], sizes, layout,
        (gains, ffn1_in, qkv_w, cg_up, ffn2_in), (input_grad, (run["sc"], run["du1"], run["g1"])),
    )
    return (run["out"], dx, sums[0], sums[1][0], *sums[2:])


def solution(mesh):
    rows = P(("grp", "blk"), None)
    in_specs = (rows, rows, P("grp")) + (P("grp", None),) * 5 + (P(),) * 13
    out_specs = (rows, rows) + (P(),) * 13
    return jax.shard_map(local, mesh=mesh, in_specs=in_specs, out_specs=out_specs, check_vma=False)
```

```python
import functools
import math

import jax
import jax.numpy as jnp
import numpy as np
from jax import lax
from jax.experimental import pallas as pl
from jax.experimental.pallas import tpu as pltpu
from jax.sharding import PartitionSpec as P

HEADS = 4
HEAD_DIM = 64
HALO = 32
LOG_BASE = 1.4426950408889634
EPSILON = 1e-05
SCORE_SCALE = HEAD_DIM ** (-0.5)
EXP_SCALE = SCORE_SCALE * LOG_BASE
HIDE = -(2.0 ** 100)
AXES = ("grp", "blk")
F32 = jnp.float32
BF16 = jnp.bfloat16
LANES = 128
VMEM_BYTES = 16 * 1024 * 1024
UNIT = 0.35e9
CARRY_BYTES = 30 * 1024 * 1024


def mm(left, right):
    return jnp.dot(left, right, preferred_element_type=F32)


def mm_nt(left, right):
    return lax.dot_general(left, right, (((1,), (1,)), ((), ())), preferred_element_type=F32)


def mm_tn(left, right):
    return lax.dot_general(left, right, (((0,), (0,)), ((), ())), preferred_element_type=F32)


def unit(v):
    center = v - jnp.mean(v, -1, keepdims=True)
    rs = lax.rsqrt(jnp.mean(center * center, -1, keepdims=True) + EPSILON)
    return center * rs, rs


def unit_back(up, m, rs, gain):
    eg = up * gain
    return rs * (eg - jnp.mean(eg, -1, keepdims=True) - m * jnp.mean(eg * m, -1, keepdims=True))


def silu_parts(u):
    sig = 0.5 + 0.5 * jnp.tanh(0.5 * u)
    h = u * sig
    return h, sig + h * (1.0 - sig)


def gelu_parts(t):
    root = math.sqrt(2.0 / math.pi)
    t2 = t * t
    th = jnp.tanh(root * t * (1.0 + 0.044715 * t2))
    half = 0.5 + 0.5 * th
    slope = half + 0.5 * root * t * (1.0 - th * th) * (1.0 + 3.0 * 0.044715 * t2)
    return t * half, slope


def rows_of(sc, r0, shape):
    row = lax.broadcasted_iota(jnp.int32, shape, 0) + r0
    shift = sc[0] - 1
    utt = row & shift
    pos = (row >> shift) + sc[1] * (512 >> shift)
    return utt, pos


def keep_mask(sc, r0, shape):
    utt, pos = rows_of(sc, r0, shape)
    ch = lax.broadcasted_iota(jnp.int32, shape, 1)
    first = utt == 0

    def pick(i):
        return jnp.where(first, sc[i], sc[i + 1])

    ok = (pos < pick(2)) & jnp.logical_not((pos >= pick(4)) & (pos < pick(6)))
    ok = ok & jnp.logical_not((ch >= pick(8)) & (ch < pick(10)))
    return ok


def turn_tables(sc, freq, rows):
    shift = sc[0] - 1
    coarse = lax.broadcasted_iota(jnp.int32, (rows // 16, LANES), 0) * 16
    fine = lax.broadcasted_iota(jnp.int32, (16, LANES), 0)
    a = ((coarse >> shift) + sc[1] * (rows >> shift)).astype(F32) * freq
    c = (fine >> shift).astype(F32) * freq
    ca, sa, cc, cs = jnp.cos(a), jnp.sin(a), jnp.cos(c), jnp.sin(c)
    cos = ca[:, None, :] * cc[None] - sa[:, None, :] * cs[None]
    sin = sa[:, None, :] * cc[None] + ca[:, None, :] * cs[None]
    return cos.reshape(rows, LANES), sin.reshape(rows, LANES)


def rotate(v, cos, sin, direction):
    lane = lax.broadcasted_iota(jnp.int32, (v.shape[0], LANES), 1)
    lower = (lane & 63) < 32
    signed = jnp.where(lower, -direction, direction) * sin
    parts = []
    for i in range(v.shape[1] // LANES):
        p = v[:, i * LANES : (i + 1) * LANES]
        other = jnp.where(lower, pltpu.roll(p, LANES - 32, 1), pltpu.roll(p, 32, 1))
        parts.append(p * cos + other * signed)
    return jnp.concatenate(parts, 1)


def edge_sends(sc, refs, a_ref, b_ref):
    odd = (sc[1] & 1) == 1
    col = 0
    count = a_ref.shape[0]
    for ref in refs if isinstance(refs, tuple) else (refs,):
        rows, width = ref.shape
        first = ref[0:count, :].astype(BF16)
        last = ref[rows - count : rows, :].astype(BF16)
        cols = slice(col, col + width)
        col += width

        @pl.when(odd)
        def _():
            a_ref[:, cols] = first
            b_ref[:, cols] = last

        @pl.when(jnp.logical_not(odd))
        def _():
            a_ref[:, cols] = last
            b_ref[:, cols] = first


def sides(sc, ha, hb, cols, before, after):
    odd = (sc[1] & 1) == 1
    first = jnp.where(odd, ha[before, cols].astype(F32), hb[before, cols].astype(F32))
    return first, jnp.where(odd, hb[after, cols].astype(F32), ha[after, cols].astype(F32))


LOWER, UPPER = slice(0, HALO), slice(HALO, 2 * HALO)


def fill_wide(sc, wide, sources, ha, hb, spots=None):
    at = 0
    for z in sources:
        rows, width = z.shape
        for c in range(width // LANES):
            cols = slice(at * LANES, (at + 1) * LANES)
            if spots is None:
                before, after = ha[:, cols].astype(F32), hb[:, cols].astype(F32)
            else:
                before, after = sides(sc, ha, hb, cols, *spots)
            wide[at, 0:HALO, :] = before
            wide[at, HALO : HALO + rows, :] = z[:, c * LANES : (c + 1) * LANES].astype(F32)
            wide[at, HALO + rows : 2 * HALO + rows, :] = after
            at += 1


CONV_ROWS = 256
TAP_ROWS = 128
TAPS = 31


def local_conv_kernel(direction, add, sc, *refs):
    *sources, taps, out, wide = refs
    if add:
        base, sources = sources[0], sources[1:]
        out[...] = base[...]
    rows = out.shape[0]
    at = 0
    for z in sources:
        for c in range(z.shape[1] // LANES):
            wide[at, 0:HALO, :] = jnp.zeros((HALO, LANES), F32)
            wide[at, HALO : HALO + rows, :] = z[:, c * LANES : (c + 1) * LANES].astype(F32)
            wide[at, HALO + rows : 2 * HALO + rows, :] = jnp.zeros((HALO, LANES), F32)
            at += 1
    conv(sc, wide, taps, out, rows, direction, add)


def add_edges(sc, rim, taps, ha, hb, spots, plane, out, direction):
    step = sc[0] * direction
    rows = plane.shape[0]
    for c in range(taps.shape[1] // LANES):
        cols = slice(c * LANES, (c + 1) * LANES)
        before, after = sides(sc, ha, hb, cols, *spots)
        rim[c, 0:HALO, :] = before
        rim[c, HALO : 5 * HALO, :] = jnp.zeros((4 * HALO, LANES), F32)
        rim[c, 5 * HALO : 6 * HALO, :] = after
    if out is not plane:
        out[HALO : rows - HALO, :] = plane[HALO : rows - HALO, :]
    for c in range(taps.shape[1] // LANES):
        cols = slice(c * LANES, (c + 1) * LANES)
        for base, start in ((0, 0), (3 * HALO, rows - HALO)):
            acc = plane[start : start + HALO, cols]
            for k in range(TAPS):
                tap = taps[k : k + 1, cols].astype(F32)
                acc = acc + rim[c, pl.ds(base + HALO + step * (k - TAPS // 2), HALO), :] * tap
            out[start : start + HALO, cols] = acc


def by_batch(sc, body):
    for batch in (1, 2):
        pl.when(sc[0] == batch)(functools.partial(body, batch))


def conv(sc, wide, taps, out, rows, direction, add):
    size = min(CONV_ROWS, rows)

    def run(batch):
        groups = {}
        for k in range(TAPS):
            at = HALO + direction * batch * (k - TAPS // 2)
            groups.setdefault(at % 8, []).append((at // 8 * 8, k))
        for c in range(taps.shape[1] // LANES):
            cols = slice(c * LANES, (c + 1) * LANES)
            ws = [taps[k : k + 1, cols].astype(F32) for k in range(TAPS)]

            def body(i, carry):
                r0 = pl.multiple_of(i * size, size)
                here = pl.ds(r0, size)
                window = wide[c, pl.ds(r0, size + 2 * HALO), :]
                acc = out[here, cols] if add else None
                for shift, members in sorted(groups.items()):
                    n = size + 8 if shift else size
                    part = None
                    for at, k in members:
                        term = window[at : at + n] * ws[k]
                        part = term if part is None else part + term
                    if shift:
                        part = pltpu.roll(part, n - shift, 0)[:size]
                    acc = part if acc is None else acc + part
                out[here, cols] = acc
                return carry

            lax.fori_loop(0, rows // size, body, 0)

    by_batch(sc, run)


def correlate(sc, wide, sources, out, row, rows):
    size = min(TAP_ROWS, rows)
    blocks = [(z, c) for z in sources for c in range(z.shape[1] // LANES)]

    def run(batch):
        for at, (z, c) in enumerate(blocks):
            cols = slice(c * LANES, (c + 1) * LANES)

            def body(i, sums):
                r0 = pl.multiple_of(i * size, size)
                zc = z[pl.ds(r0, size), cols].astype(F32)
                window = wide[at, pl.ds(r0, size + 2 * HALO), :]
                padded = jnp.concatenate([zc, jnp.zeros((8, LANES), F32)], 0)
                turned = {0: zc}
                new = []
                for k in range(TAPS):
                    start = HALO - batch * (k - TAPS // 2)
                    shift = start % 8
                    if shift not in turned:
                        turned[shift] = pltpu.roll(padded, shift, 0)
                    factor = turned[shift]
                    n = factor.shape[0]
                    prod = window[start - shift : start - shift + n] * factor
                    new.append(sums[k] + jnp.sum(prod.reshape(n // 8, 8, LANES), 0))
                return tuple(new)

            zero = tuple(jnp.zeros((8, LANES), F32) for _ in range(TAPS))
            sums = lax.fori_loop(0, rows // size, body, zero)
            for k in range(TAPS):
                to = row + at * TAPS + k
                out[to : to + 1, :] = jnp.sum(sums[k], 0, keepdims=True)

    by_batch(sc, run)


def merge_taps_kernel(sc, ec, ca, cb, att, catg, out, wide):
    fill_wide(sc, wide, (ec,), ca, cb, (UPPER, LOWER))
    correlate(sc, wide, (att, catg), out, 0, ec.shape[0])


def gate_taps_kernel(sc, emix, before, after, n, merge_taps, g4, gi, small_o, wide, total):
    fill_wide(sc, wide, (emix,), before, after)
    total[0 : 4 * TAPS, :] = merge_taps[0 : 4 * TAPS, :]
    correlate(sc, wide, (n,), total, 4 * TAPS, emix.shape[0])
    at = 8 * TAPS
    for ref in (g4, gi):
        for c in range(ref.shape[1] // LANES):
            total[at : at + 1, :] = ref[0:1, c * LANES : (c + 1) * LANES]
            at += 1
    total[at:, :] = jnp.zeros((total.shape[0] - at, LANES), F32)
    small_o[...] = total[...].astype(BF16)


def tiles(rows, size=256):
    size = min(size, rows)
    return [slice(i, i + size) for i in range(0, rows, size)]


def pre_kernel(*refs):
    hbm, refs = refs[:12], refs[12:]
    sc, x1_o, a1_o, h_o, d_o, a2_o, q_o, kv_o, kvs_o = refs[:9]
    bb, vl, ts, tw, fs, fw, gains, freq, feat, w1, w2, wq, sems = refs[9:]
    loads = [
        pltpu.make_async_copy(src, dst, sems.at[i])
        for i, (src, dst) in enumerate(zip(hbm, (bb, vl, ts, tw, fs, fw, gains, freq, feat, w1, w2, wq)))
    ]
    for load in loads:
        load.start()
    for load in loads[:8]:
        load.wait()
    sc[0] = bb[0]
    sc[1] = lax.axis_index("blk")
    for i in range(2):
        sc[2 + i] = vl[0, i]
        sc[4 + i] = ts[0, i]
        sc[6 + i] = ts[0, i] + tw[0, i]
        sc[8 + i] = fs[0, i]
        sc[10 + i] = fs[0, i] + fw[0, i]
    for i in range(12, 16):
        sc[i] = 0
    loads = loads[8:]
    rows = feat.shape[0]
    cos, sin = turn_tables(sc, freq[...], rows)
    parts = tiles(rows)
    for i, t in enumerate(parts):
        shape = (t.stop - t.start, 256)
        if i == 0:
            loads[0].wait()
        x = jnp.where(keep_mask(sc, t.start, shape), feat[t, :].astype(F32), 0.0)
        m, _ = unit(x)
        a1 = (m * gains[0:1, :]).astype(BF16)
        a1_o[t, :] = a1
        if i == 0:
            loads[1].wait()
        h, d = silu_parts(mm(a1, w1[...]))
        h = h.astype(BF16)
        h_o[t, :] = h
        d_o[t, :] = d.astype(BF16)
        if i == 0:
            loads[2].wait()
        x1 = x + 0.5 * mm(h, w2[...])
        x1_o[t, :] = x1
        m, _ = unit(x1)
        a2 = (m * gains[1:2, :]).astype(BF16)
        a2_o[t, :] = a2
        if i == 0:
            loads[3].wait()
        qkv = mm(a2, wq[...])
        q_o[t, :] = rotate(qkv[:, 0:256], cos[t], sin[t], 1.0).astype(BF16)
        k = rotate(qkv[:, 256:512], cos[t], sin[t], 1.0).astype(BF16)
        v = qkv[:, 512:768].astype(BF16)
        for o in (kv_o, kvs_o):
            o[t, 0:256] = k
            o[t, 256:512] = v


def gate_kernel(sc, x1, gains, inner, up, a3_o, rest_o, slope_o, n_o, mg_o, rs_o, ea_o, eb_o):
    rows = x1.shape[0]
    for t in tiles(rows):
        m, _ = unit(x1[t, :])
        a3 = (m * gains[2:3, :]).astype(BF16)
        a3_o[t, :] = a3
        y, slope = gelu_parts(mm(a3, up[...]))
        slope_o[t, :] = slope.astype(BF16)
        rest_o[t, :] = y[:, 0:512]
        mg, rs = unit(y[:, 512:1024])
        mg_o[t, :] = mg
        rs_o[t, :] = rs
        n_o[t, :] = (mg * inner[...]).astype(BF16)
    edge_sends(sc, n_o, ea_o.at[HALO:], eb_o.at[HALO:])
    edge_sends(sc, rest_o, ea_o.at[0:HALO], eb_o.at[0:HALO])


def mixed_kernel(sc, plane, ha, hb, rest, taps, down, mixed_o, gated_o, cat_o, rim):
    rows = plane.shape[0]
    add_edges(sc, rim, taps, ha, hb, (UPPER, UPPER), plane, mixed_o, 1)
    for t in tiles(rows):
        gated = (rest[t, :] * mixed_o[t, :]).astype(BF16)
        gated_o[t, :] = gated
        cat_o[t, :] = mm(gated, down[...]).astype(BF16)


def head_masks(rows):
    lane = lax.broadcasted_iota(jnp.int32, (rows, LANES), 1)
    return lane


def query_aug(sc, q, h, lane, utt):
    half = h % 2
    pair = q[:, (h // 2) * LANES : (h // 2 + 1) * LANES].astype(F32)
    off = HEAD_DIM * (1 - half)
    flags = jnp.where((lane == off + utt), 1.0, 0.0)
    mine = (lane >> 6) == half
    return jnp.where(mine, pair, flags).astype(BF16), jnp.where(mine, pair, 0.0).astype(BF16)


def key_bias(sc, src, lane, rows):
    row = lax.broadcasted_iota(jnp.int32, (rows, LANES), 0)
    shift = sc[0] - 1
    utt = row & shift
    pos = (row >> shift) + src * (rows >> shift)
    ok = pos < jnp.where(utt == 0, sc[2], sc[3])
    col = lane & 63
    seen = ok & (col == utt)
    return jnp.where((col < 2) & jnp.logical_not(seen), HIDE, 0.0)


def key_aug(kv, h, lane, bias):
    half = h % 2
    pair = kv[:, (h // 2) * LANES : (h // 2 + 1) * LANES].astype(F32)
    mine = (lane >> 6) == half
    return jnp.where(mine, pair, bias).astype(BF16)


def att_kernel(first, final, masks, sc, q, *rest):
    kvs, rest = rest[: len(masks)], rest[len(masks) :]
    if not first:
        c_i, l_i, acc_i = rest[:3]
        rest = rest[3:]
    if final:
        catg, out_w, c_o, l_o, *blocks, oT_o, ob_o, att_o, ea_o, eb_o, acc_o = rest
    else:
        c_o, l_o, *blocks, acc_o = rest
    if first:
        qm_o, blocks = blocks[0], blocks[1:]
    rows = q.shape[0]
    lane = lax.broadcasted_iota(jnp.int32, (rows, LANES), 1)
    utt = lax.broadcasted_iota(jnp.int32, (rows, LANES), 0) & (sc[0] - 1)
    qs = []
    for h in range(HEADS):
        with_flags, alone = query_aug(sc, q, h, lane, utt)
        qs.append(with_flags)
        if first:
            qm_o[h * rows : (h + 1) * rows, :] = alone
    if first:
        c_o[...] = jnp.full((8, rows), -1e30, F32)
        l_o[...] = jnp.zeros((8, rows), F32)
        acc_o[...] = jnp.zeros((HEADS * HEAD_DIM, rows), F32)
    else:
        c_o[...] = c_i[...]
        l_o[...] = l_i[...]
        acc_o[...] = acc_i[...]
    for mask, kv, w_o, top_o in zip(masks, kvs, blocks[0::2], blocks[1::2]):
        bias = key_bias(sc, sc[1] ^ mask, lane, rows)
        vT = kv[:, 256:512].astype(F32).T.astype(BF16)
        ahead = mm_nt(key_aug(kv, 0, lane, bias), qs[0])
        for h in range(HEADS):
            s = ahead
            if h + 1 < HEADS:
                ahead = mm_nt(key_aug(kv, h + 1, lane, bias), qs[h + 1])
            old = c_o[h : h + 1, :]
            new = jnp.maximum(old, jnp.floor(jnp.max(s, 0, keepdims=True) * EXP_SCALE))
            scale = jnp.exp2(old - new)
            c_o[h : h + 1, :] = new
            total = l_o[h : h + 1, :] * scale
            for r in tiles(rows):
                w = jnp.exp2(s[r] * EXP_SCALE - new)
                w_o[h * rows + r.start : h * rows + r.stop, :] = w.astype(BF16)
                total = total + jnp.sum(w, 0, keepdims=True)
            l_o[h : h + 1, :] = total
            hr = slice(h * HEAD_DIM, (h + 1) * HEAD_DIM)
            acc_o[hr, :] = acc_o[hr, :] * scale + mm(vT[hr, :], w_o[h * rows : (h + 1) * rows, :])
        top_o[...] = c_o[...]
    if final:
        for h in range(HEADS):
            hr = slice(h * HEAD_DIM, (h + 1) * HEAD_DIM)
            oT_o[hr, :] = acc_o[hr, :] / l_o[h : h + 1, :]
        ob = oT_o[...].T.astype(BF16)
        ob_o[...] = ob
        att_o[...] = mm(ob, out_w[...]).astype(BF16)
        edge_sends(sc, (att_o, catg), ea_o, eb_o)


def merge_kernel(
    sc, plane_i, att, catg, ha, hb, x1, taps, mw, dout, gains, w1, w2,
    out_o, un_o, em_o, ec_o, df_o, g2_o, a4_o, h_o, e2_o, du_o, g4_o, ea_o, eb_o, rim, plane,
):
    rows = att.shape[0]
    add_edges(sc, rim, taps, ha, hb, (LOWER, LOWER), plane_i, plane, 1)
    g4g = jnp.zeros((1, 256), F32)
    for t in tiles(rows):
        cat = jnp.concatenate([att[t, :], catg[t, :]], 1).astype(F32)
        united = (cat + plane[t, :]).astype(BF16)
        un_o[t, :] = united
        x2 = x1[t, :] + mm(united, mw[...])
        m2, rs2 = unit(x2)
        a4 = (m2 * gains[3:4, :]).astype(BF16)
        a4_o[t, :] = a4
        h, d = silu_parts(mm(a4, w1[...]))
        h = h.astype(BF16)
        h_o[t, :] = h
        x3 = x2 + 0.5 * mm(h, w2[...])
        m3, rs3 = unit(x3)
        out_o[t, :] = (m3 * gains[4:5, :]).astype(BF16)
        g3 = unit_back(dout[t, :], m3, rs3, gains[4:5, :])
        g4g = g4g + jnp.sum(dout[t, :] * m3, 0, keepdims=True)
        e2 = (0.5 * g3).astype(BF16)
        e2_o[t, :] = e2
        du = (mm_nt(e2, w2[...]) * d).astype(BF16)
        du_o[t, :] = du
        g2 = g3 + unit_back(mm_nt(du, w1[...]), m2, rs2, gains[3:4, :])
        g2_o[t, :] = g2
        em = g2.astype(BF16)
        em_o[t, :] = em
        df = mm_nt(em, mw[...])
        df_o[t, :] = df
        ec_o[t, :] = df.astype(BF16)
    g4_o[...] = jnp.broadcast_to(g4g, (8, 256))
    edge_sends(sc, ec_o, ea_o, eb_o)


def put_cols(buf, row, value):
    n = value.shape[0]
    for c in range(value.shape[1] // LANES):
        buf[row + c * n : row + (c + 1) * n, :] = value[:, c * LANES : (c + 1) * LANES].astype(BF16)


def grads_kernel(a4, h, e2, du, un, em, buf):
    put_cols(buf, 0, mm_tn(a4[...], du[...]))
    put_cols(buf, 2048, mm_tn(h[...], e2[...]))
    put_cols(buf, 4096, mm_tn(un[...], em[...]))


def split_kernel(
    sc, plane_i, ec, ha, hb, na, nb, rest, mixed, oT, l, taps, down, out_w,
    eatt_o, ecg_o, emix_o, dm_o, eaT_o, del_o, mb_o, ma_o, rim, plane,
):
    rows = plane_i.shape[0]
    add_edges(sc, rim, taps, ha, hb, (UPPER, LOWER), plane_i, plane, -1)
    for t in tiles(rows):
        eatt_o[t, :] = plane[t, 0:256].astype(BF16)
        ecg = plane[t, 256:512].astype(BF16)
        ecg_o[t, :] = ecg
        dg = mm_nt(ecg, down[...])
        emix_o[t, :] = (dg * rest[t, :]).astype(BF16)
        dm_o[t, :] = dg * mixed[t, :]
    every = slice(0, 2 * HALO)
    outside = []
    for c in range(2):
        cols = slice((c + 2) * LANES, (c + 3) * LANES)
        before, after = sides(sc, ha, hb, cols, every, every)
        rim[c, 0 : 2 * HALO, :] = before
        rim[c, 2 * HALO : 3 * HALO, :] = ec[0:HALO, cols].astype(F32)
        rim[c, 3 * HALO : 4 * HALO, :] = ec[rows - HALO : rows, cols].astype(F32)
        rim[c, 4 * HALO : 6 * HALO, :] = after
        parts = []
        for base in (0, 3 * HALO):
            acc = rim[c, base + HALO : base + 2 * HALO, :]
            for k in range(TAPS):
                tap = taps[k : k + 1, cols].astype(F32)
                acc = acc + rim[c, pl.ds(base + HALO - sc[0] * (k - TAPS // 2), HALO), :] * tap
            parts.append(acc)
        outside.append(jnp.concatenate(parts, 0))
    dg = mm_nt(jnp.concatenate(outside, 1).astype(BF16), down[...])
    before, after = sides(sc, na, nb, slice(None), LOWER, LOWER)
    mb_o[...] = (dg[0:HALO, :] * before).astype(BF16)
    ma_o[...] = (dg[HALO : 2 * HALO, :] * after).astype(BF16)
    doT = mm_nt(out_w[...], eatt_o[...])
    del_o[...] = jnp.zeros((8, rows), F32)
    for h in range(HEADS):
        hr = slice(h * HEAD_DIM, (h + 1) * HEAD_DIM)
        inv = 1.0 / l[h : h + 1, :]
        eaT = (doT[hr, :] * inv).astype(BF16)
        eaT_o[hr, :] = eaT
        del_o[h : h + 1, :] = jnp.sum(doT[hr, :] * oT[hr, :], 0, keepdims=True) * inv


def attback_kernel(first, kv, w, top, qm, c, eaT, delta, *rest):
    if first:
        dq_i = None
    else:
        dq_i, rest = rest[0], rest[1:]
    dq_o, d_o = rest
    rows = kv.shape[0]
    lane = lax.broadcasted_iota(jnp.int32, (rows, LANES), 1)
    nothing = jnp.zeros((HEAD_DIM, rows), BF16)
    kT = kv[:, 0:256].astype(F32).T.astype(BF16)
    for pair in range(HEADS // 2):
        cols = slice(pair * LANES, (pair + 1) * LANES)
        vcols = slice(256 + pair * LANES, 256 + (pair + 1) * LANES)
        scales = [jnp.exp2(top[h : h + 1, :] - c[h : h + 1, :]) for h in (2 * pair, 2 * pair + 1)]
        heads = [slice(h * HEAD_DIM, (h + 1) * HEAD_DIM) for h in (2 * pair, 2 * pair + 1)]
        grown = jnp.concatenate([eaT[hr, :].astype(F32) * r for hr, r in zip(heads, scales)], 0)
        ea = grown.T
        dk = jnp.zeros((rows, LANES), F32)
        dv = jnp.zeros((rows, LANES), F32)
        for half in range(2):
            h = pair * 2 + half
            hr = heads[half]
            here = slice(h * rows, (h + 1) * rows)
            mine = grown[half * HEAD_DIM : (half + 1) * HEAD_DIM, :].astype(BF16)
            dp = mm(kv[:, vcols], jnp.concatenate([mine, nothing] if half == 0 else [nothing, mine], 0))
            low = w[here, :]
            ds = (low.astype(F32) * (dp - delta[h : h + 1, :] * scales[half])).astype(BF16)
            dk = dk + mm(ds, qm[here, :])
            dv = dv + mm(low, jnp.where((lane >> 6) == half, ea, 0.0).astype(BF16))
            part = mm(kT[hr, :], ds)
            dq_o[hr, :] = part if first else dq_i[hr, :] + part
        d_o[:, cols] = (dk * SCORE_SCALE).astype(d_o.dtype)
        d_o[:, vcols] = dv.astype(d_o.dtype)


def gateback_kernel(
    sc, emix, ha, hb, mg, rs, dm, slope, a3, x1, gated, ecg, ob, eatt, taps, inner, up, gains,
    bcg_o, gi_o, buf, wide, plane,
):
    rows = emix.shape[0]
    fill_wide(sc, wide, (emix,), ha, hb)
    conv(sc, wide, taps, plane, rows, -1, False)
    gi = jnp.zeros((1, 512), F32)
    ups = []
    for t in tiles(rows):
        up_n = plane[t, :]
        dgate = unit_back(up_n, mg[t, :], rs[t, :], inner[...])
        gi = gi + jnp.sum(up_n * mg[t, :], 0, keepdims=True)
        sl = slope[t, :].astype(F32)
        eup = jnp.concatenate([dm[t, :] * sl[:, 0:512], dgate * sl[:, 512:1024]], 1).astype(BF16)
        ups.append(eup)
        m, rs1 = unit(x1[t, :])
        bcg_o[t, :] = unit_back(mm_nt(eup, up[...]), m, rs1, gains[2:3, :])
    gi_o[...] = jnp.broadcast_to(gi, (8, 512))
    eup = jnp.concatenate(ups, 0)
    put_cols(buf, 0, mm_tn(a3[...], eup))
    put_cols(buf, 2048, mm_tn(gated[...], ecg[...]))
    put_cols(buf, 3072, mm_tn(ob[...], eatt[...]))


def last_kernel(
    sc, dqT, dkv0, dkv1, dkv2, a2, x1, g2, bcg, a1, h, d, freq, wq, gains, w2, g1_o, du_o, buf,
):
    rows = x1.shape[0]
    cos, sin = turn_tables(sc, freq[...], rows)
    dq = dqT[...].T * SCORE_SCALE
    eqkvs, e1s = [], []
    for t in tiles(rows):
        dkv = dkv0[t, :] + dkv1[t, :].astype(F32) + dkv2[t, :].astype(F32)
        eq = rotate(dq[t], cos[t], sin[t], -1.0).astype(BF16)
        ek = rotate(dkv[:, 0:256], cos[t], sin[t], -1.0).astype(BF16)
        eqkv = jnp.concatenate([eq, ek, dkv[:, 256:512].astype(BF16)], 1)
        eqkvs.append(eqkv)
        m, rs = unit(x1[t, :])
        g1 = g2[t, :] + unit_back(mm_nt(eqkv, wq[...]), m, rs, gains[1:2, :]) + bcg[t, :]
        g1_o[t, :] = g1
        e1 = (0.5 * g1).astype(BF16)
        e1s.append(e1)
        du_o[t, :] = (mm_nt(e1, w2[...]) * d[t, :].astype(F32)).astype(BF16)
    put_cols(buf, 0, mm_tn(a1[...], du_o[...]))
    put_cols(buf, 2048, mm_tn(h[...], jnp.concatenate(e1s, 0)))
    put_cols(buf, 4096, mm_tn(a2[...], jnp.concatenate(eqkvs, 0)))


def input_kernel(sc, du, g1, gains, feat, w1, dx_o):
    rows = du.shape[0]
    for t in tiles(rows):
        keep = keep_mask(sc, t.start, (t.stop - t.start, 256))
        m, rs = unit(jnp.where(keep, feat[t, :].astype(F32), 0.0))
        back = unit_back(mm_nt(du[t, :], w1[...]), m, rs, gains[0:1, :])
        dx_o[t, :] = jnp.where(keep, g1[t, :] + back, 0.0)


def join_kernel(left, right, out):
    rows = right.shape[0]
    out[0:rows, :] = (left[0:rows, :].astype(F32) + right[...].astype(F32)).astype(BF16)
    if out.shape[0] > rows:
        out[rows:, :] = jnp.zeros((out.shape[0] - rows, out.shape[1]), BF16)


def rank():
    return lax.axis_index("grp") * lax.axis_size("blk") + lax.axis_index("blk")


def overlaps(sizes, low, high):
    start = 0
    for i, n in enumerate(sizes):
        a, b = max(start, low), min(start + n, high)
        if a < b:
            yield i, a - start, a - low, b - a
        start += n


def pack_kernel(sources, *refs):
    parts, keep, sends = refs[:sources], refs[sources], refs[sources + 1 :]
    half = keep.shape[0]
    bit = rank() % 2
    sizes = [ref.shape[0] for ref in parts]
    for own in range(2):

        @pl.when(bit == own)
        def _():
            for i, at, to, n in overlaps(sizes, own * half, (own + 1) * half):
                keep[to : to + n, :] = parts[i][at : at + n, :]
            start = (1 - own) * half
            for send in sends:
                for i, at, to, n in overlaps(sizes, start, start + send.shape[0]):
                    send[to : to + n, :] = parts[i][at : at + n, :]
                start += send.shape[0]


def fold_pieces_kernel(pair, mine, *refs):
    gots, keep, send = refs[:-2], refs[-2], refs[-1]
    half = keep.shape[0]
    bit = slot_bit(pair)
    sizes = [ref.shape[0] for ref in gots]
    for own in range(2):

        @pl.when(bit == own)
        def _():
            for ref, b in ((send, 1 - own), (keep, own)):
                for i, at, to, n in overlaps(sizes, b * half, (b + 1) * half):
                    value = mine[b * half + to : b * half + to + n, :].astype(F32) + gots[i][at : at + n, :].astype(F32)
                    ref[to : to + n, :] = value.astype(BF16)


def pieces_of(rows, count):
    step = -(-rows // (16 * count)) * 16
    return [min(step, rows - i * step) for i in range(count)]


def slot_bit(pair):
    index = rank()
    mask = jnp.where(index % 2 == 0, pair[0], pair[1])
    return (index // mask) % 2


def fold_kernel(pair, alone, *refs):
    if pair is None:
        mine, got, out = refs
        out[...] = (mine[...].astype(F32) + got[...].astype(F32)).astype(BF16)
        return
    *ins, keep, send = refs
    bit = slot_bit(pair)
    at = 0
    sources = list(zip(ins[0 : len(ins) - alone : 2], ins[1 : len(ins) - alone : 2]))
    for pieces in sources + [(ref,) for ref in ins[len(ins) - alone :]]:
        half = pieces[0].shape[0] // 2
        for ref, b in ((send, 1 - bit), (keep, bit)):
            here = pl.ds(pl.multiple_of(b * half, 16), half)
            value = pieces[0][here, :]
            if len(pieces) > 1:
                value = (value.astype(F32) + pieces[1][here, :].astype(F32)).astype(BF16)
            ref[at : at + half, :] = value
        at += half


def grow_into(bit, segments, mine, got, out):
    at = to = 0
    for n in segments:
        piece = slice(at, at + n)
        out[pl.ds(pl.multiple_of(to + bit * n, 16), n), :] = mine[piece, :]
        out[pl.ds(pl.multiple_of(to + (1 - bit) * n, 16), n), :] = got[piece, :]
        at += n
        to += 2 * n
    if at < mine.shape[0]:
        value = mine[at:, :].astype(F32) + got[at:, :].astype(F32)
        out[to : to + mine.shape[0] - at, :] = value.astype(BF16)


def grow_kernel(pair, segments, mine, got, out):
    grow_into(slot_bit(pair), segments, mine, got, out)


def quarter_pieces(layout, sizes, j, i, low, high):
    base = at = 0
    for n in sizes:
        start = base + j * (n // 2) + i * (n // 4)
        a, b = max(low, at), min(high, at + n // 4)
        if a < b:
            first, last = start + a - at, start + b - at
            for out, (row, count, cols) in enumerate(layout):
                if row is None or row >= sum(sizes):
                    continue
                for c in range(cols // LANES):
                    top = row + c * count
                    x, y = max(first, top), min(last, top + count)
                    if x < y:
                        yield out, a - low + x - first, x - top, y - x, c
        base += n
        at += n // 4


GAIN_OF = {2: (0, 0, 8), 4: (1, 8, 6), 6: (2, 14, 8), 11: (3, 22, 8)}
GAIN_ROWS = 30 * 256


def write_rows(layout, pieces, src, outs, bufs, sems, sums, weights, meanwhile=None):
    copies = []
    for i in range(len(layout)):
        mine = [p for p in pieces if p[0] == i]
        for _, at, to, n, c in mine:
            cols = slice(c * LANES, (c + 1) * LANES)
            value = src[at : at + n, :].astype(F32)
            bufs[i][to : to + n, cols] = value
            if i in GAIN_OF:
                g, block, _ = GAIN_OF[i]
                top = (block + c) * 256 + to
                sums[top : top + n, :] = value * weights[g][to : to + n, cols].astype(F32)
        if len(mine) * LANES == layout[i][2] and all(p[3] == layout[i][1] for p in mine):
            spots = [(slice(None), slice(None))]
        else:
            spots = [(slice(to, to + n), slice(c * LANES, (c + 1) * LANES)) for _, at, to, n, c in mine]
        for here in spots:
            copies.append(pltpu.make_async_copy(bufs[i].at[here], outs[i].at[here], sems.at[len(copies)]))
            copies[-1].start()
    if meanwhile is not None:
        copies += meanwhile()
    for copy in copies:
        copy.wait()


def each_quarter(slot, other, body):
    index = rank()
    if other:
        index = index ^ 1
    half = index % 2
    quarter = (index // jnp.where(half == 0, slot[0], slot[1])) % 2
    for j in range(2):
        for i in range(2):
            pl.when((half == j) & (quarter == i))(functools.partial(body, j, i))


def unpack_kernel(layout, sizes, slot, spans, first, *refs):
    count, parts = len(layout), len(spans)
    srcs, weights, refs = refs[:parts], refs[parts : parts + 4], refs[parts + 4 :]
    if not first:
        refs = refs[1 + count :]
    sums, outs, refs = refs[0], refs[1 : count + 1], refs[count + 1 :]
    bufs, sems = refs[:count], refs[count]
    for src, (other, flip, low, high) in zip(srcs, spans):

        def body(j, i, src=src, flip=flip, low=low, high=high):
            pieces = list(quarter_pieces(layout, sizes, j, i ^ flip, low, high))
            write_rows(layout, pieces, src, outs, bufs, sems, sums, weights)

        each_quarter(slot, other, body)


def unpack_last_kernel(layout, sizes, slot, span, rest, src, q, b, mate_q, gains, *refs):
    count = len(layout)
    weights, refs = refs[:4], refs[5 + count :]
    sums, outs, refs = refs[0], refs[1 : count + 1], refs[count + 1 :]
    bufs, small, sems, tail_sems = refs[:count], *refs[count:]

    def end(ref):
        return ref[ref.shape[0] - rest :, :].astype(F32)

    own, mate = end(q) + end(b), end(mate_q) + end(src)
    small[...] = own + mate
    late = []

    def send(i):
        late.append(pltpu.make_async_copy(bufs[i], outs[i], tail_sems.at[len(late)]))
        late[-1].start()

    for i, (row, n, cols) in enumerate(layout):
        if row is not None and row >= sum(sizes):
            for c in range(cols // LANES):
                start = row - sum(sizes) + c * n
                bufs[i][:, c * LANES : (c + 1) * LANES] = small[start : start + n, :]
            send(i)
    for c in range(2):
        start = 8 * TAPS + c
        bufs[0][4:5, c * LANES : (c + 1) * LANES] = small[start : start + 1, :]

    def write_gains():
        totals = []
        for _, block, many in GAIN_OF.values():
            total = sums[block * 256 : (block + 1) * 256, :]
            for c in range(1, many):
                total = total + sums[(block + c) * 256 : (block + c + 1) * 256, :]
            totals.append(total)
        line = lax.dot_general(
            jnp.ones((8, LANES), F32), jnp.concatenate(totals, 0), (((1,), (1,)), ((), ())),
            precision=lax.Precision.HIGHEST, preferred_element_type=F32,
        )
        for g in range(4):
            bufs[0][g : g + 1, :] = line[0:1, g * 256 : (g + 1) * 256] / gains[g : g + 1, :]
        copy = pltpu.make_async_copy(bufs[0], outs[0], sems.at[sems.shape[0] - 1])
        copy.start()
        return [copy]

    def body(j, i):
        pieces = list(quarter_pieces(layout, sizes, j, i ^ 1, span[2], span[3]))
        write_rows(layout, pieces, src, outs, bufs, sems, sums, weights, write_gains)

    each_quarter(slot, True, body)
    for copy in late:
        copy.wait()


def small_call(kernel, outs, ins, us, scratch=(), limit=None, out_space=None):
    vmem = pl.BlockSpec(memory_space=pltpu.VMEM)
    return pl.pallas_call(
        kernel,
        out_shape=[jax.ShapeDtypeStruct(s, d) for s, d in outs],
        in_specs=[vmem] * len(ins),
        out_specs=[vmem if out_space is None else pl.BlockSpec(memory_space=out_space)] * len(outs),
        scratch_shapes=list(scratch),
        compiler_params=pltpu.CompilerParams(vmem_limit_bytes=limit or VMEM_BYTES),
        cost_estimate=pl.CostEstimate(flops=int(us * UNIT), bytes_accessed=1, transcendentals=0),
    )(*ins)


def exchange(value, pair):
    count = lax.axis_size("grp") * lax.axis_size("blk")
    return lax.ppermute(value, AXES, [(i, i ^ pair[i % 2]) for i in range(count)])


def slot_pairs():
    count = lax.axis_size("grp") * lax.axis_size("blk")
    masks = [1 << i for i in range(1, count.bit_length() - 1)]
    first = list(masks)
    second = list(masks)
    if len(masks) > 2:
        first[1], first[2] = first[2], first[1]
        second[0], second[1] = second[1], second[0]
    return list(zip(first, second))


def fold(pair, *ins, alone=0):
    paired = ins[: len(ins) - alone]
    rows = sum(v.shape[0] for v in paired[0::2]) // 2 + sum(v.shape[0] for v in ins[len(paired) :]) // 2
    outs = [((rows, LANES), BF16)] * 2
    return small_call(functools.partial(fold_kernel, pair, alone), outs, ins, 0.5)


def grow_cut_kernel(pair, segments, mine, got, out, low, high, near, end):
    grow_into(slot_bit(pair), segments, mine, got, out)
    cut, step = low.shape[0], near.shape[0]
    low[...] = out[0:cut, :]
    high[...] = out[cut:, :]
    near[...] = out[cut : cut + step, :]
    end[...] = out[cut + step :, :]


def gather(mine, slots, sizes, rest):
    for i in reversed(range(1, len(slots))):
        got = exchange(mine, slots[i])
        if i > 2:
            segments, rows = (mine.shape[0],), 2 * mine.shape[0]
        elif i == 2:
            segments, rows = (mine.shape[0] - rest // 2, rest // 2), 2 * mine.shape[0]
        else:
            segments, rows = tuple(n // 8 for n in sizes), sum(sizes) // 4 + rest
        shapes = [((rows, LANES), BF16)]
        if i > 1:
            (mine,) = small_call(functools.partial(grow_kernel, slots[i], segments), shapes, [mine, got], 0.4)
            continue
        cut = rows * 5 // 192 * 16
        step = (rows - cut) // 32 * 16
        shapes += [((n, LANES), BF16) for n in (cut, rows - cut, step, rows - cut - step)]
        return small_call(functools.partial(grow_cut_kernel, slots[i], segments), shapes, [mine, got], 0.5)


def unpack(kernel, layout, name, ins, held, scratch, us):
    shapes = [(n, cols) for _, n, cols in layout]
    hbm, vmem = pl.BlockSpec(memory_space=pltpu.HBM), pl.BlockSpec(memory_space=pltpu.VMEM)
    return pl.pallas_call(
        kernel,
        out_shape=[jax.ShapeDtypeStruct(s, F32) for s in [(GAIN_ROWS, LANES)] + shapes],
        in_specs=[vmem] * len(ins) + ([vmem] + [hbm] * len(shapes) if held else []),
        out_specs=[vmem] + [hbm] * len(shapes),
        scratch_shapes=[pltpu.VMEM(s, F32) for s in shapes] + scratch + [pltpu.SemaphoreType.DMA((24,))],
        input_output_aliases={len(ins) + i: i for i in range(len(held))},
        compiler_params=pltpu.CompilerParams(vmem_limit_bytes=32 * 1024 * 1024),
        cost_estimate=pl.CostEstimate(flops=int(us * UNIT), bytes_accessed=1, transcendentals=0),
        name=name,
    )(*ins, *held)


def spread(mine, low, high, near, last, slot, sizes, rest, layout, gains, weights):
    rows, cut, step = mine.shape[0], low.shape[0], near.shape[0]
    end = rows - rest
    got_low, got_high = exchange(low, slot), exchange(high, slot)

    def write(spans, ins, held, name):
        kernel = functools.partial(unpack_kernel, layout, sizes, slot, spans, not held)
        return list(unpack(kernel, layout, name, [*ins, *weights], held, [], 0.3))

    held = write(((False, 0, 0, end),), [mine], [], "unpack_own")
    got_low, low, near, last, held[0] = lax.optimization_barrier((got_low, low, near, last, held[0]))
    mates = [exchange(v, (1, 1)) for v in (low, near, last, got_low)]
    held = write(((False, 1, 0, cut),), [got_low], held, "unpack_low")
    spans = ((True, 0, 0, cut), (True, 0, cut, cut + step), (True, 0, cut + step, end), (True, 1, 0, cut))
    held = write(spans, mates, held, "unpack_mate")
    got_high, held[0] = lax.optimization_barrier((got_high, held[0]))
    mate_high = exchange(got_high, (1, 1))
    held = write(((False, 1, cut, end),), [got_high], held, "unpack_high")
    kernel = functools.partial(unpack_last_kernel, layout, sizes, slot, (True, 1, cut, end), rest)
    scratch = [pltpu.VMEM((rest, LANES), F32), pltpu.SemaphoreType.DMA((24,))]
    ins = [mate_high, mine, got_high, mates[2], gains, *weights]
    return unpack(kernel, layout, "unpack_last", ins, held, scratch, 2.0)[1:]


def plain(kernel, ins, outs, kept, *refs):
    head = refs[: ins]
    made = refs[ins + kept : ins + kept + outs]
    scratch = refs[ins + 2 * kept + outs :]
    kernel(*head, *made, *scratch)


class Layer:
    def __init__(self, plan):
        self.plan = plan
        self.step = 0
        self.have = {}

    def __getitem__(self, key):
        return self.have[key]

    def __setitem__(self, key, value):
        self.have[key] = value

    def run(self, kernel, outs, extra=(), scratch=(), us=1.0):
        name, reads = self.plan[self.step]
        later = [r for _, more in self.plan[self.step + 1 :] for r in more]
        kept = sorted(k for k in self.have if k in later and k not in reads and k != "sc")
        self.step += 1

        def size(key):
            return self.have[key].size * self.have[key].dtype.itemsize

        while sum(map(size, kept)) > CARRY_BYTES:
            kept.remove(max(kept, key=size))
        smem = pl.BlockSpec(memory_space=pltpu.SMEM)
        vmem = pl.BlockSpec(memory_space=pltpu.VMEM)
        ins = [self.have[r] for r in reads] + list(extra)
        in_specs = [smem if r == "sc" else vmem for r in reads] + [vmem] * len(extra)
        shapes = [jax.ShapeDtypeStruct(s, d) for _, s, d in outs]
        shapes += [jax.ShapeDtypeStruct(self.have[k].shape, self.have[k].dtype) for k in kept]
        made = pl.pallas_call(
            functools.partial(plain, kernel, len(ins), len(outs), len(kept)),
            out_shape=shapes,
            in_specs=in_specs + [vmem] * len(kept),
            out_specs=[vmem] * len(shapes),
            scratch_shapes=list(scratch),
            input_output_aliases={len(ins) + i: len(outs) + i for i in range(len(kept))},
            compiler_params=pltpu.CompilerParams(vmem_limit_bytes=VMEM_BYTES),
            cost_estimate=pl.CostEstimate(flops=int(us * UNIT), bytes_accessed=1, transcendentals=0),
            name=name,
        )(*ins, *[self.have[k] for k in kept])
        for key, value in zip([o[0] for o in outs] + kept, made):
            self.have[key] = value


def swap(value, axis, mask):
    count = math.prod(lax.axis_size(a) for a in axis) if isinstance(axis, tuple) else lax.axis_size(axis)
    return lax.ppermute(value, axis, [(i, i ^ mask) for i in range(count)])


def halo(ea, eb):
    count = lax.axis_size("blk")
    near = [(i, i ^ 1) for i in range(count)]
    far = []
    for i in range(1, count - 1, 2):
        far += [(i, i + 1), (i + 1, i)]
    return lax.ppermute(ea, "blk", near), lax.ppermute(eb, "blk", far)


def local(
    features, d_out, bucket_batch, valid_len, time_start, time_width, freq_start, freq_width,
    gains, inner_gain, ffn1_in, ffn1_out, qkv_w, out_w, cg_up, cg_conv, cg_down, merge_conv,
    merge_w, ffn2_in, ffn2_out,
):
    rows, width = features.shape
    half = cg_down.shape[0]
    ff = ffn1_in.shape[1]
    blocks = lax.axis_size("blk")
    me = lax.axis_index("blk")
    freq = np.exp(np.arange(32, dtype=np.float64) * (-2.0 * math.log(10000.0) / HEAD_DIM))
    freq = jnp.asarray(np.tile(freq, 4)[None, :].astype(np.float32))
    wide = pltpu.VMEM((half // LANES, rows + 2 * HALO, LANES), F32)
    plane = pltpu.VMEM((rows, half), F32)
    rim = pltpu.VMEM((half // LANES, 6 * HALO, LANES), F32)
    pairs = [(m, m | 1) for m in range(0, blocks, 2)]
    kvs = [(f"kv{a}", f"kv{b}") for a, b in pairs]
    even = [a for a, _ in pairs[1:]]
    state = ["c", "l", "acc"]
    plan = [("gate", ["sc", "x1"])]
    plan += [("att_first", ["sc", "q", *kvs[0]])]
    plan += [("conv_gate", ["sc", "n"]), ("mixed", ["sc", "plane1", "na", "nb", "rest"])]
    far_masks = [m for a, b in pairs[1:] for m in (a, b)]
    plan += [("att_mid", ["sc", "q", f"kv{m}", *state]) for m in far_masks[:-1]]
    plan += [
        ("att_last", ["sc", "q", f"kv{far_masks[-1]}", *state, "catg"]),
        ("conv_merge", ["sc", "att", "catg"]),
        ("merge", ["sc", "plane2", "att", "catg", "ha", "hb", "x1"]),
        ("grads2", ["a4", "h2", "e2", "du2", "un", "em"]),
        ("conv_back", ["sc", "df", "ec"]),
        ("split", ["sc", "plane3", "ec", "ca", "cb", "na", "nb", "rest", "mixed", "oT", "l"]),
    ]
    back = ["qm", "c", "eaT", "delta"]

    def back_reads(m):
        return [f"kv{m}", f"w{m}", f"top{m}", *back] + ([] if m == even[0] + 1 else ["dqT"])

    for e in even:
        for m in (e + 1, e):
            plan += [("attback", back_reads(m))]
        plan += [("join_kv", [f"pd{e}", f"in{e}"])]
    plan += [
        ("attback", back_reads(1)),
        ("gateback", ["sc", "emix", "mb", "ma", "mg", "rs", "dm", "slope", "a3", "x1", "gated", "ecg", "ob", "eatt"]),
        ("pack_early", ["part1", "buf2"]),
        ("attback", back_reads(0)),
        ("fold_early", ["keep", "got0", "got1", "got2"]),
    ]
    total = f"far{even[0]}"
    for e in even[1:]:
        plan += [("join_far", [total, f"far{e}"])]
        total = f"t{e}"
    plan += [
        ("last", ["sc", "dqT", "own", "near", total, "a2", "x1", "g2", "bcg", "a1", "h1", "d1"]),
        ("pack_late", ["buf3"]),
        ("merge_taps", ["sc", "ec", "ca", "cb", "att", "catg"]),
        ("gate_taps", ["sc", "emix", "mb", "ma", "n", "tm", "g4", "gi"]),
        ("input_grad", ["sc", "du1", "g1"]),
    ]
    run = Layer(plan)
    smem = pl.BlockSpec(memory_space=pltpu.SMEM)
    vmem = pl.BlockSpec(memory_space=pltpu.VMEM)
    raw = (bucket_batch, valid_len, time_start, time_width, freq_start, freq_width, gains, freq,
           features, ffn1_in, ffn1_out, qkv_w)
    def narrow(name, kind=BF16):
        return (name, (rows, width), kind)

    def middle(name, kind=BF16):
        return (name, (rows, half), kind)

    def broad(name, kind=BF16):
        return (name, (rows, ff), kind)

    outs = [narrow("x1", F32), narrow("a1"), broad("h1"), broad("d1"), narrow("a2"), narrow("q"), middle("kv0"), middle("kvs")]
    made = pl.pallas_call(
        pre_kernel,
        out_shape=[jax.ShapeDtypeStruct((16,), jnp.int32)] + [jax.ShapeDtypeStruct(o[1], o[2]) for o in outs],
        in_specs=[pl.BlockSpec(memory_space=pltpu.HBM)] * 12,
        out_specs=[smem] + [vmem] * 8,
        scratch_shapes=[pltpu.SMEM(v.shape, v.dtype) for v in raw[:6]]
        + [pltpu.VMEM(v.shape, v.dtype) for v in raw[6:]] + [pltpu.SemaphoreType.DMA((12,))],
        compiler_params=pltpu.CompilerParams(vmem_limit_bytes=VMEM_BYTES),
        cost_estimate=pl.CostEstimate(flops=int(4.0 * UNIT), bytes_accessed=1, transcendentals=0),
        name="pre",
    )(raw[0], *[pltpu.with_memory_space_constraint(v, pltpu.HBM) for v in raw[1:]])
    for key, value in zip(["sc"] + [o[0] for o in outs], made):
        run[key] = value
    held = {0: run["kvs"]}
    bit = blocks // 2
    while bit > 1:
        held.update({m | bit: swap(held[m], "blk", bit) for m in list(held)})
        bit //= 2
    held[1] = swap(held[0], "blk", 1)

    def send_edges():
        return halo(run["ea"], run["eb"])

    edge = [("ea", (HALO, half), BF16), ("eb", (HALO, half), BF16)]
    edge2 = [("ea", (2 * HALO, half), BF16), ("eb", (2 * HALO, half), BF16)]
    stats = [("c", (8, rows), F32), ("l", (8, rows), F32)]

    def kept(*masks):
        return [o for m in masks for o in ((f"w{m}", (HEADS * rows, rows), BF16), (f"top{m}", (8, rows), F32))]


    run.run(
        gate_kernel,
        [narrow("a3"), middle("rest", F32), broad("slope"), middle("n"), middle("mg", F32), ("rs", (rows, 1), F32)] + edge2,
        [gains, inner_gain[None, :], cg_up], us=2.5,
    )
    edges = send_edges()
    run["kv1"] = held[1]
    run.run(functools.partial(att_kernel, True, False, pairs[0]), stats + [("qm", (HEADS * rows, LANES), BF16)] + kept(*pairs[0]) + [("acc", (width, rows), F32)], us=0.5)
    run.run(functools.partial(local_conv_kernel, 1, False), [middle("plane1", F32)], [cg_conv], [wide], us=0.3)
    run["na"], run["nb"] = edges
    run.run(
        mixed_kernel, [middle("mixed", F32), middle("gated"), narrow("catg")],
        [cg_conv, cg_down], [rim], us=1.5,
    )
    for a, b in pairs[1:]:
        late, _ = lax.optimization_barrier((held[a], run["catg"]))
        run[f"kv{a}"] = late
        mate = swap(late, "blk", 1)
        run.run(
            functools.partial(att_kernel, False, False, (a,)), stats + kept(a) + [("acc", (width, rows), F32)], us=2.8,
        )
        run[f"kv{b}"] = mate
        if b < blocks - 1:
            run.run(
                functools.partial(att_kernel, False, False, (b,)), stats + kept(b) + [("acc", (width, rows), F32)], us=2.8,
            )
    run.run(
        functools.partial(att_kernel, False, True, (blocks - 1,)),
        stats + kept(blocks - 1) + [("oT", (width, rows), F32), narrow("ob"), narrow("att")] + edge,
        [out_w], [pltpu.VMEM((width, rows), F32)], us=3.0,
    )
    edges = send_edges()
    run.run(functools.partial(local_conv_kernel, 1, False), [middle("plane2", F32)], [merge_conv], [wide], us=0.3)
    run["ha"], run["hb"] = edges
    run.run(
        merge_kernel,
        [narrow("out"), middle("un"), narrow("em"), middle("ec"), middle("df", F32), narrow("g2", F32), narrow("a4"),
         broad("h2"), narrow("e2"), broad("du2"), ("g4", (8, width), F32)] + edge2,
        [merge_conv, merge_w, d_out, gains, ffn2_in, ffn2_out], [rim, plane], us=5.5,
    )
    edges = send_edges()
    run.run(grads_kernel, [("part1", (5120, LANES), BF16)], us=0.3)
    run.run(functools.partial(local_conv_kernel, -1, True), [middle("plane3", F32)], [merge_conv], [wide], us=0.3)
    run["ca"], run["cb"] = edges
    run.run(
        split_kernel,
        [narrow("eatt"), narrow("ecg"), middle("emix"), middle("dm", F32), ("eaT", (width, rows), BF16),
         ("delta", (8, rows), F32), ("mb", (HALO, half), BF16), ("ma", (HALO, half), BF16)],
        [merge_conv, cg_down, out_w], [rim, plane], us=2.0,
    )

    tall = ("dqT", (width, rows), F32)
    pair_sum = (rows, 2 * width)
    for e in even:
        for m in (e + 1, e):
            run.run(
                functools.partial(attback_kernel, m == even[0] + 1), [tall, (f"pd{m}", pair_sum, BF16)], us=0.5
            )
            if m & 1:
                arrival = swap(run[f"pd{m}"], "blk", 1)
        run[f"in{e}"] = arrival
        run.run(join_kernel, [(f"s{e}", (rows + 32, 2 * width), BF16)], us=0.2)
    fars = {e: swap(run[f"s{e}"], "blk", e) for e in even}
    run.run(functools.partial(attback_kernel, False), [tall, ("pd1", pair_sum, BF16)], us=0.05)
    near = swap(run["pd1"], "blk", 1)
    run.run(
        gateback_kernel,
        [narrow("bcg", F32), ("gi", (8, half), F32), ("buf2", (3584, LANES), BF16)],
        [cg_conv, inner_gain[None, :], cg_up, gains], [wide, plane], us=0.5,
    )
    count = lax.axis_size("grp") * blocks
    used, late, rest = 8704, 5632, 256
    slots = slot_pairs()
    grain = 16 << (len(slots) - 2)
    sizes = (used + 8 * (-((used + late) // 8 + rest) % grain), late)
    cuts = pieces_of(sizes[0] // 2, 3)
    run.run(
        functools.partial(pack_kernel, 2),
        [("keep", (sizes[0] // 2, LANES), BF16)] + [(f"send{i}", (n, LANES), BF16) for i, n in enumerate(cuts)], us=0.1,
    )
    gots = [exchange(run[f"send{i}"], (1, 1)) for i in range(3)]
    run.run(functools.partial(attback_kernel, False), [tall, ("own", pair_sum, F32)], us=0.5)
    for i in range(3):
        run[f"got{i}"] = gots[i]
    for e in even:
        run[f"far{e}"] = fars[e]
    run["near"] = near
    run.run(
        functools.partial(fold_pieces_kernel, slots[0]),
        [("early", (sizes[0] // 4, LANES), BF16), ("send_early", (sizes[0] // 4, LANES), BF16)], us=0.2,
    )
    early_got = exchange(run["send_early"], slots[0])
    for e in even[1:]:
        run.run(join_kernel, [(f"t{e}", (rows + 32, 2 * width), BF16)], us=0.2)
    run.run(
        last_kernel,
        [narrow("g1", F32), broad("du1"), ("buf3", (5632, LANES), BF16)],
        [freq, qkv_w, gains, ffn1_out], us=0.3,
    )
    quarter = ((sizes[1] // 4, LANES), BF16)
    cuts = pieces_of(sizes[1] // 2, 2)
    run.run(
        functools.partial(pack_kernel, 1),
        [("keep3", (sizes[1] // 2, LANES), BF16)] + [(f"late{i}", (n, LANES), BF16) for i, n in enumerate(cuts)], us=0.1,
    )
    gots = [exchange(run[f"late{i}"], (1, 1)) for i in range(2)]
    gots[0], early_got = lax.optimization_barrier((gots[0], early_got))
    keep3, send3 = small_call(functools.partial(fold_pieces_kernel, slots[0]), [quarter, quarter], [run["keep3"], *gots], 0.3)
    late_got = exchange(send3, slots[0])
    _, run["ec"] = lax.optimization_barrier((send3, run["ec"]))
    run.run(merge_taps_kernel, [("tm", (128, LANES), F32)], (), [wide], us=1.0)
    late_got, run["tm"] = lax.optimization_barrier((late_got, run["tm"]))
    keep, send = fold(slots[1], run["early"], early_got, keep3, late_got)
    got = exchange(send, slots[1])
    _, run["gi"] = lax.optimization_barrier((send, run["gi"]))
    run.run(gate_taps_kernel, [("small", (rest, LANES), BF16)], (), [wide, pltpu.VMEM((rest, LANES), F32)], us=1.0)
    keep, send = fold(slots[2], keep, got, run["small"], alone=1)
    got = exchange(send, slots[2])
    for pair in slots[3:]:
        keep, send = fold(pair, keep, got)
        got = exchange(send, pair)
    _, run["g1"] = lax.optimization_barrier((send, run["g1"]))
    run.run(input_kernel, [narrow("dx", F32)], [gains, features, ffn1_in], us=0.3)
    got, run["dx"] = lax.optimization_barrier((got, run["dx"]))
    (mine,) = small_call(functools.partial(fold_kernel, None, 0), [(keep.shape, BF16)], [keep, got], 0.3)
    base = sizes[0]
    tail = base + late
    layout = (
        (None, 5, 256), (tail + 8 * TAPS + 2, 1, 512),
        (base, 256, 1024), (base + 2048, 1024, 256), (base + 4096, 256, 768), (8192, 256, 256),
        (5120, 256, 1024), (tail + 4 * TAPS, TAPS, 512), (7168, 512, 256), (tail, TAPS, 512), (4096, 512, 256),
        (0, 256, 1024), (2048, 1024, 256),
    )
    whole = gather(mine, slots, sizes, rest)
    weights = (ffn1_in, qkv_w, cg_up, ffn2_in)
    sums = spread(*whole, slots[0], sizes, rest, layout, gains, weights)
    return (run["out"], run["dx"], sums[0], sums[1][0], *sums[2:])


def solution(mesh):
    rows = P(("grp", "blk"), None)
    in_specs = (rows, rows, P("grp")) + (P("grp", None),) * 5 + (P(),) * 13
    out_specs = (rows, rows) + (P(),) * 13
    return jax.shard_map(local, mesh=mesh, in_specs=in_specs, out_specs=out_specs, check_vma=False)
```

```python
import functools
import math

import jax
import jax.numpy as jnp
import numpy as np
from jax import lax
from jax.experimental import pallas as pl
from jax.experimental.pallas import tpu as pltpu
from jax.sharding import PartitionSpec as P

HEADS = 4
HEAD_DIM = 64
HALO = 32
LOG_BASE = 1.4426950408889634
EPSILON = 1e-05
SCORE_SCALE = HEAD_DIM ** (-0.5)
EXP_SCALE = SCORE_SCALE * LOG_BASE
HIDE = -(2.0 ** 100)
AXES = ("grp", "blk")
F32 = jnp.float32
BF16 = jnp.bfloat16
LANES = 128
VMEM_BYTES = 16 * 1024 * 1024
UNIT = 0.35e9
CARRY_BYTES = 30 * 1024 * 1024


def mm(left, right):
    return jnp.dot(left, right, preferred_element_type=F32)


def mm_nt(left, right):
    return lax.dot_general(left, right, (((1,), (1,)), ((), ())), preferred_element_type=F32)


def mm_tn(left, right):
    return lax.dot_general(left, right, (((0,), (0,)), ((), ())), preferred_element_type=F32)


def unit(v):
    center = v - jnp.mean(v, -1, keepdims=True)
    rs = lax.rsqrt(jnp.mean(center * center, -1, keepdims=True) + EPSILON)
    return center * rs, rs


def unit_back(up, m, rs, gain):
    eg = up * gain
    return rs * (eg - jnp.mean(eg, -1, keepdims=True) - m * jnp.mean(eg * m, -1, keepdims=True))


def silu_parts(u):
    sig = 0.5 + 0.5 * jnp.tanh(0.5 * u)
    h = u * sig
    return h, sig + h * (1.0 - sig)


def gelu_parts(t):
    root = math.sqrt(2.0 / math.pi)
    t2 = t * t
    th = jnp.tanh(root * t * (1.0 + 0.044715 * t2))
    half = 0.5 + 0.5 * th
    slope = half + 0.5 * root * t * (1.0 - th * th) * (1.0 + 3.0 * 0.044715 * t2)
    return t * half, slope


def rows_of(sc, r0, shape):
    row = lax.broadcasted_iota(jnp.int32, shape, 0) + r0
    shift = sc[0] - 1
    utt = row & shift
    pos = (row >> shift) + sc[1] * (512 >> shift)
    return utt, pos


def keep_mask(sc, r0, shape):
    utt, pos = rows_of(sc, r0, shape)
    ch = lax.broadcasted_iota(jnp.int32, shape, 1)
    first = utt == 0

    def pick(i):
        return jnp.where(first, sc[i], sc[i + 1])

    ok = (pos < pick(2)) & jnp.logical_not((pos >= pick(4)) & (pos < pick(6)))
    ok = ok & jnp.logical_not((ch >= pick(8)) & (ch < pick(10)))
    return ok


def turn_tables(sc, freq, rows):
    shift = sc[0] - 1
    coarse = lax.broadcasted_iota(jnp.int32, (rows // 16, LANES), 0) * 16
    fine = lax.broadcasted_iota(jnp.int32, (16, LANES), 0)
    a = ((coarse >> shift) + sc[1] * (rows >> shift)).astype(F32) * freq
    c = (fine >> shift).astype(F32) * freq
    ca, sa, cc, cs = jnp.cos(a), jnp.sin(a), jnp.cos(c), jnp.sin(c)
    cos = ca[:, None, :] * cc[None] - sa[:, None, :] * cs[None]
    sin = sa[:, None, :] * cc[None] + ca[:, None, :] * cs[None]
    return cos.reshape(rows, LANES), sin.reshape(rows, LANES)


def rotate(v, cos, sin, direction):
    lane = lax.broadcasted_iota(jnp.int32, (v.shape[0], LANES), 1)
    lower = (lane & 63) < 32
    signed = jnp.where(lower, -direction, direction) * sin
    parts = []
    for i in range(v.shape[1] // LANES):
        p = v[:, i * LANES : (i + 1) * LANES]
        other = jnp.where(lower, pltpu.roll(p, LANES - 32, 1), pltpu.roll(p, 32, 1))
        parts.append(p * cos + other * signed)
    return jnp.concatenate(parts, 1)


def edge_sends(sc, refs, a_ref, b_ref):
    odd = (sc[1] & 1) == 1
    col = 0
    count = a_ref.shape[0]
    for ref in refs if isinstance(refs, tuple) else (refs,):
        rows, width = ref.shape
        first = ref[0:count, :].astype(BF16)
        last = ref[rows - count : rows, :].astype(BF16)
        cols = slice(col, col + width)
        col += width

        @pl.when(odd)
        def _():
            a_ref[:, cols] = first
            b_ref[:, cols] = last

        @pl.when(jnp.logical_not(odd))
        def _():
            a_ref[:, cols] = last
            b_ref[:, cols] = first


def sides(sc, ha, hb, cols, before, after):
    odd = (sc[1] & 1) == 1
    first = jnp.where(odd, ha[before, cols].astype(F32), hb[before, cols].astype(F32))
    return first, jnp.where(odd, hb[after, cols].astype(F32), ha[after, cols].astype(F32))


LOWER, UPPER = slice(0, HALO), slice(HALO, 2 * HALO)


def fill_wide(sc, wide, sources, ha, hb, spots=None):
    at = 0
    for z in sources:
        rows, width = z.shape
        for c in range(width // LANES):
            cols = slice(at * LANES, (at + 1) * LANES)
            if spots is None:
                before, after = ha[:, cols].astype(F32), hb[:, cols].astype(F32)
            else:
                before, after = sides(sc, ha, hb, cols, *spots)
            wide[at, 0:HALO, :] = before
            wide[at, HALO : HALO + rows, :] = z[:, c * LANES : (c + 1) * LANES].astype(F32)
            wide[at, HALO + rows : 2 * HALO + rows, :] = after
            at += 1


CONV_ROWS = 256
TAP_ROWS = 128
TAPS = 31


def local_conv_kernel(direction, add, sc, *refs):
    *sources, taps, out, wide = refs
    if add:
        base, sources = sources[0], sources[1:]
        out[...] = base[...]
    rows = out.shape[0]
    at = 0
    for z in sources:
        for c in range(z.shape[1] // LANES):
            wide[at, 0:HALO, :] = jnp.zeros((HALO, LANES), F32)
            wide[at, HALO : HALO + rows, :] = z[:, c * LANES : (c + 1) * LANES].astype(F32)
            wide[at, HALO + rows : 2 * HALO + rows, :] = jnp.zeros((HALO, LANES), F32)
            at += 1
    conv(sc, wide, taps, out, rows, direction, add)


def add_edges(sc, rim, taps, ha, hb, spots, plane, out, direction):
    step = sc[0] * direction
    rows = plane.shape[0]
    for c in range(taps.shape[1] // LANES):
        cols = slice(c * LANES, (c + 1) * LANES)
        before, after = sides(sc, ha, hb, cols, *spots)
        rim[c, 0:HALO, :] = before
        rim[c, HALO : 5 * HALO, :] = jnp.zeros((4 * HALO, LANES), F32)
        rim[c, 5 * HALO : 6 * HALO, :] = after
    if out is not plane:
        out[HALO : rows - HALO, :] = plane[HALO : rows - HALO, :]
    for c in range(taps.shape[1] // LANES):
        cols = slice(c * LANES, (c + 1) * LANES)
        for base, start in ((0, 0), (3 * HALO, rows - HALO)):
            acc = plane[start : start + HALO, cols]
            for k in range(TAPS):
                tap = taps[k : k + 1, cols].astype(F32)
                acc = acc + rim[c, pl.ds(base + HALO + step * (k - TAPS // 2), HALO), :] * tap
            out[start : start + HALO, cols] = acc


def by_batch(sc, body):
    for batch in (1, 2):
        pl.when(sc[0] == batch)(functools.partial(body, batch))


def conv(sc, wide, taps, out, rows, direction, add):
    size = min(CONV_ROWS, rows)

    def run(batch):
        groups = {}
        for k in range(TAPS):
            at = HALO + direction * batch * (k - TAPS // 2)
            groups.setdefault(at % 8, []).append((at // 8 * 8, k))
        chunks = rows // size

        def block(c, carry):
            cols = pl.ds(pl.multiple_of(c * LANES, LANES), LANES)
            ws = [taps[k : k + 1, cols].astype(F32) for k in range(TAPS)]

            def body(i, carry):
                r0 = pl.multiple_of(i * size, size)
                here = pl.ds(r0, size)
                window = wide[c, pl.ds(r0, size + 2 * HALO), :]
                acc = out[here, cols] if add else None
                for shift, members in sorted(groups.items()):
                    n = size + 8 if shift else size
                    part = None
                    for at, k in members:
                        term = window[at : at + n] * ws[k]
                        part = term if part is None else part + term
                    if shift:
                        part = pltpu.roll(part, n - shift, 0)[:size]
                    acc = part if acc is None else acc + part
                out[here, cols] = acc
                return carry

            return lax.fori_loop(0, chunks, body, carry)

        lax.fori_loop(0, taps.shape[1] // LANES, block, 0)

    by_batch(sc, run)


def correlate(sc, wide, sources, out, row, rows):
    size = min(TAP_ROWS, rows)
    chunks = rows // size

    def run(batch):
        done = 0
        for z in sources:
            blocks = z.shape[1] // LANES

            def block(c, carry, z=z, done=done):
                cols = pl.ds(pl.multiple_of(c * LANES, LANES), LANES)

                def body(i, sums):
                    r0 = pl.multiple_of(i * size, size)
                    zc = z[pl.ds(r0, size), cols].astype(F32)
                    window = wide[done + c, pl.ds(r0, size + 2 * HALO), :]
                    padded = jnp.concatenate([zc, jnp.zeros((8, LANES), F32)], 0)
                    turned = {0: zc}
                    new = []
                    for k in range(TAPS):
                        start = HALO - batch * (k - TAPS // 2)
                        shift = start % 8
                        if shift not in turned:
                            turned[shift] = pltpu.roll(padded, shift, 0)
                        factor = turned[shift]
                        n = factor.shape[0]
                        prod = window[start - shift : start - shift + n] * factor
                        new.append(sums[k] + jnp.sum(prod.reshape(n // 8, 8, LANES), 0))
                    return tuple(new)

                zero = tuple(jnp.zeros((8, LANES), F32) for _ in range(TAPS))
                sums = lax.fori_loop(0, chunks, body, zero)
                for k in range(TAPS):
                    out[pl.ds(row + (done + c) * TAPS + k, 1), :] = jnp.sum(sums[k], 0, keepdims=True)
                return carry

            lax.fori_loop(0, blocks, block, 0)
            done += blocks

    by_batch(sc, run)


def merge_taps_kernel(sc, ec, ca, cb, att, catg, out, wide):
    fill_wide(sc, wide, (ec,), ca, cb, (UPPER, LOWER))
    correlate(sc, wide, (att, catg), out, 0, ec.shape[0])


def gate_taps_kernel(sc, emix, before, after, n, merge_taps, g4, gi, small_o, wide, total):
    fill_wide(sc, wide, (emix,), before, after)
    total[0 : 4 * TAPS, :] = merge_taps[0 : 4 * TAPS, :]
    correlate(sc, wide, (n,), total, 4 * TAPS, emix.shape[0])
    at = 8 * TAPS
    for ref in (g4, gi):
        for c in range(ref.shape[1] // LANES):
            total[at : at + 1, :] = ref[0:1, c * LANES : (c + 1) * LANES]
            at += 1
    total[at:, :] = jnp.zeros((total.shape[0] - at, LANES), F32)
    small_o[...] = total[...].astype(BF16)


def tiles(rows, size=512):
    size = min(size, rows)
    return [slice(i, i + size) for i in range(0, rows, size)]


def pre_kernel(*refs):
    hbm, refs = refs[:12], refs[12:]
    sc, x1_o, a1_o, h_o, d_o, a2_o, q_o, kv_o, kvs_o = refs[:9]
    bb, vl, ts, tw, fs, fw, gains, freq, feat, w1, w2, wq, sems = refs[9:]
    loads = [
        pltpu.make_async_copy(src, dst, sems.at[i])
        for i, (src, dst) in enumerate(zip(hbm, (bb, vl, ts, tw, fs, fw, gains, freq, feat, w1, w2, wq)))
    ]
    for load in loads:
        load.start()
    for load in loads[:8]:
        load.wait()
    sc[0] = bb[0]
    sc[1] = lax.axis_index("blk")
    for i in range(2):
        sc[2 + i] = vl[0, i]
        sc[4 + i] = ts[0, i]
        sc[6 + i] = ts[0, i] + tw[0, i]
        sc[8 + i] = fs[0, i]
        sc[10 + i] = fs[0, i] + fw[0, i]
    for i in range(12, 16):
        sc[i] = 0
    loads = loads[8:]
    rows = feat.shape[0]
    cos, sin = turn_tables(sc, freq[...], rows)
    parts = tiles(rows)
    for i, t in enumerate(parts):
        shape = (t.stop - t.start, 256)
        if i == 0:
            loads[0].wait()
        x = jnp.where(keep_mask(sc, t.start, shape), feat[t, :].astype(F32), 0.0)
        m, _ = unit(x)
        a1 = (m * gains[0:1, :]).astype(BF16)
        a1_o[t, :] = a1
        if i == 0:
            loads[1].wait()
        h, d = silu_parts(mm(a1, w1[...]))
        h = h.astype(BF16)
        h_o[t, :] = h
        d_o[t, :] = d.astype(BF16)
        if i == 0:
            loads[2].wait()
        x1 = x + 0.5 * mm(h, w2[...])
        x1_o[t, :] = x1
        m, _ = unit(x1)
        a2 = (m * gains[1:2, :]).astype(BF16)
        a2_o[t, :] = a2
        if i == 0:
            loads[3].wait()
        qkv = mm(a2, wq[...])
        q_o[t, :] = rotate(qkv[:, 0:256], cos[t], sin[t], 1.0).astype(BF16)
        k = rotate(qkv[:, 256:512], cos[t], sin[t], 1.0).astype(BF16)
        v = qkv[:, 512:768].astype(BF16)
        for o in (kv_o, kvs_o):
            o[t, 0:256] = k
            o[t, 256:512] = v


def gate_kernel(sc, x1, gains, inner, up, a3_o, rest_o, slope_o, n_o, mg_o, rs_o, ea_o, eb_o):
    rows = x1.shape[0]
    for t in tiles(rows):
        m, _ = unit(x1[t, :])
        a3 = (m * gains[2:3, :]).astype(BF16)
        a3_o[t, :] = a3
        y, slope = gelu_parts(mm(a3, up[...]))
        slope_o[t, :] = slope.astype(BF16)
        rest_o[t, :] = y[:, 0:512]
        mg, rs = unit(y[:, 512:1024])
        mg_o[t, :] = mg
        rs_o[t, :] = rs
        n_o[t, :] = (mg * inner[...]).astype(BF16)
    edge_sends(sc, n_o, ea_o.at[HALO:], eb_o.at[HALO:])
    edge_sends(sc, rest_o, ea_o.at[0:HALO], eb_o.at[0:HALO])


def mixed_kernel(sc, plane, ha, hb, rest, taps, down, mixed_o, gated_o, cat_o, rim):
    rows = plane.shape[0]
    add_edges(sc, rim, taps, ha, hb, (UPPER, UPPER), plane, mixed_o, 1)
    for t in tiles(rows):
        gated = (rest[t, :] * mixed_o[t, :]).astype(BF16)
        gated_o[t, :] = gated
        cat_o[t, :] = mm(gated, down[...]).astype(BF16)


def head_masks(rows):
    lane = lax.broadcasted_iota(jnp.int32, (rows, LANES), 1)
    return lane


def query_aug(sc, q, h, lane, utt):
    half = h % 2
    pair = q[:, (h // 2) * LANES : (h // 2 + 1) * LANES].astype(F32)
    off = HEAD_DIM * (1 - half)
    flags = jnp.where((lane == off + utt), 1.0, 0.0)
    mine = (lane >> 6) == half
    return jnp.where(mine, pair, flags).astype(BF16), jnp.where(mine, pair, 0.0).astype(BF16)


def key_bias(sc, src, lane, rows):
    row = lax.broadcasted_iota(jnp.int32, (rows, LANES), 0)
    shift = sc[0] - 1
    utt = row & shift
    pos = (row >> shift) + src * (rows >> shift)
    ok = pos < jnp.where(utt == 0, sc[2], sc[3])
    col = lane & 63
    seen = ok & (col == utt)
    return jnp.where((col < 2) & jnp.logical_not(seen), HIDE, 0.0)


def key_aug(kv, h, lane, bias):
    half = h % 2
    pair = kv[:, (h // 2) * LANES : (h // 2 + 1) * LANES].astype(F32)
    mine = (lane >> 6) == half
    return jnp.where(mine, pair, bias).astype(BF16)


def att_kernel(first, final, masks, sc, q, *rest):
    kvs, rest = rest[: len(masks)], rest[len(masks) :]
    if not first:
        c_i, l_i, acc_i = rest[:3]
        rest = rest[3:]
    if final:
        catg, out_w, c_o, l_o, *blocks, oT_o, ob_o, att_o, ea_o, eb_o, acc_o = rest
    else:
        c_o, l_o, *blocks, acc_o = rest
    if first:
        qm_o, blocks = blocks[0], blocks[1:]
    rows = q.shape[0]
    lane = lax.broadcasted_iota(jnp.int32, (rows, LANES), 1)
    utt = lax.broadcasted_iota(jnp.int32, (rows, LANES), 0) & (sc[0] - 1)
    qs = []
    for h in range(HEADS):
        with_flags, alone = query_aug(sc, q, h, lane, utt)
        qs.append(with_flags)
        if first:
            qm_o[h * rows : (h + 1) * rows, :] = alone
    if first:
        c_o[...] = jnp.full((8, rows), -1e30, F32)
        l_o[...] = jnp.zeros((8, rows), F32)
        acc_o[...] = jnp.zeros((HEADS * HEAD_DIM, rows), F32)
    else:
        c_o[...] = c_i[...]
        l_o[...] = l_i[...]
        acc_o[...] = acc_i[...]
    for mask, kv, w_o, top_o in zip(masks, kvs, blocks[0::2], blocks[1::2]):
        bias = key_bias(sc, sc[1] ^ mask, lane, rows)
        vT = kv[:, 256:512].astype(F32).T.astype(BF16)
        ahead = mm_nt(key_aug(kv, 0, lane, bias), qs[0])
        for h in range(HEADS):
            s = ahead
            if h + 1 < HEADS:
                ahead = mm_nt(key_aug(kv, h + 1, lane, bias), qs[h + 1])
            old = c_o[h : h + 1, :]
            new = jnp.maximum(old, jnp.floor(jnp.max(s, 0, keepdims=True) * EXP_SCALE))
            scale = jnp.exp2(old - new)
            c_o[h : h + 1, :] = new
            total = l_o[h : h + 1, :] * scale
            for r in tiles(rows, 256):
                w = jnp.exp2(s[r] * EXP_SCALE - new)
                w_o[h * rows + r.start : h * rows + r.stop, :] = w.astype(BF16)
                total = total + jnp.sum(w, 0, keepdims=True)
            l_o[h : h + 1, :] = total
            hr = slice(h * HEAD_DIM, (h + 1) * HEAD_DIM)
            acc_o[hr, :] = acc_o[hr, :] * scale + mm(vT[hr, :], w_o[h * rows : (h + 1) * rows, :])
        top_o[...] = c_o[...]
    if final:
        for h in range(HEADS):
            hr = slice(h * HEAD_DIM, (h + 1) * HEAD_DIM)
            oT_o[hr, :] = acc_o[hr, :] / l_o[h : h + 1, :]
        ob = oT_o[...].T.astype(BF16)
        ob_o[...] = ob
        att_o[...] = mm(ob, out_w[...]).astype(BF16)
        edge_sends(sc, (att_o, catg), ea_o, eb_o)


def merge_kernel(
    sc, plane_i, att, catg, ha, hb, x1, taps, mw, dout, gains, w1, w2,
    out_o, un_o, em_o, ec_o, df_o, g2_o, a4_o, h_o, e2_o, du_o, g4_o, ea_o, eb_o, rim, plane,
):
    rows = att.shape[0]
    add_edges(sc, rim, taps, ha, hb, (LOWER, LOWER), plane_i, plane, 1)
    g4g = jnp.zeros((1, 256), F32)
    for t in tiles(rows):
        cat = jnp.concatenate([att[t, :], catg[t, :]], 1).astype(F32)
        united = (cat + plane[t, :]).astype(BF16)
        un_o[t, :] = united
        x2 = x1[t, :] + mm(united, mw[...])
        m2, rs2 = unit(x2)
        a4 = (m2 * gains[3:4, :]).astype(BF16)
        a4_o[t, :] = a4
        h, d = silu_parts(mm(a4, w1[...]))
        h = h.astype(BF16)
        h_o[t, :] = h
        x3 = x2 + 0.5 * mm(h, w2[...])
        m3, rs3 = unit(x3)
        out_o[t, :] = (m3 * gains[4:5, :]).astype(BF16)
        g3 = unit_back(dout[t, :], m3, rs3, gains[4:5, :])
        g4g = g4g + jnp.sum(dout[t, :] * m3, 0, keepdims=True)
        e2 = (0.5 * g3).astype(BF16)
        e2_o[t, :] = e2
        du = (mm_nt(e2, w2[...]) * d).astype(BF16)
        du_o[t, :] = du
        g2 = g3 + unit_back(mm_nt(du, w1[...]), m2, rs2, gains[3:4, :])
        g2_o[t, :] = g2
        em = g2.astype(BF16)
        em_o[t, :] = em
        df = mm_nt(em, mw[...])
        df_o[t, :] = df
        ec_o[t, :] = df.astype(BF16)
    g4_o[...] = jnp.broadcast_to(g4g, (8, 256))
    edge_sends(sc, ec_o, ea_o, eb_o)


def put_cols(buf, row, value):
    n = value.shape[0]
    for c in range(value.shape[1] // LANES):
        buf[row + c * n : row + (c + 1) * n, :] = value[:, c * LANES : (c + 1) * LANES].astype(BF16)


def grads_kernel(a4, h, e2, du, un, em, buf):
    put_cols(buf, 0, mm_tn(a4[...], du[...]))
    put_cols(buf, 2048, mm_tn(h[...], e2[...]))
    put_cols(buf, 4096, mm_tn(un[...], em[...]))


def split_kernel(
    sc, plane_i, ec, ha, hb, na, nb, rest, mixed, oT, l, taps, down, out_w,
    eatt_o, ecg_o, emix_o, dm_o, eaT_o, del_o, mb_o, ma_o, rim, plane,
):
    rows = plane_i.shape[0]
    add_edges(sc, rim, taps, ha, hb, (UPPER, LOWER), plane_i, plane, -1)
    for t in tiles(rows):
        eatt_o[t, :] = plane[t, 0:256].astype(BF16)
        ecg = plane[t, 256:512].astype(BF16)
        ecg_o[t, :] = ecg
        dg = mm_nt(ecg, down[...])
        emix_o[t, :] = (dg * rest[t, :]).astype(BF16)
        dm_o[t, :] = dg * mixed[t, :]
    every = slice(0, 2 * HALO)
    outside = []
    for c in range(2):
        cols = slice((c + 2) * LANES, (c + 3) * LANES)
        before, after = sides(sc, ha, hb, cols, every, every)
        rim[c, 0 : 2 * HALO, :] = before
        rim[c, 2 * HALO : 3 * HALO, :] = ec[0:HALO, cols].astype(F32)
        rim[c, 3 * HALO : 4 * HALO, :] = ec[rows - HALO : rows, cols].astype(F32)
        rim[c, 4 * HALO : 6 * HALO, :] = after
        parts = []
        for base in (0, 3 * HALO):
            acc = rim[c, base + HALO : base + 2 * HALO, :]
            for k in range(TAPS):
                tap = taps[k : k + 1, cols].astype(F32)
                acc = acc + rim[c, pl.ds(base + HALO - sc[0] * (k - TAPS // 2), HALO), :] * tap
            parts.append(acc)
        outside.append(jnp.concatenate(parts, 0))
    dg = mm_nt(jnp.concatenate(outside, 1).astype(BF16), down[...])
    before, after = sides(sc, na, nb, slice(None), LOWER, LOWER)
    mb_o[...] = (dg[0:HALO, :] * before).astype(BF16)
    ma_o[...] = (dg[HALO : 2 * HALO, :] * after).astype(BF16)
    doT = mm_nt(out_w[...], eatt_o[...])
    del_o[...] = jnp.zeros((8, rows), F32)
    for h in range(HEADS):
        hr = slice(h * HEAD_DIM, (h + 1) * HEAD_DIM)
        inv = 1.0 / l[h : h + 1, :]
        eaT = (doT[hr, :] * inv).astype(BF16)
        eaT_o[hr, :] = eaT
        del_o[h : h + 1, :] = jnp.sum(doT[hr, :] * oT[hr, :], 0, keepdims=True) * inv


def attback_kernel(first, kv, w, top, qm, c, eaT, delta, *rest):
    if first:
        dq_i = None
    else:
        dq_i, rest = rest[0], rest[1:]
    dq_o, d_o = rest
    rows = kv.shape[0]
    lane = lax.broadcasted_iota(jnp.int32, (rows, LANES), 1)
    nothing = jnp.zeros((HEAD_DIM, rows), BF16)
    kT = kv[:, 0:256].astype(F32).T.astype(BF16)
    for pair in range(HEADS // 2):
        cols = slice(pair * LANES, (pair + 1) * LANES)
        vcols = slice(256 + pair * LANES, 256 + (pair + 1) * LANES)
        scales = [jnp.exp2(top[h : h + 1, :] - c[h : h + 1, :]) for h in (2 * pair, 2 * pair + 1)]
        heads = [slice(h * HEAD_DIM, (h + 1) * HEAD_DIM) for h in (2 * pair, 2 * pair + 1)]
        grown = jnp.concatenate([eaT[hr, :].astype(F32) * r for hr, r in zip(heads, scales)], 0)
        ea = grown.T
        dk = jnp.zeros((rows, LANES), F32)
        dv = jnp.zeros((rows, LANES), F32)
        for half in range(2):
            h = pair * 2 + half
            hr = heads[half]
            here = slice(h * rows, (h + 1) * rows)
            mine = grown[half * HEAD_DIM : (half + 1) * HEAD_DIM, :].astype(BF16)
            dp = mm(kv[:, vcols], jnp.concatenate([mine, nothing] if half == 0 else [nothing, mine], 0))
            low = w[here, :]
            ds = (low.astype(F32) * (dp - delta[h : h + 1, :] * scales[half])).astype(BF16)
            dk = dk + mm(ds, qm[here, :])
            dv = dv + mm(low, jnp.where((lane >> 6) == half, ea, 0.0).astype(BF16))
            part = mm(kT[hr, :], ds)
            dq_o[hr, :] = part if first else dq_i[hr, :] + part
        d_o[:, cols] = (dk * SCORE_SCALE).astype(d_o.dtype)
        d_o[:, vcols] = dv.astype(d_o.dtype)


def gateback_kernel(
    sc, emix, ha, hb, mg, rs, dm, slope, a3, x1, gated, ecg, ob, eatt, taps, inner, up, gains,
    bcg_o, gi_o, buf, wide, plane,
):
    rows = emix.shape[0]
    fill_wide(sc, wide, (emix,), ha, hb)
    conv(sc, wide, taps, plane, rows, -1, False)
    gi = jnp.zeros((1, 512), F32)
    ups = []
    for t in tiles(rows):
        up_n = plane[t, :]
        dgate = unit_back(up_n, mg[t, :], rs[t, :], inner[...])
        gi = gi + jnp.sum(up_n * mg[t, :], 0, keepdims=True)
        sl = slope[t, :].astype(F32)
        eup = jnp.concatenate([dm[t, :] * sl[:, 0:512], dgate * sl[:, 512:1024]], 1).astype(BF16)
        ups.append(eup)
        m, rs1 = unit(x1[t, :])
        bcg_o[t, :] = unit_back(mm_nt(eup, up[...]), m, rs1, gains[2:3, :])
    gi_o[...] = jnp.broadcast_to(gi, (8, 512))
    eup = jnp.concatenate(ups, 0)
    put_cols(buf, 0, mm_tn(a3[...], eup))
    put_cols(buf, 2048, mm_tn(gated[...], ecg[...]))
    put_cols(buf, 3072, mm_tn(ob[...], eatt[...]))


def last_kernel(
    sc, dqT, dkv0, dkv1, dkv2, a2, x1, g2, bcg, a1, h, d, freq, wq, gains, w2, g1_o, du_o, buf,
):
    rows = x1.shape[0]
    cos, sin = turn_tables(sc, freq[...], rows)
    dq = dqT[...].T * SCORE_SCALE
    eqkvs, e1s = [], []
    for t in tiles(rows):
        dkv = dkv0[t, :] + dkv1[t, :].astype(F32) + dkv2[t, :].astype(F32)
        eq = rotate(dq[t], cos[t], sin[t], -1.0).astype(BF16)
        ek = rotate(dkv[:, 0:256], cos[t], sin[t], -1.0).astype(BF16)
        eqkv = jnp.concatenate([eq, ek, dkv[:, 256:512].astype(BF16)], 1)
        eqkvs.append(eqkv)
        m, rs = unit(x1[t, :])
        g1 = g2[t, :] + unit_back(mm_nt(eqkv, wq[...]), m, rs, gains[1:2, :]) + bcg[t, :]
        g1_o[t, :] = g1
        e1 = (0.5 * g1).astype(BF16)
        e1s.append(e1)
        du_o[t, :] = (mm_nt(e1, w2[...]) * d[t, :].astype(F32)).astype(BF16)
    put_cols(buf, 0, mm_tn(a1[...], du_o[...]))
    put_cols(buf, 2048, mm_tn(h[...], jnp.concatenate(e1s, 0)))
    put_cols(buf, 4096, mm_tn(a2[...], jnp.concatenate(eqkvs, 0)))


def input_kernel(sc, du, g1, gains, feat, w1, dx_o):
    rows = du.shape[0]
    for t in tiles(rows):
        keep = keep_mask(sc, t.start, (t.stop - t.start, 256))
        m, rs = unit(jnp.where(keep, feat[t, :].astype(F32), 0.0))
        back = unit_back(mm_nt(du[t, :], w1[...]), m, rs, gains[0:1, :])
        dx_o[t, :] = jnp.where(keep, g1[t, :] + back, 0.0)


def join_kernel(left, right, out):
    rows = right.shape[0]
    out[0:rows, :] = (left[0:rows, :].astype(F32) + right[...].astype(F32)).astype(BF16)
    if out.shape[0] > rows:
        out[rows:, :] = jnp.zeros((out.shape[0] - rows, out.shape[1]), BF16)


def rank():
    return lax.axis_index("grp") * lax.axis_size("blk") + lax.axis_index("blk")


def overlaps(sizes, low, high):
    start = 0
    for i, n in enumerate(sizes):
        a, b = max(start, low), min(start + n, high)
        if a < b:
            yield i, a - start, a - low, b - a
        start += n


def pack_kernel(sources, *refs):
    parts, keep, sends = refs[:sources], refs[sources], refs[sources + 1 :]
    half = keep.shape[0]
    bit = rank() % 2
    sizes = [ref.shape[0] for ref in parts]
    for own in range(2):

        @pl.when(bit == own)
        def _():
            for i, at, to, n in overlaps(sizes, own * half, (own + 1) * half):
                keep[to : to + n, :] = parts[i][at : at + n, :]
            start = (1 - own) * half
            for send in sends:
                for i, at, to, n in overlaps(sizes, start, start + send.shape[0]):
                    send[to : to + n, :] = parts[i][at : at + n, :]
                start += send.shape[0]


def fold_pieces_kernel(pair, mine, *refs):
    gots, keep, send = refs[:-2], refs[-2], refs[-1]
    half = keep.shape[0]
    bit = slot_bit(pair)
    sizes = [ref.shape[0] for ref in gots]
    for own in range(2):

        @pl.when(bit == own)
        def _():
            for ref, b in ((send, 1 - own), (keep, own)):
                for i, at, to, n in overlaps(sizes, b * half, (b + 1) * half):
                    value = mine[b * half + to : b * half + to + n, :].astype(F32) + gots[i][at : at + n, :].astype(F32)
                    ref[to : to + n, :] = value.astype(BF16)


def pieces_of(rows, count):
    step = -(-rows // (16 * count)) * 16
    return [min(step, rows - i * step) for i in range(count)]


def slot_bit(pair):
    index = rank()
    mask = jnp.where(index % 2 == 0, pair[0], pair[1])
    return (index // mask) % 2


def fold_kernel(pair, alone, *refs):
    if pair is None:
        mine, got, out = refs
        out[...] = (mine[...].astype(F32) + got[...].astype(F32)).astype(BF16)
        return
    *ins, keep, send = refs
    bit = slot_bit(pair)
    at = 0
    sources = list(zip(ins[0 : len(ins) - alone : 2], ins[1 : len(ins) - alone : 2]))
    for pieces in sources + [(ref,) for ref in ins[len(ins) - alone :]]:
        half = pieces[0].shape[0] // 2
        for ref, b in ((send, 1 - bit), (keep, bit)):
            here = pl.ds(pl.multiple_of(b * half, 16), half)
            value = pieces[0][here, :]
            if len(pieces) > 1:
                value = (value.astype(F32) + pieces[1][here, :].astype(F32)).astype(BF16)
            ref[at : at + half, :] = value
        at += half


def grow_into(bit, segments, mine, got, out):
    at = to = 0
    for n in segments:
        piece = slice(at, at + n)
        out[pl.ds(pl.multiple_of(to + bit * n, 16), n), :] = mine[piece, :]
        out[pl.ds(pl.multiple_of(to + (1 - bit) * n, 16), n), :] = got[piece, :]
        at += n
        to += 2 * n
    if at < mine.shape[0]:
        value = mine[at:, :].astype(F32) + got[at:, :].astype(F32)
        out[to : to + mine.shape[0] - at, :] = value.astype(BF16)


def grow_kernel(pair, segments, mine, got, out):
    grow_into(slot_bit(pair), segments, mine, got, out)


def quarter_pieces(layout, sizes, j, i, low, high):
    base = at = 0
    for n in sizes:
        start = base + j * (n // 2) + i * (n // 4)
        a, b = max(low, at), min(high, at + n // 4)
        if a < b:
            first, last = start + a - at, start + b - at
            for out, (row, count, cols) in enumerate(layout):
                if row is None or row >= sum(sizes):
                    continue
                for c in range(cols // LANES):
                    top = row + c * count
                    x, y = max(first, top), min(last, top + count)
                    if x < y:
                        yield out, a - low + x - first, x - top, y - x, c
        base += n
        at += n // 4


GAIN_OF = {2: (0, 0, 8), 4: (1, 8, 6), 6: (2, 14, 8), 11: (3, 22, 8)}
GAIN_ROWS = 30 * 256


def write_rows(layout, pieces, src, outs, bufs, sems, sums, weights, meanwhile=None):
    copies = []
    for i in range(len(layout)):
        mine = [p for p in pieces if p[0] == i]
        for _, at, to, n, c in mine:
            cols = slice(c * LANES, (c + 1) * LANES)
            value = src[at : at + n, :].astype(F32)
            bufs[i][to : to + n, cols] = value
            if i in GAIN_OF:
                g, block, _ = GAIN_OF[i]
                top = (block + c) * 256 + to
                sums[top : top + n, :] = value * weights[g][to : to + n, cols].astype(F32)
        if len(mine) * LANES == layout[i][2] and all(p[3] == layout[i][1] for p in mine):
            spots = [(slice(None), slice(None))]
        else:
            spots = [(slice(to, to + n), slice(c * LANES, (c + 1) * LANES)) for _, at, to, n, c in mine]
        for here in spots:
            copies.append(pltpu.make_async_copy(bufs[i].at[here], outs[i].at[here], sems.at[len(copies)]))
            copies[-1].start()
    if meanwhile is not None:
        copies += meanwhile()
    for copy in copies:
        copy.wait()


def each_quarter(slot, other, body):
    index = rank()
    if other:
        index = index ^ 1
    half = index % 2
    quarter = (index // jnp.where(half == 0, slot[0], slot[1])) % 2
    for j in range(2):
        for i in range(2):
            pl.when((half == j) & (quarter == i))(functools.partial(body, j, i))


def unpack_kernel(layout, sizes, slot, spans, first, *refs):
    count, parts = len(layout), len(spans)
    srcs, weights, refs = refs[:parts], refs[parts : parts + 4], refs[parts + 4 :]
    if not first:
        refs = refs[1 + count :]
    sums, outs, refs = refs[0], refs[1 : count + 1], refs[count + 1 :]
    bufs, sems = refs[:count], refs[count]
    for src, (other, flip, low, high) in zip(srcs, spans):

        def body(j, i, src=src, flip=flip, low=low, high=high):
            pieces = list(quarter_pieces(layout, sizes, j, i ^ flip, low, high))
            write_rows(layout, pieces, src, outs, bufs, sems, sums, weights)

        each_quarter(slot, other, body)


def unpack_last_kernel(layout, sizes, slot, span, rest, src, q, b, mate_q, gains, *refs):
    count = len(layout)
    weights, refs = refs[:4], refs[5 + count :]
    sums, outs, refs = refs[0], refs[1 : count + 1], refs[count + 1 :]
    bufs, small, sems, tail_sems = refs[:count], *refs[count:]

    def end(ref):
        return ref[ref.shape[0] - rest :, :].astype(F32)

    own, mate = end(q) + end(b), end(mate_q) + end(src)
    small[...] = own + mate
    late = []

    def send(i):
        late.append(pltpu.make_async_copy(bufs[i], outs[i], tail_sems.at[len(late)]))
        late[-1].start()

    for i, (row, n, cols) in enumerate(layout):
        if row is not None and row >= sum(sizes):
            for c in range(cols // LANES):
                start = row - sum(sizes) + c * n
                bufs[i][:, c * LANES : (c + 1) * LANES] = small[start : start + n, :]
            send(i)
    for c in range(2):
        start = 8 * TAPS + c
        bufs[0][4:5, c * LANES : (c + 1) * LANES] = small[start : start + 1, :]

    def write_gains():
        totals = []
        for _, block, many in GAIN_OF.values():
            total = sums[block * 256 : (block + 1) * 256, :]
            for c in range(1, many):
                total = total + sums[(block + c) * 256 : (block + c + 1) * 256, :]
            totals.append(total)
        line = lax.dot_general(
            jnp.ones((8, LANES), F32), jnp.concatenate(totals, 0), (((1,), (1,)), ((), ())),
            precision=lax.Precision.HIGHEST, preferred_element_type=F32,
        )
        for g in range(4):
            bufs[0][g : g + 1, :] = line[0:1, g * 256 : (g + 1) * 256] / gains[g : g + 1, :]
        copy = pltpu.make_async_copy(bufs[0], outs[0], sems.at[sems.shape[0] - 1])
        copy.start()
        return [copy]

    def body(j, i):
        pieces = list(quarter_pieces(layout, sizes, j, i ^ 1, span[2], span[3]))
        write_rows(layout, pieces, src, outs, bufs, sems, sums, weights, write_gains)

    each_quarter(slot, True, body)
    for copy in late:
        copy.wait()


def small_call(kernel, outs, ins, us, scratch=(), limit=None, out_space=None):
    vmem = pl.BlockSpec(memory_space=pltpu.VMEM)
    return pl.pallas_call(
        kernel,
        out_shape=[jax.ShapeDtypeStruct(s, d) for s, d in outs],
        in_specs=[vmem] * len(ins),
        out_specs=[vmem if out_space is None else pl.BlockSpec(memory_space=out_space)] * len(outs),
        scratch_shapes=list(scratch),
        compiler_params=pltpu.CompilerParams(vmem_limit_bytes=limit or VMEM_BYTES),
        cost_estimate=pl.CostEstimate(flops=int(us * UNIT), bytes_accessed=1, transcendentals=0),
    )(*ins)


def exchange(value, pair):
    count = lax.axis_size("grp") * lax.axis_size("blk")
    return lax.ppermute(value, AXES, [(i, i ^ pair[i % 2]) for i in range(count)])


def slot_pairs():
    count = lax.axis_size("grp") * lax.axis_size("blk")
    masks = [1 << i for i in range(1, count.bit_length() - 1)]
    first = list(masks)
    second = list(masks)
    if len(masks) > 3:
        first = [masks[1], masks[0]] + masks[2:]
        second = masks[2:4] + masks[0:2] + masks[4:]
    return list(zip(first, second))


def fold(pair, *ins, alone=0):
    paired = ins[: len(ins) - alone]
    rows = sum(v.shape[0] for v in paired[0::2]) // 2 + sum(v.shape[0] for v in ins[len(paired) :]) // 2
    outs = [((rows, LANES), BF16)] * 2
    return small_call(functools.partial(fold_kernel, pair, alone), outs, ins, 0.5)


def grow_cut_kernel(pair, segments, mine, got, out, low, high, near, end):
    grow_into(slot_bit(pair), segments, mine, got, out)
    cut, step = low.shape[0], near.shape[0]
    low[...] = out[0:cut, :]
    high[...] = out[cut:, :]
    near[...] = out[cut : cut + step, :]
    end[...] = out[cut + step :, :]


def gather(mine, slots, sizes, rest):
    for i in reversed(range(1, len(slots))):
        got = exchange(mine, slots[i])
        if i > 2:
            segments, rows = (mine.shape[0],), 2 * mine.shape[0]
        elif i == 2:
            segments, rows = tuple(n // 16 for n in sizes) + (rest // 2,), 2 * mine.shape[0]
        else:
            segments, rows = tuple(n // 8 for n in sizes), sum(sizes) // 4 + rest
        shapes = [((rows, LANES), BF16)]
        if i > 1:
            (mine,) = small_call(functools.partial(grow_kernel, slots[i], segments), shapes, [mine, got], 0.4)
            continue
        cut = rows * 5 // 192 * 16
        step = (rows - cut) // 32 * 16
        shapes += [((n, LANES), BF16) for n in (cut, rows - cut, step, rows - cut - step)]
        return small_call(functools.partial(grow_cut_kernel, slots[i], segments), shapes, [mine, got], 0.5)


def unpack(kernel, layout, name, ins, held, scratch, us):
    shapes = [(n, cols) for _, n, cols in layout]
    hbm, vmem = pl.BlockSpec(memory_space=pltpu.HBM), pl.BlockSpec(memory_space=pltpu.VMEM)
    return pl.pallas_call(
        kernel,
        out_shape=[jax.ShapeDtypeStruct(s, F32) for s in [(GAIN_ROWS, LANES)] + shapes],
        in_specs=[vmem] * len(ins) + ([vmem] + [hbm] * len(shapes) if held else []),
        out_specs=[vmem] + [hbm] * len(shapes),
        scratch_shapes=[pltpu.VMEM(s, F32) for s in shapes] + scratch + [pltpu.SemaphoreType.DMA((24,))],
        input_output_aliases={len(ins) + i: i for i in range(len(held))},
        compiler_params=pltpu.CompilerParams(vmem_limit_bytes=32 * 1024 * 1024),
        cost_estimate=pl.CostEstimate(flops=int(us * UNIT), bytes_accessed=1, transcendentals=0),
        name=name,
    )(*ins, *held)


def spread(mine, low, high, near, last, slot, sizes, rest, layout, gains, weights):
    rows, cut, step = mine.shape[0], low.shape[0], near.shape[0]
    end = rows - rest
    got_low, got_high = exchange(low, slot), exchange(high, slot)

    def write(spans, ins, held, name):
        kernel = functools.partial(unpack_kernel, layout, sizes, slot, spans, not held)
        return list(unpack(kernel, layout, name, [*ins, *weights], held, [], 0.3))

    held = write(((False, 0, 0, end),), [mine], [], "unpack_own")
    got_low, low, near, last, held[0] = lax.optimization_barrier((got_low, low, near, last, held[0]))
    mates = [exchange(v, (1, 1)) for v in (low, near, last, got_low)]
    held = write(((False, 1, 0, cut),), [got_low], held, "unpack_low")
    spans = ((True, 0, 0, cut), (True, 0, cut, cut + step), (True, 0, cut + step, end), (True, 1, 0, cut))
    held = write(spans, mates, held, "unpack_mate")
    got_high, held[0] = lax.optimization_barrier((got_high, held[0]))
    mate_high = exchange(got_high, (1, 1))
    held = write(((False, 1, cut, end),), [got_high], held, "unpack_high")
    kernel = functools.partial(unpack_last_kernel, layout, sizes, slot, (True, 1, cut, end), rest)
    scratch = [pltpu.VMEM((rest, LANES), F32), pltpu.SemaphoreType.DMA((24,))]
    ins = [mate_high, mine, got_high, mates[2], gains, *weights]
    return unpack(kernel, layout, "unpack_last", ins, held, scratch, 2.0)[1:]


def plain(kernel, ins, outs, kept, *refs):
    head = refs[: ins]
    made = refs[ins + kept : ins + kept + outs]
    scratch = refs[ins + 2 * kept + outs :]
    kernel(*head, *made, *scratch)


class Layer:
    def __init__(self, plan):
        self.plan = plan
        self.step = 0
        self.have = {}

    def __getitem__(self, key):
        return self.have[key]

    def __setitem__(self, key, value):
        self.have[key] = value

    def run(self, kernel, outs, extra=(), scratch=(), us=1.0):
        name, reads = self.plan[self.step]
        later = [r for _, more in self.plan[self.step + 1 :] for r in more]
        kept = sorted(k for k in self.have if k in later and k not in reads and k != "sc")
        self.step += 1

        def size(key):
            return self.have[key].size * self.have[key].dtype.itemsize

        while sum(map(size, kept)) > CARRY_BYTES:
            kept.remove(max(kept, key=size))
        smem = pl.BlockSpec(memory_space=pltpu.SMEM)
        vmem = pl.BlockSpec(memory_space=pltpu.VMEM)
        ins = [self.have[r] for r in reads] + list(extra)
        in_specs = [smem if r == "sc" else vmem for r in reads] + [vmem] * len(extra)
        shapes = [jax.ShapeDtypeStruct(s, d) for _, s, d in outs]
        shapes += [jax.ShapeDtypeStruct(self.have[k].shape, self.have[k].dtype) for k in kept]
        made = pl.pallas_call(
            functools.partial(plain, kernel, len(ins), len(outs), len(kept)),
            out_shape=shapes,
            in_specs=in_specs + [vmem] * len(kept),
            out_specs=[vmem] * len(shapes),
            scratch_shapes=list(scratch),
            input_output_aliases={len(ins) + i: len(outs) + i for i in range(len(kept))},
            compiler_params=pltpu.CompilerParams(vmem_limit_bytes=VMEM_BYTES),
            cost_estimate=pl.CostEstimate(flops=int(us * UNIT), bytes_accessed=1, transcendentals=0),
            name=name,
        )(*ins, *[self.have[k] for k in kept])
        for key, value in zip([o[0] for o in outs] + kept, made):
            self.have[key] = value


def swap(value, axis, mask):
    count = math.prod(lax.axis_size(a) for a in axis) if isinstance(axis, tuple) else lax.axis_size(axis)
    return lax.ppermute(value, axis, [(i, i ^ mask) for i in range(count)])


def halo(ea, eb):
    count = lax.axis_size("blk")
    near = [(i, i ^ 1) for i in range(count)]
    far = []
    for i in range(1, count - 1, 2):
        far += [(i, i + 1), (i + 1, i)]
    return lax.ppermute(ea, "blk", near), lax.ppermute(eb, "blk", far)


def local(
    features, d_out, bucket_batch, valid_len, time_start, time_width, freq_start, freq_width,
    gains, inner_gain, ffn1_in, ffn1_out, qkv_w, out_w, cg_up, cg_conv, cg_down, merge_conv,
    merge_w, ffn2_in, ffn2_out,
):
    rows, width = features.shape
    half = cg_down.shape[0]
    ff = ffn1_in.shape[1]
    blocks = lax.axis_size("blk")
    me = lax.axis_index("blk")
    freq = np.exp(np.arange(32, dtype=np.float64) * (-2.0 * math.log(10000.0) / HEAD_DIM))
    freq = jnp.asarray(np.tile(freq, 4)[None, :].astype(np.float32))
    wide = pltpu.VMEM((half // LANES, rows + 2 * HALO, LANES), F32)
    plane = pltpu.VMEM((rows, half), F32)
    rim = pltpu.VMEM((half // LANES, 6 * HALO, LANES), F32)
    pairs = [(m, m | 1) for m in range(0, blocks, 2)]
    kvs = [(f"kv{a}", f"kv{b}") for a, b in pairs]
    even = [a for a, _ in pairs[1:]]
    state = ["c", "l", "acc"]
    plan = [("gate", ["sc", "x1"])]
    plan += [("att_first", ["sc", "q", *kvs[0]])]
    plan += [("conv_gate", ["sc", "n"]), ("mixed", ["sc", "plane1", "na", "nb", "rest"])]
    far_masks = [m for a, b in pairs[1:] for m in (a, b)]
    plan += [("att_mid", ["sc", "q", f"kv{m}", *state]) for m in far_masks[:-1]]
    plan += [
        ("att_last", ["sc", "q", f"kv{far_masks[-1]}", *state, "catg"]),
        ("conv_merge", ["sc", "att", "catg"]),
        ("merge", ["sc", "plane2", "att", "catg", "ha", "hb", "x1"]),
        ("grads2", ["a4", "h2", "e2", "du2", "un", "em"]),
        ("conv_back", ["sc", "df", "ec"]),
        ("split", ["sc", "plane3", "ec", "ca", "cb", "na", "nb", "rest", "mixed", "oT", "l"]),
    ]
    back = ["qm", "c", "eaT", "delta"]

    def back_reads(m):
        return [f"kv{m}", f"w{m}", f"top{m}", *back] + ([] if m == even[0] + 1 else ["dqT"])

    for e in even:
        for m in (e + 1, e):
            plan += [("attback", back_reads(m))]
        plan += [("join_kv", [f"pd{e}", f"in{e}"])]
    plan += [
        ("attback", back_reads(1)),
        ("gateback", ["sc", "emix", "mb", "ma", "mg", "rs", "dm", "slope", "a3", "x1", "gated", "ecg", "ob", "eatt"]),
        ("pack_early", ["part1", "buf2"]),
        ("attback", back_reads(0)),
        ("fold_early", ["keep", "got0", "got1", "got2"]),
    ]
    total = f"far{even[0]}"
    for e in even[1:]:
        plan += [("join_far", [total, f"far{e}"])]
        total = f"t{e}"
    plan += [
        ("last", ["sc", "dqT", "own", "near", total, "a2", "x1", "g2", "bcg", "a1", "h1", "d1"]),
        ("pack_late", ["buf3"]),
        ("merge_taps", ["sc", "ec", "ca", "cb", "att", "catg"]),
        ("gate_taps", ["sc", "emix", "mb", "ma", "n", "tm", "g4", "gi"]),
        ("input_grad", ["sc", "du1", "g1"]),
    ]
    run = Layer(plan)
    smem = pl.BlockSpec(memory_space=pltpu.SMEM)
    vmem = pl.BlockSpec(memory_space=pltpu.VMEM)
    raw = (bucket_batch, valid_len, time_start, time_width, freq_start, freq_width, gains, freq,
           features, ffn1_in, ffn1_out, qkv_w)
    def narrow(name, kind=BF16):
        return (name, (rows, width), kind)

    def middle(name, kind=BF16):
        return (name, (rows, half), kind)

    def broad(name, kind=BF16):
        return (name, (rows, ff), kind)

    outs = [narrow("x1", F32), narrow("a1"), broad("h1"), broad("d1"), narrow("a2"), narrow("q"), middle("kv0"), middle("kvs")]
    made = pl.pallas_call(
        pre_kernel,
        out_shape=[jax.ShapeDtypeStruct((16,), jnp.int32)] + [jax.ShapeDtypeStruct(o[1], o[2]) for o in outs],
        in_specs=[pl.BlockSpec(memory_space=pltpu.HBM)] * 12,
        out_specs=[smem] + [vmem] * 8,
        scratch_shapes=[pltpu.SMEM(v.shape, v.dtype) for v in raw[:6]]
        + [pltpu.VMEM(v.shape, v.dtype) for v in raw[6:]] + [pltpu.SemaphoreType.DMA((12,))],
        compiler_params=pltpu.CompilerParams(vmem_limit_bytes=VMEM_BYTES),
        cost_estimate=pl.CostEstimate(flops=int(4.0 * UNIT), bytes_accessed=1, transcendentals=0),
        name="pre",
    )(raw[0], *[pltpu.with_memory_space_constraint(v, pltpu.HBM) for v in raw[1:]])
    for key, value in zip(["sc"] + [o[0] for o in outs], made):
        run[key] = value
    held = {0: run["kvs"]}
    bit = blocks // 2
    while bit > 1:
        held.update({m | bit: swap(held[m], "blk", bit) for m in list(held)})
        bit //= 2
    held[1] = swap(held[0], "blk", 1)

    def send_edges():
        return halo(run["ea"], run["eb"])

    edge = [("ea", (HALO, half), BF16), ("eb", (HALO, half), BF16)]
    edge2 = [("ea", (2 * HALO, half), BF16), ("eb", (2 * HALO, half), BF16)]
    stats = [("c", (8, rows), F32), ("l", (8, rows), F32)]

    def kept(*masks):
        return [o for m in masks for o in ((f"w{m}", (HEADS * rows, rows), BF16), (f"top{m}", (8, rows), F32))]


    run.run(
        gate_kernel,
        [narrow("a3"), middle("rest", F32), broad("slope"), middle("n"), middle("mg", F32), ("rs", (rows, 1), F32)] + edge2,
        [gains, inner_gain[None, :], cg_up], us=2.5,
    )
    edges = send_edges()
    run["kv1"] = held[1]
    run.run(functools.partial(att_kernel, True, False, pairs[0]), stats + [("qm", (HEADS * rows, LANES), BF16)] + kept(*pairs[0]) + [("acc", (width, rows), F32)], us=0.5)
    run.run(functools.partial(local_conv_kernel, 1, False), [middle("plane1", F32)], [cg_conv], [wide], us=0.3)
    run["na"], run["nb"] = edges
    run.run(
        mixed_kernel, [middle("mixed", F32), middle("gated"), narrow("catg")],
        [cg_conv, cg_down], [rim], us=1.5,
    )
    for a, b in pairs[1:]:
        late, _ = lax.optimization_barrier((held[a], run["catg"]))
        run[f"kv{a}"] = late
        mate = swap(late, "blk", 1)
        run.run(
            functools.partial(att_kernel, False, False, (a,)), stats + kept(a) + [("acc", (width, rows), F32)], us=2.8,
        )
        run[f"kv{b}"] = mate
        if b < blocks - 1:
            run.run(
                functools.partial(att_kernel, False, False, (b,)), stats + kept(b) + [("acc", (width, rows), F32)], us=2.8,
            )
    run.run(
        functools.partial(att_kernel, False, True, (blocks - 1,)),
        stats + kept(blocks - 1) + [("oT", (width, rows), F32), narrow("ob"), narrow("att")] + edge,
        [out_w], [pltpu.VMEM((width, rows), F32)], us=3.0,
    )
    edges = send_edges()
    run.run(functools.partial(local_conv_kernel, 1, False), [middle("plane2", F32)], [merge_conv], [wide], us=0.3)
    run["ha"], run["hb"] = edges
    run.run(
        merge_kernel,
        [narrow("out"), middle("un"), narrow("em"), middle("ec"), middle("df", F32), narrow("g2", F32), narrow("a4"),
         broad("h2"), narrow("e2"), broad("du2"), ("g4", (8, width), F32)] + edge2,
        [merge_conv, merge_w, d_out, gains, ffn2_in, ffn2_out], [rim, plane], us=5.5,
    )
    edges = send_edges()
    run.run(grads_kernel, [("part1", (5120, LANES), BF16)], us=0.3)
    run.run(functools.partial(local_conv_kernel, -1, True), [middle("plane3", F32)], [merge_conv], [wide], us=0.3)
    run["ca"], run["cb"] = edges
    run.run(
        split_kernel,
        [narrow("eatt"), narrow("ecg"), middle("emix"), middle("dm", F32), ("eaT", (width, rows), BF16),
         ("delta", (8, rows), F32), ("mb", (HALO, half), BF16), ("ma", (HALO, half), BF16)],
        [merge_conv, cg_down, out_w], [rim, plane], us=2.0,
    )

    tall = ("dqT", (width, rows), F32)
    pair_sum = (rows, 2 * width)
    for e in even:
        for m in (e + 1, e):
            run.run(
                functools.partial(attback_kernel, m == even[0] + 1), [tall, (f"pd{m}", pair_sum, BF16)], us=0.5
            )
            if m & 1:
                arrival = swap(run[f"pd{m}"], "blk", 1)
        run[f"in{e}"] = arrival
        run.run(join_kernel, [(f"s{e}", (rows + 32, 2 * width), BF16)], us=0.2)
    fars = {e: swap(run[f"s{e}"], "blk", e) for e in even}
    run.run(functools.partial(attback_kernel, False), [tall, ("pd1", pair_sum, BF16)], us=0.05)
    near = swap(run["pd1"], "blk", 1)
    run.run(
        gateback_kernel,
        [narrow("bcg", F32), ("gi", (8, half), F32), ("buf2", (3584, LANES), BF16)],
        [cg_conv, inner_gain[None, :], cg_up, gains], [wide, plane], us=0.5,
    )
    count = lax.axis_size("grp") * blocks
    used, late, rest = 8704, 5632, 256
    slots = slot_pairs()
    grain = 16 << (len(slots) - 2)
    sizes = (used + 8 * (-((used + late) // 8 + rest) % grain), late)
    cuts = pieces_of(sizes[0] // 2, 3)
    run.run(
        functools.partial(pack_kernel, 2),
        [("keep", (sizes[0] // 2, LANES), BF16)] + [(f"send{i}", (n, LANES), BF16) for i, n in enumerate(cuts)], us=0.1,
    )
    gots = [exchange(run[f"send{i}"], (1, 1)) for i in range(3)]
    run.run(functools.partial(attback_kernel, False), [tall, ("own", pair_sum, F32)], us=0.5)
    for i in range(3):
        run[f"got{i}"] = gots[i]
    for e in even:
        run[f"far{e}"] = fars[e]
    run["near"] = near
    run.run(
        functools.partial(fold_pieces_kernel, slots[0]),
        [("early", (sizes[0] // 4, LANES), BF16), ("send_early", (sizes[0] // 4, LANES), BF16)], us=0.2,
    )
    early_got = exchange(run["send_early"], slots[0])
    for e in even[1:]:
        run.run(join_kernel, [(f"t{e}", (rows + 32, 2 * width), BF16)], us=0.2)
    run.run(
        last_kernel,
        [narrow("g1", F32), broad("du1"), ("buf3", (5632, LANES), BF16)],
        [freq, qkv_w, gains, ffn1_out], us=0.3,
    )
    quarter = ((sizes[1] // 4, LANES), BF16)
    cuts = pieces_of(sizes[1] // 2, 2)
    run.run(
        functools.partial(pack_kernel, 1),
        [("keep3", (sizes[1] // 2, LANES), BF16)] + [(f"late{i}", (n, LANES), BF16) for i, n in enumerate(cuts)], us=0.1,
    )
    gots = [exchange(run[f"late{i}"], (1, 1)) for i in range(2)]
    gots[0], early_got = lax.optimization_barrier((gots[0], early_got))
    keep3, send3 = small_call(functools.partial(fold_pieces_kernel, slots[0]), [quarter, quarter], [run["keep3"], *gots], 0.3)
    late_got = exchange(send3, slots[0])
    _, early = lax.optimization_barrier((send3, run["early"]))
    early, early_send = fold(slots[1], early, early_got)
    early_got = exchange(early_send, slots[1])
    _, run["ec"] = lax.optimization_barrier((early_send, run["ec"]))
    run.run(merge_taps_kernel, [("tm", (128, LANES), F32)], (), [wide], us=1.0)
    late_got, run["tm"] = lax.optimization_barrier((late_got, run["tm"]))
    keep, send = fold(slots[1], keep3, late_got)
    got = exchange(send, slots[1])
    _, run["gi"] = lax.optimization_barrier((send, run["gi"]))
    run.run(gate_taps_kernel, [("small", (rest, LANES), BF16)], (), [wide, pltpu.VMEM((rest, LANES), F32)], us=1.0)
    keep, send = fold(slots[2], early, early_got, keep, got, run["small"], alone=1)
    got = exchange(send, slots[2])
    for pair in slots[3:]:
        keep, send = fold(pair, keep, got)
        got = exchange(send, pair)
    _, run["g1"] = lax.optimization_barrier((send, run["g1"]))
    run.run(input_kernel, [narrow("dx", F32)], [gains, features, ffn1_in], us=0.3)
    got, run["dx"] = lax.optimization_barrier((got, run["dx"]))
    (mine,) = small_call(functools.partial(fold_kernel, None, 0), [(keep.shape, BF16)], [keep, got], 0.3)
    base = sizes[0]
    tail = base + late
    layout = (
        (None, 5, 256), (tail + 8 * TAPS + 2, 1, 512),
        (base, 256, 1024), (base + 2048, 1024, 256), (base + 4096, 256, 768), (8192, 256, 256),
        (5120, 256, 1024), (tail + 4 * TAPS, TAPS, 512), (7168, 512, 256), (tail, TAPS, 512), (4096, 512, 256),
        (0, 256, 1024), (2048, 1024, 256),
    )
    whole = gather(mine, slots, sizes, rest)
    weights = (ffn1_in, qkv_w, cg_up, ffn2_in)
    sums = spread(*whole, slots[0], sizes, rest, layout, gains, weights)
    return (run["out"], run["dx"], sums[0], sums[1][0], *sums[2:])


def solution(mesh):
    rows = P(("grp", "blk"), None)
    in_specs = (rows, rows, P("grp")) + (P("grp", None),) * 5 + (P(),) * 13
    out_specs = (rows, rows) + (P(),) * 13
    return jax.shard_map(local, mesh=mesh, in_specs=in_specs, out_specs=out_specs, check_vma=False)
```

```python
import functools
import math

import jax
import jax.numpy as jnp
import numpy as np
from jax import lax
from jax.experimental import pallas as pl
from jax.experimental.pallas import tpu as pltpu
from jax.sharding import PartitionSpec as P

HEADS = 4
HEAD_DIM = 64
HALO = 32
LOG_BASE = 1.4426950408889634
EPSILON = 1e-05
SCORE_SCALE = HEAD_DIM ** (-0.5)
EXP_SCALE = SCORE_SCALE * LOG_BASE
HIDE = -(2.0 ** 100)
AXES = ("grp", "blk")
F32 = jnp.float32
BF16 = jnp.bfloat16
LANES = 128
VMEM_BYTES = 16 * 1024 * 1024
UNIT = 0.35e9
CARRY_BYTES = 30 * 1024 * 1024


def mm(left, right):
    return jnp.dot(left, right, preferred_element_type=F32)


def mm_nt(left, right):
    return lax.dot_general(left, right, (((1,), (1,)), ((), ())), preferred_element_type=F32)


def mm_tn(left, right):
    return lax.dot_general(left, right, (((0,), (0,)), ((), ())), preferred_element_type=F32)


def unit(v):
    center = v - jnp.mean(v, -1, keepdims=True)
    rs = lax.rsqrt(jnp.mean(center * center, -1, keepdims=True) + EPSILON)
    return center * rs, rs


def unit_back(up, m, rs, gain):
    eg = up * gain
    return rs * (eg - jnp.mean(eg, -1, keepdims=True) - m * jnp.mean(eg * m, -1, keepdims=True))


def silu_parts(u):
    sig = 0.5 + 0.5 * jnp.tanh(0.5 * u)
    h = u * sig
    return h, sig + h * (1.0 - sig)


def gelu_parts(t):
    root = math.sqrt(2.0 / math.pi)
    t2 = t * t
    th = jnp.tanh(root * t * (1.0 + 0.044715 * t2))
    half = 0.5 + 0.5 * th
    slope = half + 0.5 * root * t * (1.0 - th * th) * (1.0 + 3.0 * 0.044715 * t2)
    return t * half, slope


def rows_of(sc, r0, shape):
    row = lax.broadcasted_iota(jnp.int32, shape, 0) + r0
    shift = sc[0] - 1
    utt = row & shift
    pos = (row >> shift) + sc[1] * (512 >> shift)
    return utt, pos


def keep_mask(sc, r0, shape):
    utt, pos = rows_of(sc, r0, shape)
    ch = lax.broadcasted_iota(jnp.int32, shape, 1)
    first = utt == 0

    def pick(i):
        return jnp.where(first, sc[i], sc[i + 1])

    ok = (pos < pick(2)) & jnp.logical_not((pos >= pick(4)) & (pos < pick(6)))
    ok = ok & jnp.logical_not((ch >= pick(8)) & (ch < pick(10)))
    return ok


def turn_tables(sc, freq, rows):
    shift = sc[0] - 1
    coarse = lax.broadcasted_iota(jnp.int32, (rows // 16, LANES), 0) * 16
    fine = lax.broadcasted_iota(jnp.int32, (16, LANES), 0)
    a = ((coarse >> shift) + sc[1] * (rows >> shift)).astype(F32) * freq
    c = (fine >> shift).astype(F32) * freq
    ca, sa, cc, cs = jnp.cos(a), jnp.sin(a), jnp.cos(c), jnp.sin(c)
    cos = ca[:, None, :] * cc[None] - sa[:, None, :] * cs[None]
    sin = sa[:, None, :] * cc[None] + ca[:, None, :] * cs[None]
    return cos.reshape(rows, LANES), sin.reshape(rows, LANES)


def rotate(v, cos, sin, direction):
    lane = lax.broadcasted_iota(jnp.int32, (v.shape[0], LANES), 1)
    lower = (lane & 63) < 32
    signed = jnp.where(lower, -direction, direction) * sin
    parts = []
    for i in range(v.shape[1] // LANES):
        p = v[:, i * LANES : (i + 1) * LANES]
        other = jnp.where(lower, pltpu.roll(p, LANES - 32, 1), pltpu.roll(p, 32, 1))
        parts.append(p * cos + other * signed)
    return jnp.concatenate(parts, 1)


def edge_sends(sc, refs, a_ref, b_ref):
    odd = (sc[1] & 1) == 1
    col = 0
    count = a_ref.shape[0]
    for ref in refs if isinstance(refs, tuple) else (refs,):
        rows, width = ref.shape
        first = ref[0:count, :].astype(BF16)
        last = ref[rows - count : rows, :].astype(BF16)
        cols = slice(col, col + width)
        col += width

        @pl.when(odd)
        def _():
            a_ref[:, cols] = first
            b_ref[:, cols] = last

        @pl.when(jnp.logical_not(odd))
        def _():
            a_ref[:, cols] = last
            b_ref[:, cols] = first


def sides(sc, ha, hb, cols, before, after):
    odd = (sc[1] & 1) == 1
    first = jnp.where(odd, ha[before, cols].astype(F32), hb[before, cols].astype(F32))
    return first, jnp.where(odd, hb[after, cols].astype(F32), ha[after, cols].astype(F32))


LOWER, UPPER = slice(0, HALO), slice(HALO, 2 * HALO)


def fill_wide(sc, wide, sources, ha, hb, spots=None):
    at = 0
    for z in sources:
        rows, width = z.shape
        for c in range(width // LANES):
            cols = slice(at * LANES, (at + 1) * LANES)
            if spots is None:
                before, after = ha[:, cols].astype(F32), hb[:, cols].astype(F32)
            else:
                before, after = sides(sc, ha, hb, cols, *spots)
            wide[at, 0:HALO, :] = before
            wide[at, HALO : HALO + rows, :] = z[:, c * LANES : (c + 1) * LANES].astype(F32)
            wide[at, HALO + rows : 2 * HALO + rows, :] = after
            at += 1


CONV_ROWS = 256
TAP_ROWS = 128
TAPS = 31


def local_conv_kernel(direction, add, sc, *refs):
    *sources, taps, out, wide = refs
    if add:
        base, sources = sources[0], sources[1:]
        out[...] = base[...]
    rows = out.shape[0]
    at = 0
    for z in sources:
        for c in range(z.shape[1] // LANES):
            wide[at, 0:HALO, :] = jnp.zeros((HALO, LANES), F32)
            wide[at, HALO : HALO + rows, :] = z[:, c * LANES : (c + 1) * LANES].astype(F32)
            wide[at, HALO + rows : 2 * HALO + rows, :] = jnp.zeros((HALO, LANES), F32)
            at += 1
    conv(sc, wide, taps, out, rows, direction, add)


def add_edges(sc, rim, taps, ha, hb, spots, plane, out, direction):
    step = sc[0] * direction
    rows = plane.shape[0]
    for c in range(taps.shape[1] // LANES):
        cols = slice(c * LANES, (c + 1) * LANES)
        before, after = sides(sc, ha, hb, cols, *spots)
        rim[c, 0:HALO, :] = before
        rim[c, HALO : 5 * HALO, :] = jnp.zeros((4 * HALO, LANES), F32)
        rim[c, 5 * HALO : 6 * HALO, :] = after
    if out is not plane:
        out[HALO : rows - HALO, :] = plane[HALO : rows - HALO, :]
    for c in range(taps.shape[1] // LANES):
        cols = slice(c * LANES, (c + 1) * LANES)
        for base, start in ((0, 0), (3 * HALO, rows - HALO)):
            acc = plane[start : start + HALO, cols]
            for k in range(TAPS):
                tap = taps[k : k + 1, cols].astype(F32)
                acc = acc + rim[c, pl.ds(base + HALO + step * (k - TAPS // 2), HALO), :] * tap
            out[start : start + HALO, cols] = acc


def by_batch(sc, body):
    for batch in (1, 2):
        pl.when(sc[0] == batch)(functools.partial(body, batch))


def conv(sc, wide, taps, out, rows, direction, add):
    size = min(CONV_ROWS, rows)

    def run(batch):
        groups = {}
        for k in range(TAPS):
            at = HALO + direction * batch * (k - TAPS // 2)
            groups.setdefault(at % 8, []).append((at // 8 * 8, k))
        chunks = rows // size

        def block(c, carry):
            cols = pl.ds(pl.multiple_of(c * LANES, LANES), LANES)
            ws = [taps[k : k + 1, cols].astype(F32) for k in range(TAPS)]

            def body(i, carry):
                r0 = pl.multiple_of(i * size, size)
                here = pl.ds(r0, size)
                window = wide[c, pl.ds(r0, size + 2 * HALO), :]
                acc = out[here, cols] if add else None
                for shift, members in sorted(groups.items()):
                    n = size + 8 if shift else size
                    part = None
                    for at, k in members:
                        term = window[at : at + n] * ws[k]
                        part = term if part is None else part + term
                    if shift:
                        part = pltpu.roll(part, n - shift, 0)[:size]
                    acc = part if acc is None else acc + part
                out[here, cols] = acc
                return carry

            return lax.fori_loop(0, chunks, body, carry)

        lax.fori_loop(0, taps.shape[1] // LANES, block, 0)

    by_batch(sc, run)


def correlate(sc, wide, sources, out, row, rows):
    size = min(TAP_ROWS, rows)
    chunks = rows // size

    def run(batch):
        done = 0
        for z in sources:
            blocks = z.shape[1] // LANES

            def block(c, carry, z=z, done=done):
                cols = pl.ds(pl.multiple_of(c * LANES, LANES), LANES)

                def body(i, sums):
                    r0 = pl.multiple_of(i * size, size)
                    zc = z[pl.ds(r0, size), cols].astype(F32)
                    window = wide[done + c, pl.ds(r0, size + 2 * HALO), :]
                    padded = jnp.concatenate([zc, jnp.zeros((8, LANES), F32)], 0)
                    turned = {0: zc}
                    new = []
                    for k in range(TAPS):
                        start = HALO - batch * (k - TAPS // 2)
                        shift = start % 8
                        if shift not in turned:
                            turned[shift] = pltpu.roll(padded, shift, 0)
                        factor = turned[shift]
                        n = factor.shape[0]
                        prod = window[start - shift : start - shift + n] * factor
                        new.append(sums[k] + jnp.sum(prod.reshape(n // 8, 8, LANES), 0))
                    return tuple(new)

                zero = tuple(jnp.zeros((8, LANES), F32) for _ in range(TAPS))
                sums = lax.fori_loop(0, chunks, body, zero)
                for k in range(TAPS):
                    out[pl.ds(row + (done + c) * TAPS + k, 1), :] = jnp.sum(sums[k], 0, keepdims=True)
                return carry

            lax.fori_loop(0, blocks, block, 0)
            done += blocks

    by_batch(sc, run)


def merge_taps_kernel(sc, ec, ca, cb, att, catg, out, wide):
    fill_wide(sc, wide, (ec,), ca, cb, (UPPER, LOWER))
    correlate(sc, wide, (att, catg), out, 0, ec.shape[0])


def gate_taps_kernel(sc, emix, before, after, n, merge_taps, g4, gi, small_o, wide, total):
    fill_wide(sc, wide, (emix,), before, after)
    total[0 : 4 * TAPS, :] = merge_taps[0 : 4 * TAPS, :]
    correlate(sc, wide, (n,), total, 4 * TAPS, emix.shape[0])
    at = 8 * TAPS
    for ref in (g4, gi):
        for c in range(ref.shape[1] // LANES):
            total[at : at + 1, :] = ref[0:1, c * LANES : (c + 1) * LANES]
            at += 1
    total[at:, :] = jnp.zeros((total.shape[0] - at, LANES), F32)
    small_o[...] = total[...].astype(BF16)


def tiles(rows, size=512):
    size = min(size, rows)
    return [slice(i, i + size) for i in range(0, rows, size)]


def pre_kernel(*refs):
    hbm, refs = refs[:12], refs[12:]
    sc, x1_o, a1_o, h_o, d_o, a2_o, q_o, kv_o, kvs_o = refs[:9]
    bb, vl, ts, tw, fs, fw, gains, freq, feat, w1, w2, wq, sems = refs[9:]
    loads = [
        pltpu.make_async_copy(src, dst, sems.at[i])
        for i, (src, dst) in enumerate(zip(hbm, (bb, vl, ts, tw, fs, fw, gains, freq, feat, w1, w2, wq)))
    ]
    for load in loads:
        load.start()
    for load in loads[:8]:
        load.wait()
    sc[0] = bb[0]
    sc[1] = lax.axis_index("blk")
    for i in range(2):
        sc[2 + i] = vl[0, i]
        sc[4 + i] = ts[0, i]
        sc[6 + i] = ts[0, i] + tw[0, i]
        sc[8 + i] = fs[0, i]
        sc[10 + i] = fs[0, i] + fw[0, i]
    for i in range(12, 16):
        sc[i] = 0
    loads = loads[8:]
    rows = feat.shape[0]
    cos, sin = turn_tables(sc, freq[...], rows)
    parts = tiles(rows)
    for i, t in enumerate(parts):
        shape = (t.stop - t.start, 256)
        if i == 0:
            loads[0].wait()
        x = jnp.where(keep_mask(sc, t.start, shape), feat[t, :].astype(F32), 0.0)
        m, _ = unit(x)
        a1 = (m * gains[0:1, :]).astype(BF16)
        a1_o[t, :] = a1
        if i == 0:
            loads[1].wait()
        h, d = silu_parts(mm(a1, w1[...]))
        h = h.astype(BF16)
        h_o[t, :] = h
        d_o[t, :] = d.astype(BF16)
        if i == 0:
            loads[2].wait()
        x1 = x + 0.5 * mm(h, w2[...])
        x1_o[t, :] = x1
        m, _ = unit(x1)
        a2 = (m * gains[1:2, :]).astype(BF16)
        a2_o[t, :] = a2
        if i == 0:
            loads[3].wait()
        qkv = mm(a2, wq[...])
        q_o[t, :] = rotate(qkv[:, 0:256], cos[t], sin[t], 1.0).astype(BF16)
        k = rotate(qkv[:, 256:512], cos[t], sin[t], 1.0).astype(BF16)
        v = qkv[:, 512:768].astype(BF16)
        for o in (kv_o, kvs_o):
            o[t, 0:256] = k
            o[t, 256:512] = v


def gate_kernel(sc, x1, gains, inner, up, a3_o, rest_o, slope_o, n_o, mg_o, rs_o, ea_o, eb_o):
    rows = x1.shape[0]
    for t in tiles(rows):
        m, _ = unit(x1[t, :])
        a3 = (m * gains[2:3, :]).astype(BF16)
        a3_o[t, :] = a3
        y, slope = gelu_parts(mm(a3, up[...]))
        slope_o[t, :] = slope.astype(BF16)
        rest_o[t, :] = y[:, 0:512]
        mg, rs = unit(y[:, 512:1024])
        mg_o[t, :] = mg
        rs_o[t, :] = rs
        n_o[t, :] = (mg * inner[...]).astype(BF16)
    edge_sends(sc, n_o, ea_o.at[HALO:], eb_o.at[HALO:])
    edge_sends(sc, rest_o, ea_o.at[0:HALO], eb_o.at[0:HALO])


def mixed_kernel(sc, plane, ha, hb, rest, taps, down, mixed_o, gated_o, cat_o, rim):
    rows = plane.shape[0]
    add_edges(sc, rim, taps, ha, hb, (UPPER, UPPER), plane, mixed_o, 1)
    for t in tiles(rows):
        gated = (rest[t, :] * mixed_o[t, :]).astype(BF16)
        gated_o[t, :] = gated
        cat_o[t, :] = mm(gated, down[...]).astype(BF16)


def head_masks(rows):
    lane = lax.broadcasted_iota(jnp.int32, (rows, LANES), 1)
    return lane


def query_aug(sc, q, h, lane, utt):
    half = h % 2
    pair = q[:, (h // 2) * LANES : (h // 2 + 1) * LANES].astype(F32)
    off = HEAD_DIM * (1 - half)
    flags = jnp.where((lane == off + utt), 1.0, 0.0)
    mine = (lane >> 6) == half
    return jnp.where(mine, pair, flags).astype(BF16), jnp.where(mine, pair, 0.0).astype(BF16)


def key_bias(sc, src, lane, rows):
    row = lax.broadcasted_iota(jnp.int32, (rows, LANES), 0)
    shift = sc[0] - 1
    utt = row & shift
    pos = (row >> shift) + src * (rows >> shift)
    ok = pos < jnp.where(utt == 0, sc[2], sc[3])
    col = lane & 63
    seen = ok & (col == utt)
    return jnp.where((col < 2) & jnp.logical_not(seen), HIDE, 0.0)


def key_aug(kv, h, lane, bias):
    half = h % 2
    pair = kv[:, (h // 2) * LANES : (h // 2 + 1) * LANES].astype(F32)
    mine = (lane >> 6) == half
    return jnp.where(mine, pair, bias).astype(BF16)


def att_kernel(first, final, masks, sc, q, *rest):
    kvs, rest = rest[: len(masks)], rest[len(masks) :]
    if not first:
        c_i, l_i, acc_i = rest[:3]
        rest = rest[3:]
    if final:
        catg, out_w, c_o, l_o, *blocks, oT_o, ob_o, att_o, ea_o, eb_o, acc_o = rest
    else:
        c_o, l_o, *blocks, acc_o = rest
    if first:
        qm_o, blocks = blocks[0], blocks[1:]
    rows = q.shape[0]
    lane = lax.broadcasted_iota(jnp.int32, (rows, LANES), 1)
    utt = lax.broadcasted_iota(jnp.int32, (rows, LANES), 0) & (sc[0] - 1)
    qs = []
    for h in range(HEADS):
        with_flags, alone = query_aug(sc, q, h, lane, utt)
        qs.append(with_flags)
        if first:
            qm_o[h * rows : (h + 1) * rows, :] = alone
    if first:
        c_o[...] = jnp.full((8, rows), -1e30, F32)
        l_o[...] = jnp.zeros((8, rows), F32)
        acc_o[...] = jnp.zeros((HEADS * HEAD_DIM, rows), F32)
    else:
        c_o[...] = c_i[...]
        l_o[...] = l_i[...]
        acc_o[...] = acc_i[...]
    for mask, kv, w_o, top_o in zip(masks, kvs, blocks[0::2], blocks[1::2]):
        bias = key_bias(sc, sc[1] ^ mask, lane, rows)
        vT = kv[:, 256:512].astype(F32).T.astype(BF16)
        ahead = mm_nt(key_aug(kv, 0, lane, bias), qs[0])
        for h in range(HEADS):
            s = ahead
            if h + 1 < HEADS:
                ahead = mm_nt(key_aug(kv, h + 1, lane, bias), qs[h + 1])
            old = c_o[h : h + 1, :]
            new = jnp.maximum(old, jnp.floor(jnp.max(s, 0, keepdims=True) * EXP_SCALE))
            scale = jnp.exp2(old - new)
            c_o[h : h + 1, :] = new
            total = l_o[h : h + 1, :] * scale
            for r in tiles(rows, 256):
                w = jnp.exp2(s[r] * EXP_SCALE - new)
                w_o[h * rows + r.start : h * rows + r.stop, :] = w.astype(BF16)
                total = total + jnp.sum(w, 0, keepdims=True)
            l_o[h : h + 1, :] = total
            hr = slice(h * HEAD_DIM, (h + 1) * HEAD_DIM)
            acc_o[hr, :] = acc_o[hr, :] * scale + mm(vT[hr, :], w_o[h * rows : (h + 1) * rows, :])
        top_o[...] = c_o[...]
    if final:
        for h in range(HEADS):
            hr = slice(h * HEAD_DIM, (h + 1) * HEAD_DIM)
            oT_o[hr, :] = acc_o[hr, :] / l_o[h : h + 1, :]
        ob = oT_o[...].T.astype(BF16)
        ob_o[...] = ob
        att_o[...] = mm(ob, out_w[...]).astype(BF16)
        edge_sends(sc, (att_o, catg), ea_o, eb_o)


def merge_kernel(
    sc, plane_i, att, catg, ha, hb, x1, taps, mw, dout, gains, w1, w2,
    out_o, un_o, em_o, ec_o, df_o, g2_o, a4_o, h_o, e2_o, du_o, g4_o, ea_o, eb_o, rim, plane,
):
    rows = att.shape[0]
    add_edges(sc, rim, taps, ha, hb, (LOWER, LOWER), plane_i, plane, 1)
    g4g = jnp.zeros((1, 256), F32)
    for t in tiles(rows):
        cat = jnp.concatenate([att[t, :], catg[t, :]], 1).astype(F32)
        united = (cat + plane[t, :]).astype(BF16)
        un_o[t, :] = united
        x2 = x1[t, :] + mm(united, mw[...])
        m2, rs2 = unit(x2)
        a4 = (m2 * gains[3:4, :]).astype(BF16)
        a4_o[t, :] = a4
        h, d = silu_parts(mm(a4, w1[...]))
        h = h.astype(BF16)
        h_o[t, :] = h
        x3 = x2 + 0.5 * mm(h, w2[...])
        m3, rs3 = unit(x3)
        out_o[t, :] = (m3 * gains[4:5, :]).astype(BF16)
        g3 = unit_back(dout[t, :], m3, rs3, gains[4:5, :])
        g4g = g4g + jnp.sum(dout[t, :] * m3, 0, keepdims=True)
        e2 = (0.5 * g3).astype(BF16)
        e2_o[t, :] = e2
        du = (mm_nt(e2, w2[...]) * d).astype(BF16)
        du_o[t, :] = du
        g2 = g3 + unit_back(mm_nt(du, w1[...]), m2, rs2, gains[3:4, :])
        g2_o[t, :] = g2
        em = g2.astype(BF16)
        em_o[t, :] = em
        df = mm_nt(em, mw[...])
        df_o[t, :] = df
        ec_o[t, :] = df.astype(BF16)
    g4_o[...] = jnp.broadcast_to(g4g, (8, 256))
    edge_sends(sc, ec_o, ea_o, eb_o)


def put_cols(buf, row, value):
    n = value.shape[0]
    for c in range(value.shape[1] // LANES):
        buf[row + c * n : row + (c + 1) * n, :] = value[:, c * LANES : (c + 1) * LANES].astype(BF16)


def grads_kernel(a4, h, e2, du, un, em, buf):
    put_cols(buf, 0, mm_tn(a4[...], du[...]))
    put_cols(buf, 2048, mm_tn(h[...], e2[...]))
    put_cols(buf, 4096, mm_tn(un[...], em[...]))


def split_kernel(
    sc, plane_i, ec, ha, hb, na, nb, rest, mixed, oT, l, taps, down, out_w,
    eatt_o, ecg_o, emix_o, dm_o, eaT_o, del_o, mb_o, ma_o, rim, plane,
):
    rows = plane_i.shape[0]
    add_edges(sc, rim, taps, ha, hb, (UPPER, LOWER), plane_i, plane, -1)
    for t in tiles(rows):
        eatt_o[t, :] = plane[t, 0:256].astype(BF16)
        ecg = plane[t, 256:512].astype(BF16)
        ecg_o[t, :] = ecg
        dg = mm_nt(ecg, down[...])
        emix_o[t, :] = (dg * rest[t, :]).astype(BF16)
        dm_o[t, :] = dg * mixed[t, :]
    every = slice(0, 2 * HALO)
    outside = []
    for c in range(2):
        cols = slice((c + 2) * LANES, (c + 3) * LANES)
        before, after = sides(sc, ha, hb, cols, every, every)
        rim[c, 0 : 2 * HALO, :] = before
        rim[c, 2 * HALO : 3 * HALO, :] = ec[0:HALO, cols].astype(F32)
        rim[c, 3 * HALO : 4 * HALO, :] = ec[rows - HALO : rows, cols].astype(F32)
        rim[c, 4 * HALO : 6 * HALO, :] = after
        parts = []
        for base in (0, 3 * HALO):
            acc = rim[c, base + HALO : base + 2 * HALO, :]
            for k in range(TAPS):
                tap = taps[k : k + 1, cols].astype(F32)
                acc = acc + rim[c, pl.ds(base + HALO - sc[0] * (k - TAPS // 2), HALO), :] * tap
            parts.append(acc)
        outside.append(jnp.concatenate(parts, 0))
    dg = mm_nt(jnp.concatenate(outside, 1).astype(BF16), down[...])
    before, after = sides(sc, na, nb, slice(None), LOWER, LOWER)
    mb_o[...] = (dg[0:HALO, :] * before).astype(BF16)
    ma_o[...] = (dg[HALO : 2 * HALO, :] * after).astype(BF16)
    doT = mm_nt(out_w[...], eatt_o[...])
    del_o[...] = jnp.zeros((8, rows), F32)
    for h in range(HEADS):
        hr = slice(h * HEAD_DIM, (h + 1) * HEAD_DIM)
        inv = 1.0 / l[h : h + 1, :]
        eaT = (doT[hr, :] * inv).astype(BF16)
        eaT_o[hr, :] = eaT
        del_o[h : h + 1, :] = jnp.sum(doT[hr, :] * oT[hr, :], 0, keepdims=True) * inv


def attback_kernel(first, kv, w, top, qm, c, eaT, delta, *rest):
    if first:
        dq_i = None
    else:
        dq_i, rest = rest[0], rest[1:]
    dq_o, d_o = rest
    rows = kv.shape[0]
    lane = lax.broadcasted_iota(jnp.int32, (rows, LANES), 1)
    nothing = jnp.zeros((HEAD_DIM, rows), BF16)
    kT = kv[:, 0:256].astype(F32).T.astype(BF16)
    for pair in range(HEADS // 2):
        cols = slice(pair * LANES, (pair + 1) * LANES)
        vcols = slice(256 + pair * LANES, 256 + (pair + 1) * LANES)
        scales = [jnp.exp2(top[h : h + 1, :] - c[h : h + 1, :]) for h in (2 * pair, 2 * pair + 1)]
        heads = [slice(h * HEAD_DIM, (h + 1) * HEAD_DIM) for h in (2 * pair, 2 * pair + 1)]
        grown = jnp.concatenate([eaT[hr, :].astype(F32) * r for hr, r in zip(heads, scales)], 0)
        ea = grown.T
        dk = jnp.zeros((rows, LANES), F32)
        dv = jnp.zeros((rows, LANES), F32)
        for half in range(2):
            h = pair * 2 + half
            hr = heads[half]
            here = slice(h * rows, (h + 1) * rows)
            mine = grown[half * HEAD_DIM : (half + 1) * HEAD_DIM, :].astype(BF16)
            dp = mm(kv[:, vcols], jnp.concatenate([mine, nothing] if half == 0 else [nothing, mine], 0))
            low = w[here, :]
            ds = (low.astype(F32) * (dp - delta[h : h + 1, :] * scales[half])).astype(BF16)
            dk = dk + mm(ds, qm[here, :])
            dv = dv + mm(low, jnp.where((lane >> 6) == half, ea, 0.0).astype(BF16))
            part = mm(kT[hr, :], ds)
            dq_o[hr, :] = part if first else dq_i[hr, :] + part
        d_o[:, cols] = (dk * SCORE_SCALE).astype(d_o.dtype)
        d_o[:, vcols] = dv.astype(d_o.dtype)


def gateback_kernel(
    sc, emix, ha, hb, mg, rs, dm, slope, a3, x1, gated, ecg, ob, eatt, taps, inner, up, gains,
    bcg_o, gi_o, buf, wide, plane,
):
    rows = emix.shape[0]
    fill_wide(sc, wide, (emix,), ha, hb)
    conv(sc, wide, taps, plane, rows, -1, False)
    gi = jnp.zeros((1, 512), F32)
    ups = []
    for t in tiles(rows):
        up_n = plane[t, :]
        dgate = unit_back(up_n, mg[t, :], rs[t, :], inner[...])
        gi = gi + jnp.sum(up_n * mg[t, :], 0, keepdims=True)
        sl = slope[t, :].astype(F32)
        eup = jnp.concatenate([dm[t, :] * sl[:, 0:512], dgate * sl[:, 512:1024]], 1).astype(BF16)
        ups.append(eup)
        m, rs1 = unit(x1[t, :])
        bcg_o[t, :] = unit_back(mm_nt(eup, up[...]), m, rs1, gains[2:3, :])
    gi_o[...] = jnp.broadcast_to(gi, (8, 512))
    eup = jnp.concatenate(ups, 0)
    put_cols(buf, 0, mm_tn(a3[...], eup))
    put_cols(buf, 2048, mm_tn(gated[...], ecg[...]))
    put_cols(buf, 3072, mm_tn(ob[...], eatt[...]))


def last_kernel(
    sc, dqT, dkv0, dkv1, dkv2, a2, x1, g2, bcg, a1, h, d, freq, wq, gains, w2, g1_o, du_o, buf,
):
    rows = x1.shape[0]
    cos, sin = turn_tables(sc, freq[...], rows)
    dq = dqT[...].T * SCORE_SCALE
    eqkvs, e1s = [], []
    for t in tiles(rows):
        dkv = dkv0[t, :] + dkv1[t, :].astype(F32) + dkv2[t, :].astype(F32)
        eq = rotate(dq[t], cos[t], sin[t], -1.0).astype(BF16)
        ek = rotate(dkv[:, 0:256], cos[t], sin[t], -1.0).astype(BF16)
        eqkv = jnp.concatenate([eq, ek, dkv[:, 256:512].astype(BF16)], 1)
        eqkvs.append(eqkv)
        m, rs = unit(x1[t, :])
        g1 = g2[t, :] + unit_back(mm_nt(eqkv, wq[...]), m, rs, gains[1:2, :]) + bcg[t, :]
        g1_o[t, :] = g1
        e1 = (0.5 * g1).astype(BF16)
        e1s.append(e1)
        du_o[t, :] = (mm_nt(e1, w2[...]) * d[t, :].astype(F32)).astype(BF16)
    put_cols(buf, 0, mm_tn(a1[...], du_o[...]))
    put_cols(buf, 2048, mm_tn(h[...], jnp.concatenate(e1s, 0)))
    put_cols(buf, 4096, mm_tn(a2[...], jnp.concatenate(eqkvs, 0)))


def input_kernel(sc, du, g1, gains, feat, w1, dx_o):
    rows = du.shape[0]
    for t in tiles(rows):
        keep = keep_mask(sc, t.start, (t.stop - t.start, 256))
        m, rs = unit(jnp.where(keep, feat[t, :].astype(F32), 0.0))
        back = unit_back(mm_nt(du[t, :], w1[...]), m, rs, gains[0:1, :])
        dx_o[t, :] = jnp.where(keep, g1[t, :] + back, 0.0)


def join_kernel(left, right, out):
    rows = right.shape[0]
    out[0:rows, :] = (left[0:rows, :].astype(F32) + right[...].astype(F32)).astype(BF16)
    if out.shape[0] > rows:
        out[rows:, :] = jnp.zeros((out.shape[0] - rows, out.shape[1]), BF16)


def rank():
    return lax.axis_index("grp") * lax.axis_size("blk") + lax.axis_index("blk")


def overlaps(sizes, low, high):
    start = 0
    for i, n in enumerate(sizes):
        a, b = max(start, low), min(start + n, high)
        if a < b:
            yield i, a - start, a - low, b - a
        start += n


def pack_kernel(sources, *refs):
    parts, keep, sends = refs[:sources], refs[sources], refs[sources + 1 :]
    half = keep.shape[0]
    bit = rank() % 2
    sizes = [ref.shape[0] for ref in parts]
    for own in range(2):

        @pl.when(bit == own)
        def _():
            for i, at, to, n in overlaps(sizes, own * half, (own + 1) * half):
                keep[to : to + n, :] = parts[i][at : at + n, :]
            start = (1 - own) * half
            for send in sends:
                for i, at, to, n in overlaps(sizes, start, start + send.shape[0]):
                    send[to : to + n, :] = parts[i][at : at + n, :]
                start += send.shape[0]


def fold_pieces_kernel(pair, mine, *refs):
    gots, keep, send = refs[:-2], refs[-2], refs[-1]
    half = keep.shape[0]
    bit = slot_bit(pair)
    sizes = [ref.shape[0] for ref in gots]
    for own in range(2):

        @pl.when(bit == own)
        def _():
            for ref, b in ((send, 1 - own), (keep, own)):
                for i, at, to, n in overlaps(sizes, b * half, (b + 1) * half):
                    value = mine[b * half + to : b * half + to + n, :].astype(F32) + gots[i][at : at + n, :].astype(F32)
                    ref[to : to + n, :] = value.astype(BF16)


def pieces_of(rows, count):
    step = -(-rows // (16 * count)) * 16
    return [min(step, rows - i * step) for i in range(count)]


def slot_bit(pair):
    index = rank()
    mask = jnp.where(index % 2 == 0, pair[0], pair[1])
    return (index // mask) % 2


def fold_kernel(pair, alone, *refs):
    if pair is None:
        mine, got, out = refs
        out[...] = (mine[...].astype(F32) + got[...].astype(F32)).astype(BF16)
        return
    *ins, keep, send = refs
    bit = slot_bit(pair)
    at = 0
    sources = list(zip(ins[0 : len(ins) - alone : 2], ins[1 : len(ins) - alone : 2]))
    for pieces in sources + [(ref,) for ref in ins[len(ins) - alone :]]:
        half = pieces[0].shape[0] // 2
        for ref, b in ((send, 1 - bit), (keep, bit)):
            here = pl.ds(pl.multiple_of(b * half, 16), half)
            value = pieces[0][here, :]
            if len(pieces) > 1:
                value = (value.astype(F32) + pieces[1][here, :].astype(F32)).astype(BF16)
            ref[at : at + half, :] = value
        at += half


def grow_into(bit, segments, mine, got, out):
    at = to = 0
    for n in segments:
        piece = slice(at, at + n)
        out[pl.ds(pl.multiple_of(to + bit * n, 16), n), :] = mine[piece, :]
        out[pl.ds(pl.multiple_of(to + (1 - bit) * n, 16), n), :] = got[piece, :]
        at += n
        to += 2 * n
    if at < mine.shape[0]:
        value = mine[at:, :].astype(F32) + got[at:, :].astype(F32)
        out[to : to + mine.shape[0] - at, :] = value.astype(BF16)


def grow_kernel(pair, segments, mine, got, out):
    grow_into(slot_bit(pair), segments, mine, got, out)


def quarter_pieces(layout, sizes, j, i, low, high):
    base = at = 0
    for n in sizes:
        start = base + j * (n // 2) + i * (n // 4)
        a, b = max(low, at), min(high, at + n // 4)
        if a < b:
            first, last = start + a - at, start + b - at
            for out, (row, count, cols) in enumerate(layout):
                if row is None or row >= sum(sizes):
                    continue
                for c in range(cols // LANES):
                    top = row + c * count
                    x, y = max(first, top), min(last, top + count)
                    if x < y:
                        yield out, a - low + x - first, x - top, y - x, c
        base += n
        at += n // 4


GAIN_OF = {2: (0, 0, 8), 4: (1, 8, 6), 6: (2, 14, 8), 11: (3, 22, 8)}
GAIN_ROWS = 30 * 256


def write_rows(layout, pieces, src, outs, bufs, sems, sums, weights, meanwhile=None):
    copies = []
    for i in range(len(layout)):
        mine = [p for p in pieces if p[0] == i]
        for _, at, to, n, c in mine:
            cols = slice(c * LANES, (c + 1) * LANES)
            value = src[at : at + n, :].astype(F32)
            bufs[i][to : to + n, cols] = value
            if i in GAIN_OF:
                g, block, _ = GAIN_OF[i]
                top = (block + c) * 256 + to
                sums[top : top + n, :] = value * weights[g][to : to + n, cols].astype(F32)
        if len(mine) * LANES == layout[i][2] and all(p[3] == layout[i][1] for p in mine):
            spots = [(slice(None), slice(None))]
        else:
            spots = [(slice(to, to + n), slice(c * LANES, (c + 1) * LANES)) for _, at, to, n, c in mine]
        for here in spots:
            copies.append(pltpu.make_async_copy(bufs[i].at[here], outs[i].at[here], sems.at[len(copies)]))
            copies[-1].start()
    if meanwhile is not None:
        copies += meanwhile()
    for copy in copies:
        copy.wait()


def each_quarter(slot, other, body):
    index = rank()
    if other:
        index = index ^ 1
    half = index % 2
    quarter = (index // jnp.where(half == 0, slot[0], slot[1])) % 2
    for j in range(2):
        for i in range(2):
            pl.when((half == j) & (quarter == i))(functools.partial(body, j, i))


def unpack_kernel(layout, sizes, slot, spans, first, *refs):
    count, parts = len(layout), len(spans)
    srcs, weights, refs = refs[:parts], refs[parts : parts + 4], refs[parts + 4 :]
    if not first:
        refs = refs[1 + count :]
    sums, outs, refs = refs[0], refs[1 : count + 1], refs[count + 1 :]
    bufs, sems = refs[:count], refs[count]
    for src, (other, flip, low, high) in zip(srcs, spans):

        def body(j, i, src=src, flip=flip, low=low, high=high):
            pieces = list(quarter_pieces(layout, sizes, j, i ^ flip, low, high))
            write_rows(layout, pieces, src, outs, bufs, sems, sums, weights)

        each_quarter(slot, other, body)


def unpack_last_kernel(layout, sizes, slot, span, rest, src, q, b, mate_q, gains, *refs):
    count = len(layout)
    weights, refs = refs[:4], refs[5 + count :]
    sums, outs, refs = refs[0], refs[1 : count + 1], refs[count + 1 :]
    bufs, small, sems, tail_sems = refs[:count], *refs[count:]

    def end(ref):
        return ref[ref.shape[0] - rest :, :].astype(F32)

    own, mate = end(q) + end(b), end(mate_q) + end(src)
    small[...] = own + mate
    late = []

    def send(i):
        late.append(pltpu.make_async_copy(bufs[i], outs[i], tail_sems.at[len(late)]))
        late[-1].start()

    for i, (row, n, cols) in enumerate(layout):
        if row is not None and row >= sum(sizes):
            for c in range(cols // LANES):
                start = row - sum(sizes) + c * n
                bufs[i][:, c * LANES : (c + 1) * LANES] = small[start : start + n, :]
            send(i)
    for c in range(2):
        start = 8 * TAPS + c
        bufs[0][4:5, c * LANES : (c + 1) * LANES] = small[start : start + 1, :]

    def write_gains():
        totals = []
        for _, block, many in GAIN_OF.values():
            total = sums[block * 256 : (block + 1) * 256, :]
            for c in range(1, many):
                total = total + sums[(block + c) * 256 : (block + c + 1) * 256, :]
            totals.append(total)
        line = lax.dot_general(
            jnp.ones((8, LANES), F32), jnp.concatenate(totals, 0), (((1,), (1,)), ((), ())),
            precision=lax.Precision.HIGHEST, preferred_element_type=F32,
        )
        for g in range(4):
            bufs[0][g : g + 1, :] = line[0:1, g * 256 : (g + 1) * 256] / gains[g : g + 1, :]
        copy = pltpu.make_async_copy(bufs[0], outs[0], sems.at[sems.shape[0] - 1])
        copy.start()
        return [copy]

    def body(j, i):
        pieces = list(quarter_pieces(layout, sizes, j, i ^ 1, span[2], span[3]))
        write_rows(layout, pieces, src, outs, bufs, sems, sums, weights, write_gains)

    each_quarter(slot, True, body)
    for copy in late:
        copy.wait()


def small_call(kernel, outs, ins, us, scratch=(), limit=None, out_space=None):
    vmem = pl.BlockSpec(memory_space=pltpu.VMEM)
    return pl.pallas_call(
        kernel,
        out_shape=[jax.ShapeDtypeStruct(s, d) for s, d in outs],
        in_specs=[vmem] * len(ins),
        out_specs=[vmem if out_space is None else pl.BlockSpec(memory_space=out_space)] * len(outs),
        scratch_shapes=list(scratch),
        compiler_params=pltpu.CompilerParams(vmem_limit_bytes=limit or VMEM_BYTES),
        cost_estimate=pl.CostEstimate(flops=int(us * UNIT), bytes_accessed=1, transcendentals=0),
    )(*ins)


def exchange(value, pair):
    count = lax.axis_size("grp") * lax.axis_size("blk")
    return lax.ppermute(value, AXES, [(i, i ^ pair[i % 2]) for i in range(count)])


def slot_pairs():
    count = lax.axis_size("grp") * lax.axis_size("blk")
    masks = [1 << i for i in range(1, count.bit_length() - 1)]
    first = list(masks)
    second = list(masks)
    if len(masks) > 3:
        first = masks[0:4] + masks[4:]
        second = masks[2:4] + masks[0:2] + masks[4:]
    return list(zip(first, second))


def fold(pair, *ins, alone=0):
    paired = ins[: len(ins) - alone]
    rows = sum(v.shape[0] for v in paired[0::2]) // 2 + sum(v.shape[0] for v in ins[len(paired) :]) // 2
    outs = [((rows, LANES), BF16)] * 2
    return small_call(functools.partial(fold_kernel, pair, alone), outs, ins, 0.5)


def grow_cut_kernel(pair, segments, mine, got, out, low, high, near, end):
    grow_into(slot_bit(pair), segments, mine, got, out)
    cut, step = low.shape[0], near.shape[0]
    low[...] = out[0:cut, :]
    high[...] = out[cut:, :]
    near[...] = out[cut : cut + step, :]
    end[...] = out[cut + step :, :]


def gather(mine, slots, sizes, rest):
    for i in reversed(range(1, len(slots))):
        got = exchange(mine, slots[i])
        if i > 2:
            segments, rows = (mine.shape[0],), 2 * mine.shape[0]
        elif i == 2:
            segments, rows = tuple(n // 16 for n in sizes) + (rest // 2,), 2 * mine.shape[0]
        else:
            segments, rows = tuple(n // 8 for n in sizes), sum(sizes) // 4 + rest
        shapes = [((rows, LANES), BF16)]
        if i > 1:
            (mine,) = small_call(functools.partial(grow_kernel, slots[i], segments), shapes, [mine, got], 0.4)
            continue
        cut = rows * 5 // 192 * 16
        step = (rows - cut) // 32 * 16
        shapes += [((n, LANES), BF16) for n in (cut, rows - cut, step, rows - cut - step)]
        return small_call(functools.partial(grow_cut_kernel, slots[i], segments), shapes, [mine, got], 0.5)


def unpack(kernel, layout, name, ins, held, scratch, us):
    shapes = [(n, cols) for _, n, cols in layout]
    hbm, vmem = pl.BlockSpec(memory_space=pltpu.HBM), pl.BlockSpec(memory_space=pltpu.VMEM)
    return pl.pallas_call(
        kernel,
        out_shape=[jax.ShapeDtypeStruct(s, F32) for s in [(GAIN_ROWS, LANES)] + shapes],
        in_specs=[vmem] * len(ins) + ([vmem] + [hbm] * len(shapes) if held else []),
        out_specs=[vmem] + [hbm] * len(shapes),
        scratch_shapes=[pltpu.VMEM(s, F32) for s in shapes] + scratch + [pltpu.SemaphoreType.DMA((24,))],
        input_output_aliases={len(ins) + i: i for i in range(len(held))},
        compiler_params=pltpu.CompilerParams(vmem_limit_bytes=32 * 1024 * 1024),
        cost_estimate=pl.CostEstimate(flops=int(us * UNIT), bytes_accessed=1, transcendentals=0),
        name=name,
    )(*ins, *held)


def spread(mine, low, high, near, last, slot, sizes, rest, layout, gains, weights):
    rows, cut, step = mine.shape[0], low.shape[0], near.shape[0]
    end = rows - rest
    got_low, got_high = exchange(low, slot), exchange(high, slot)

    def write(spans, ins, held, name):
        kernel = functools.partial(unpack_kernel, layout, sizes, slot, spans, not held)
        return list(unpack(kernel, layout, name, [*ins, *weights], held, [], 0.3))

    held = write(((False, 0, 0, end),), [mine], [], "unpack_own")
    got_low, low, near, last, held[0] = lax.optimization_barrier((got_low, low, near, last, held[0]))
    mates = [exchange(v, (1, 1)) for v in (low, near, last, got_low)]
    held = write(((False, 1, 0, cut),), [got_low], held, "unpack_low")
    spans = ((True, 0, 0, cut), (True, 0, cut, cut + step), (True, 0, cut + step, end), (True, 1, 0, cut))
    held = write(spans, mates, held, "unpack_mate")
    got_high, held[0] = lax.optimization_barrier((got_high, held[0]))
    mate_high = exchange(got_high, (1, 1))
    held = write(((False, 1, cut, end),), [got_high], held, "unpack_high")
    kernel = functools.partial(unpack_last_kernel, layout, sizes, slot, (True, 1, cut, end), rest)
    scratch = [pltpu.VMEM((rest, LANES), F32), pltpu.SemaphoreType.DMA((24,))]
    ins = [mate_high, mine, got_high, mates[2], gains, *weights]
    return unpack(kernel, layout, "unpack_last", ins, held, scratch, 2.0)[1:]


def plain(kernel, ins, outs, kept, *refs):
    head = refs[: ins]
    made = refs[ins + kept : ins + kept + outs]
    scratch = refs[ins + 2 * kept + outs :]
    kernel(*head, *made, *scratch)


class Layer:
    def __init__(self, plan):
        self.plan = plan
        self.step = 0
        self.have = {}

    def __getitem__(self, key):
        return self.have[key]

    def __setitem__(self, key, value):
        self.have[key] = value

    def run(self, kernel, outs, extra=(), scratch=(), us=1.0):
        name, reads = self.plan[self.step]
        later = [r for _, more in self.plan[self.step + 1 :] for r in more]
        kept = sorted(k for k in self.have if k in later and k not in reads and k != "sc")
        self.step += 1

        def size(key):
            return self.have[key].size * self.have[key].dtype.itemsize

        while sum(map(size, kept)) > CARRY_BYTES:
            kept.remove(max(kept, key=size))
        smem = pl.BlockSpec(memory_space=pltpu.SMEM)
        vmem = pl.BlockSpec(memory_space=pltpu.VMEM)
        ins = [self.have[r] for r in reads] + list(extra)
        in_specs = [smem if r == "sc" else vmem for r in reads] + [vmem] * len(extra)
        shapes = [jax.ShapeDtypeStruct(s, d) for _, s, d in outs]
        shapes += [jax.ShapeDtypeStruct(self.have[k].shape, self.have[k].dtype) for k in kept]
        made = pl.pallas_call(
            functools.partial(plain, kernel, len(ins), len(outs), len(kept)),
            out_shape=shapes,
            in_specs=in_specs + [vmem] * len(kept),
            out_specs=[vmem] * len(shapes),
            scratch_shapes=list(scratch),
            input_output_aliases={len(ins) + i: len(outs) + i for i in range(len(kept))},
            compiler_params=pltpu.CompilerParams(vmem_limit_bytes=VMEM_BYTES),
            cost_estimate=pl.CostEstimate(flops=int(us * UNIT), bytes_accessed=1, transcendentals=0),
            name=name,
        )(*ins, *[self.have[k] for k in kept])
        for key, value in zip([o[0] for o in outs] + kept, made):
            self.have[key] = value


def swap(value, axis, mask):
    count = math.prod(lax.axis_size(a) for a in axis) if isinstance(axis, tuple) else lax.axis_size(axis)
    return lax.ppermute(value, axis, [(i, i ^ mask) for i in range(count)])


def halo(ea, eb):
    count = lax.axis_size("blk")
    near = [(i, i ^ 1) for i in range(count)]
    far = []
    for i in range(1, count - 1, 2):
        far += [(i, i + 1), (i + 1, i)]
    return lax.ppermute(ea, "blk", near), lax.ppermute(eb, "blk", far)


def local(
    features, d_out, bucket_batch, valid_len, time_start, time_width, freq_start, freq_width,
    gains, inner_gain, ffn1_in, ffn1_out, qkv_w, out_w, cg_up, cg_conv, cg_down, merge_conv,
    merge_w, ffn2_in, ffn2_out,
):
    rows, width = features.shape
    half = cg_down.shape[0]
    ff = ffn1_in.shape[1]
    blocks = lax.axis_size("blk")
    me = lax.axis_index("blk")
    freq = np.exp(np.arange(32, dtype=np.float64) * (-2.0 * math.log(10000.0) / HEAD_DIM))
    freq = jnp.asarray(np.tile(freq, 4)[None, :].astype(np.float32))
    wide = pltpu.VMEM((half // LANES, rows + 2 * HALO, LANES), F32)
    plane = pltpu.VMEM((rows, half), F32)
    rim = pltpu.VMEM((half // LANES, 6 * HALO, LANES), F32)
    pairs = [(m, m | 1) for m in range(0, blocks, 2)]
    kvs = [(f"kv{a}", f"kv{b}") for a, b in pairs]
    even = [a for a, _ in pairs[1:]]
    state = ["c", "l", "acc"]
    plan = [("gate", ["sc", "x1"])]
    plan += [("att_first", ["sc", "q", *kvs[0]])]
    plan += [("conv_gate", ["sc", "n"]), ("mixed", ["sc", "plane1", "na", "nb", "rest"])]
    far_masks = [m for a, b in pairs[1:] for m in (a, b)]
    plan += [("att_mid", ["sc", "q", f"kv{m}", *state]) for m in far_masks[:-1]]
    plan += [
        ("att_last", ["sc", "q", f"kv{far_masks[-1]}", *state, "catg"]),
        ("conv_merge", ["sc", "att", "catg"]),
        ("merge", ["sc", "plane2", "att", "catg", "ha", "hb", "x1"]),
        ("conv_back", ["sc", "df", "ec"]),
        ("split", ["sc", "plane3", "ec", "ca", "cb", "na", "nb", "rest", "mixed", "oT", "l"]),
    ]
    back = ["qm", "c", "eaT", "delta"]

    def back_reads(m):
        return [f"kv{m}", f"w{m}", f"top{m}", *back] + ([] if m == even[0] + 1 else ["dqT"])

    for e in even:
        for m in (e + 1, e):
            plan += [("attback", back_reads(m))]
        plan += [("join_kv", [f"pd{e}", f"in{e}"])]
    plan += [
        ("attback", back_reads(1)),
        ("gateback", ["sc", "emix", "mb", "ma", "mg", "rs", "dm", "slope", "a3", "x1", "gated", "ecg", "ob", "eatt"]),
        ("grads2", ["a4", "h2", "e2", "du2", "un", "em"]),
        ("pack_early", ["part1", "buf2"]),
        ("attback", back_reads(0)),
        ("fold_early", ["keep", "got0", "got1", "got2"]),
    ]
    total = f"far{even[0]}"
    for e in even[1:]:
        plan += [("join_far", [total, f"far{e}"])]
        total = f"t{e}"
    plan += [
        ("last", ["sc", "dqT", "own", "near", total, "a2", "x1", "g2", "bcg", "a1", "h1", "d1"]),
        ("pack_late", ["buf3"]),
        ("merge_taps", ["sc", "ec", "ca", "cb", "att", "catg"]),
        ("gate_taps", ["sc", "emix", "mb", "ma", "n", "tm", "g4", "gi"]),
        ("input_grad", ["sc", "du1", "g1"]),
    ]
    run = Layer(plan)
    smem = pl.BlockSpec(memory_space=pltpu.SMEM)
    vmem = pl.BlockSpec(memory_space=pltpu.VMEM)
    raw = (bucket_batch, valid_len, time_start, time_width, freq_start, freq_width, gains, freq,
           features, ffn1_in, ffn1_out, qkv_w)
    def narrow(name, kind=BF16):
        return (name, (rows, width), kind)

    def middle(name, kind=BF16):
        return (name, (rows, half), kind)

    def broad(name, kind=BF16):
        return (name, (rows, ff), kind)

    outs = [narrow("x1", F32), narrow("a1"), broad("h1"), broad("d1"), narrow("a2"), narrow("q"), middle("kv0"), middle("kvs")]
    made = pl.pallas_call(
        pre_kernel,
        out_shape=[jax.ShapeDtypeStruct((16,), jnp.int32)] + [jax.ShapeDtypeStruct(o[1], o[2]) for o in outs],
        in_specs=[pl.BlockSpec(memory_space=pltpu.HBM)] * 12,
        out_specs=[smem] + [vmem] * 8,
        scratch_shapes=[pltpu.SMEM(v.shape, v.dtype) for v in raw[:6]]
        + [pltpu.VMEM(v.shape, v.dtype) for v in raw[6:]] + [pltpu.SemaphoreType.DMA((12,))],
        compiler_params=pltpu.CompilerParams(vmem_limit_bytes=VMEM_BYTES),
        cost_estimate=pl.CostEstimate(flops=int(4.0 * UNIT), bytes_accessed=1, transcendentals=0),
        name="pre",
    )(raw[0], *[pltpu.with_memory_space_constraint(v, pltpu.HBM) for v in raw[1:]])
    for key, value in zip(["sc"] + [o[0] for o in outs], made):
        run[key] = value
    held = {0: run["kvs"]}
    bit = blocks // 2
    while bit > 1:
        held.update({m | bit: swap(held[m], "blk", bit) for m in list(held)})
        bit //= 2
    held[1] = swap(held[0], "blk", 1)

    def send_edges():
        return halo(run["ea"], run["eb"])

    edge = [("ea", (HALO, half), BF16), ("eb", (HALO, half), BF16)]
    edge2 = [("ea", (2 * HALO, half), BF16), ("eb", (2 * HALO, half), BF16)]
    stats = [("c", (8, rows), F32), ("l", (8, rows), F32)]

    def kept(*masks):
        return [o for m in masks for o in ((f"w{m}", (HEADS * rows, rows), BF16), (f"top{m}", (8, rows), F32))]


    run.run(
        gate_kernel,
        [narrow("a3"), middle("rest", F32), broad("slope"), middle("n"), middle("mg", F32), ("rs", (rows, 1), F32)] + edge2,
        [gains, inner_gain[None, :], cg_up], us=2.5,
    )
    edges = send_edges()
    run["kv1"] = held[1]
    run.run(functools.partial(att_kernel, True, False, pairs[0]), stats + [("qm", (HEADS * rows, LANES), BF16)] + kept(*pairs[0]) + [("acc", (width, rows), F32)], us=0.5)
    run.run(functools.partial(local_conv_kernel, 1, False), [middle("plane1", F32)], [cg_conv], [wide], us=0.3)
    run["na"], run["nb"] = edges
    run.run(
        mixed_kernel, [middle("mixed", F32), middle("gated"), narrow("catg")],
        [cg_conv, cg_down], [rim], us=1.5,
    )
    for a, b in pairs[1:]:
        late, _ = lax.optimization_barrier((held[a], run["catg"]))
        run[f"kv{a}"] = late
        mate = swap(late, "blk", 1)
        run.run(
            functools.partial(att_kernel, False, False, (a,)), stats + kept(a) + [("acc", (width, rows), F32)], us=2.8,
        )
        run[f"kv{b}"] = mate
        if b < blocks - 1:
            run.run(
                functools.partial(att_kernel, False, False, (b,)), stats + kept(b) + [("acc", (width, rows), F32)], us=2.8,
            )
    run.run(
        functools.partial(att_kernel, False, True, (blocks - 1,)),
        stats + kept(blocks - 1) + [("oT", (width, rows), F32), narrow("ob"), narrow("att")] + edge,
        [out_w], [pltpu.VMEM((width, rows), F32)], us=3.0,
    )
    edges = send_edges()
    run.run(functools.partial(local_conv_kernel, 1, False), [middle("plane2", F32)], [merge_conv], [wide], us=0.3)
    run["ha"], run["hb"] = edges
    run.run(
        merge_kernel,
        [narrow("out"), middle("un"), narrow("em"), middle("ec"), middle("df", F32), narrow("g2", F32), narrow("a4"),
         broad("h2"), narrow("e2"), broad("du2"), ("g4", (8, width), F32)] + edge2,
        [merge_conv, merge_w, d_out, gains, ffn2_in, ffn2_out], [rim, plane], us=5.5,
    )
    edges = send_edges()
    run.run(functools.partial(local_conv_kernel, -1, True), [middle("plane3", F32)], [merge_conv], [wide], us=0.3)
    run["ca"], run["cb"] = edges
    run.run(
        split_kernel,
        [narrow("eatt"), narrow("ecg"), middle("emix"), middle("dm", F32), ("eaT", (width, rows), BF16),
         ("delta", (8, rows), F32), ("mb", (HALO, half), BF16), ("ma", (HALO, half), BF16)],
        [merge_conv, cg_down, out_w], [rim, plane], us=2.0,
    )

    tall = ("dqT", (width, rows), F32)
    pair_sum = (rows, 2 * width)
    for e in even:
        for m in (e + 1, e):
            run.run(
                functools.partial(attback_kernel, m == even[0] + 1), [tall, (f"pd{m}", pair_sum, BF16)], us=0.5
            )
            if m & 1:
                arrival = swap(run[f"pd{m}"], "blk", 1)
        run[f"in{e}"] = arrival
        run.run(join_kernel, [(f"s{e}", (rows + 32, 2 * width), BF16)], us=0.2)
    fars = {e: swap(run[f"s{e}"], "blk", e) for e in even}
    run.run(functools.partial(attback_kernel, False), [tall, ("pd1", pair_sum, BF16)], us=0.05)
    near = swap(run["pd1"], "blk", 1)
    run.run(
        gateback_kernel,
        [narrow("bcg", F32), ("gi", (8, half), F32), ("buf2", (3584, LANES), BF16)],
        [cg_conv, inner_gain[None, :], cg_up, gains], [wide, plane], us=0.5,
    )
    count = lax.axis_size("grp") * blocks
    used, late, rest = 8704, 5632, 256
    slots = slot_pairs()
    grain = 16 << (len(slots) - 2)
    sizes = (used + 8 * (-((used + late) // 8 + rest) % grain), late)
    run.run(grads_kernel, [("part1", (5120, LANES), BF16)], us=0.05)
    cuts = pieces_of(sizes[0] // 2, 3)
    run.run(
        functools.partial(pack_kernel, 2),
        [("keep", (sizes[0] // 2, LANES), BF16)] + [(f"send{i}", (n, LANES), BF16) for i, n in enumerate(cuts)], us=0.1,
    )
    gots = [exchange(run[f"send{i}"], (1, 1)) for i in range(3)]
    run.run(functools.partial(attback_kernel, False), [tall, ("own", pair_sum, F32)], us=0.5)
    for i in range(3):
        run[f"got{i}"] = gots[i]
    for e in even:
        run[f"far{e}"] = fars[e]
    run["near"] = near
    run.run(
        functools.partial(fold_pieces_kernel, slots[0]),
        [("early", (sizes[0] // 4, LANES), BF16), ("send_early", (sizes[0] // 4, LANES), BF16)], us=0.2,
    )
    early_got = exchange(run["send_early"], slots[0])
    for e in even[1:]:
        run.run(join_kernel, [(f"t{e}", (rows + 32, 2 * width), BF16)], us=0.2)
    run.run(
        last_kernel,
        [narrow("g1", F32), broad("du1"), ("buf3", (5632, LANES), BF16)],
        [freq, qkv_w, gains, ffn1_out], us=0.3,
    )
    quarter = ((sizes[1] // 4, LANES), BF16)
    cuts = pieces_of(sizes[1] // 2, 2)
    run.run(
        functools.partial(pack_kernel, 1),
        [("keep3", (sizes[1] // 2, LANES), BF16)] + [(f"late{i}", (n, LANES), BF16) for i, n in enumerate(cuts)], us=0.1,
    )
    gots = [exchange(run[f"late{i}"], (1, 1)) for i in range(2)]
    gots[0], early_got = lax.optimization_barrier((gots[0], early_got))
    keep3, send3 = small_call(functools.partial(fold_pieces_kernel, slots[0]), [quarter, quarter], [run["keep3"], *gots], 0.3)
    late_got = exchange(send3, slots[0])
    _, early = lax.optimization_barrier((send3, run["early"]))
    early, early_send = fold(slots[1], early, early_got)
    early_got = exchange(early_send, slots[1])
    _, run["ec"] = lax.optimization_barrier((early_send, run["ec"]))
    run.run(merge_taps_kernel, [("tm", (128, LANES), F32)], (), [wide], us=1.0)
    late_got, run["tm"] = lax.optimization_barrier((late_got, run["tm"]))
    keep, send = fold(slots[1], keep3, late_got)
    got = exchange(send, slots[1])
    _, run["gi"] = lax.optimization_barrier((send, run["gi"]))
    run.run(gate_taps_kernel, [("small", (rest, LANES), BF16)], (), [wide, pltpu.VMEM((rest, LANES), F32)], us=1.0)
    keep, send = fold(slots[2], early, early_got, keep, got, run["small"], alone=1)
    got = exchange(send, slots[2])
    for pair in slots[3:]:
        keep, send = fold(pair, keep, got)
        got = exchange(send, pair)
    _, run["g1"] = lax.optimization_barrier((send, run["g1"]))
    run.run(input_kernel, [narrow("dx", F32)], [gains, features, ffn1_in], us=0.3)
    got, run["dx"] = lax.optimization_barrier((got, run["dx"]))
    (mine,) = small_call(functools.partial(fold_kernel, None, 0), [(keep.shape, BF16)], [keep, got], 0.3)
    base = sizes[0]
    tail = base + late
    layout = (
        (None, 5, 256), (tail + 8 * TAPS + 2, 1, 512),
        (base, 256, 1024), (base + 2048, 1024, 256), (base + 4096, 256, 768), (8192, 256, 256),
        (5120, 256, 1024), (tail + 4 * TAPS, TAPS, 512), (7168, 512, 256), (tail, TAPS, 512), (4096, 512, 256),
        (0, 256, 1024), (2048, 1024, 256),
    )
    whole = gather(mine, slots, sizes, rest)
    weights = (ffn1_in, qkv_w, cg_up, ffn2_in)
    sums = spread(*whole, slots[0], sizes, rest, layout, gains, weights)
    return (run["out"], run["dx"], sums[0], sums[1][0], *sums[2:])


def solution(mesh):
    rows = P(("grp", "blk"), None)
    in_specs = (rows, rows, P("grp")) + (P("grp", None),) * 5 + (P(),) * 13
    out_specs = (rows, rows) + (P(),) * 13
    return jax.shard_map(local, mesh=mesh, in_specs=in_specs, out_specs=out_specs, check_vma=False)
```
